32 devices in a mesh: dp: 16 (over z, y, x), tensor: 2 (over core).
Axes of the slice: x: 2, y: 2, z: 4, core: 2. Of those that a mesh axis runs over, the one named last changes fastest.
Arguments:
- hidden_in: bfloat16 [64, 512, 1024], P('dp', 'tensor'), may hold values from -6 to 6
- segment_ids: int32 [64, 512], P('dp'), may hold values from 0 to 7, as said below
- adapter_pick: int32 [64], P('dp'), may hold values from 0 to 7
- w_qkv: bfloat16 [3, 1024, 1024], P(None, 'dp', 'tensor'), may hold values from -0.1875 to 0.1875
- w_out: bfloat16 [1024, 1024], P('tensor', 'dp'), may hold values from -0.5 to 0.5
- w_up: bfloat16 [1024, 4096], P('dp', 'tensor'), may hold values from -0.1875 to 0.1875
- w_down: bfloat16 [4096, 1024], P('tensor', 'dp'), may hold values from -0.09375 to 0.09375
- ln_gain: float32 [2, 1024], replicated, may hold values from 0.5 to 1.5
- ln_bias: float32 [2, 1024], replicated, may hold values from -1.5 to 1.5
- adapt_a: bfloat16 [4, 8, 1024, 16], replicated, may hold values from -0.1875 to 0.1875
- adapt_b: bfloat16 [4, 8, 16, 1024], replicated, may hold values from -0.75 to 0.75
- up_a: bfloat16 [8, 1024, 16], replicated, may hold values from -0.1875 to 0.1875
- up_b: bfloat16 [8, 16, 4096], replicated, may hold values from -0.75 to 0.75
- down_a: bfloat16 [8, 4096, 16], replicated, may hold values from -0.09375 to 0.09375
- down_b: bfloat16 [8, 16, 1024], replicated, may hold values from -0.75 to 0.75
- grad_out: bfloat16 [64, 512, 1024], P('dp', 'tensor'), may hold values from -6 to 6
Outputs:
- layer_out: bfloat16 [64, 512, 1024], P('dp', 'tensor')
- grad_in: float32 [64, 512, 1024], P('dp', 'tensor')
- grad_adapt_a: float32 [4, 8, 1024, 16], replicated
- grad_adapt_b: float32 [4, 8, 16, 1024], replicated
- grad_up_a: float32 [8, 1024, 16], replicated
- grad_up_b: float32 [8, 16, 4096], replicated
- grad_down_a: float32 [8, 4096, 16], replicated
- grad_down_b: float32 [8, 16, 1024], replicated
The draws below stay inside these ranges and needn't reach their ends.
Inputs may be any that keep to these rules, and one draw needn't show every extreme that they name: `segment_ids`: within a sequence the ids start at 0 and rise by one at each new document, never falling; a sequence holds at most 8 documents. Among the sequences 4 k to 4 (k + 1) - 1, one holds a single document and another holds 8.
All inputs are finite; a program needn't handle non-finite values.
Results may differ from the reference program's by a relative error of at most 0.015.
Values may be sent and summed in bfloat16 or wider, within the bound.
No kernel may reach another device: no remote copies, remote signals or barrier semaphores. Data moves between devices by JAX's collectives and lax.ppermute only.
A program may use at most 256 MiB of HBM per device.

```python
import math
import jax
import jax.numpy as jnp
from jax import lax

D = 1024
HEAD_DIM = 64
FF = 4096
RANK = 16
ADAPTERS = 8
L = 512
SEQ_GRP = 4
SEQS = 64


def draw_segment_ids(key, part):
    key = jax.random.fold_in(key, 11)
    key_break, key_pick, key_offset = jax.random.split(key, 3)
    coins = jax.random.randint(key_break, (SEQS, L), 0, L)
    breaks = (coins < 4).astype(jnp.int32)
    positions = jnp.arange(L)[None, :]
    breaks = breaks * (positions > 0).astype(jnp.int32)
    group_count = SEQS // SEQ_GRP
    chosen = jax.random.randint(key_pick, (group_count, 1), 0, SEQ_GRP)
    members = jnp.arange(SEQ_GRP)[None, :]
    single = (members == chosen).reshape(SEQS, 1).astype(jnp.int32)
    busy = (members == (chosen + 1) % SEQ_GRP).reshape(SEQS, 1).astype(jnp.int32)
    stride = L // 8
    offsets = jax.random.randint(key_offset, (SEQS, 7), 0, stride)
    starts = jnp.arange(1, 8)[None, :] * stride + offsets
    forced = jnp.sum((starts[:, None, :] == positions[:, :, None]).astype(jnp.int32), axis=2)
    forced = jnp.minimum(forced, 1)
    breaks = jnp.maximum(breaks, forced * busy)
    breaks = breaks * (1 - single)
    return jnp.minimum(jnp.cumsum(breaks, axis=1), 7).astype(jnp.int32)


def with_ends(drawn, rng, least, largest):
    index_at = [jax.random.randint(jax.random.fold_in(rng, axis), (), 0, length) for axis, length in enumerate(drawn.shape)]
    longest = drawn.shape.index(max(drawn.shape))
    neighbour = index_at[:longest] + [(index_at[longest] + 1) % drawn.shape[longest]] + index_at[longest + 1:]
    return drawn.at[tuple(index_at)].set(least).at[tuple(neighbour)].set(largest)


def steps_of(key, extent, shards, least, high):
    def one(dim, parts):
        draws = jax.random.uniform(jax.random.fold_in(jax.random.fold_in(key, 6), dim), (parts,), jnp.float32, least / len(shards), high / len(shards))
        return jnp.repeat(jnp.exp(draws), extent[dim] // parts).reshape((-1,) + (1,) * (len(extent) - dim - 1))

    level = one(*shards[0])
    for cut in shards[1:]:
        level = level * one(*cut)
    return level


def gaussian(own_key, dims, width, bound, cuts=(), dtype=jnp.bfloat16):
    values = width * jax.random.normal(own_key, dims, jnp.float32)
    if cuts:
        values = values * steps_of(own_key, dims, cuts, -0.22, 0.18)
    return jnp.clip(values, -bound, bound).astype(dtype)


def setup_inputs(seed: int = 0) -> dict:
    key_of = jax.random.split(jax.random.key(seed), 17)
    return {
        "hidden_in": gaussian(key_of[0], (SEQS, L, D), 1.0, 6.0, ((0, 16), (1, 2))),
        "segment_ids": draw_segment_ids(jax.random.fold_in(key_of[16], 71), 0),
        "adapter_pick": with_ends(jax.random.randint(key_of[2], (SEQS,), 0, ADAPTERS), jax.random.fold_in(key_of[2], 1), 0, ADAPTERS - 1).astype(jnp.int32),
        "w_qkv": gaussian(key_of[3], (3, D, D), D ** -0.5, 0.1875, ((1, 16), (2, 2))),
        "w_out": gaussian(key_of[4], (D, D), (D // 8) ** -0.5, 0.5, ((0, 2), (1, 16))),
        "w_up": gaussian(key_of[5], (D, FF), D ** -0.5, 0.1875, ((0, 16), (1, 2))),
        "w_down": gaussian(key_of[6], (FF, D), FF ** -0.5, 0.09375, ((0, 2), (1, 16))),
        "ln_gain": jnp.clip(1.0 + 0.1 * jax.random.normal(key_of[7], (2, D), jnp.float32), 0.5, 1.5),
        "ln_bias": gaussian(key_of[8], (2, D), 0.3, 1.5, (), jnp.float32),
        "adapt_a": gaussian(key_of[9], (4, ADAPTERS, D, RANK), D ** -0.5, 0.1875),
        "adapt_b": gaussian(key_of[10], (4, ADAPTERS, RANK, D), (4 * RANK) ** -0.5, 0.75),
        "up_a": gaussian(key_of[11], (ADAPTERS, D, RANK), D ** -0.5, 0.1875),
        "up_b": gaussian(key_of[12], (ADAPTERS, RANK, FF), (4 * RANK) ** -0.5, 0.75),
        "down_a": gaussian(key_of[13], (ADAPTERS, FF, RANK), FF ** -0.5, 0.09375),
        "down_b": gaussian(key_of[14], (ADAPTERS, RANK, D), (4 * RANK) ** -0.5, 0.75),
        "grad_out": gaussian(key_of[15], (SEQS, L, D), 1.0, 6.0, ((0, 16), (1, 2))),
    }


@jax.custom_vjp
def low(v):
    return lax.optimization_barrier(v.astype(jnp.bfloat16)).astype(jnp.float32)

@jax.custom_vjp
def low_back(v):
    return v

def low_keep(v):
    return (low(v), None)

def low_pass(kept, grad):
    return (grad,)

def back_keep(v):
    return (v, None)

def back_low(kept, grad):
    return (low(grad),)
low.defvjp(low_keep, low_pass)
low_back.defvjp(back_keep, back_low)

def matmul_high(left, right):
    return jnp.matmul(left, right, precision=lax.Precision.HIGHEST)

def layer_norm(values, gain_row, bias_row):
    centre = lax.optimization_barrier(jnp.mean(values, axis=-1, keepdims=True))
    centred = values - centre
    variance = lax.optimization_barrier(jnp.mean(centred * centred, axis=-1, keepdims=True))
    return centred * lax.rsqrt(variance + 1e-06) * gain_row + bias_row

def pick_rows(onehot, stacked):
    return jnp.einsum('be,e...->b...', onehot, stacked, precision=lax.Precision.HIGHEST)

def adapted(inputs, weight, factor_one, factor_two):
    rank_part = jnp.einsum('bld,bdr->blr', inputs, factor_one, precision=lax.Precision.HIGHEST)
    low_rank = jnp.einsum('blr,brf->blf', rank_part, factor_two, precision=lax.Precision.HIGHEST)
    return matmul_high(inputs, weight) + low_rank

def attend_one(bundle):
    queries, key_rows, value_rows, segments = bundle
    score_scale = 1.0 / math.sqrt(HEAD_DIM)
    scores = jnp.einsum('qhe,khe->hqk', queries, key_rows, precision=lax.Precision.HIGHEST) * score_scale
    scores = low_back(scores)
    same_doc = segments[:, None] == segments[None, :]
    scores = jnp.where(same_doc[None], scores, jnp.float32(-1000000000.0))
    row_peak = lax.optimization_barrier(jnp.max(scores, axis=-1, keepdims=True))
    weights = jnp.exp(scores - row_peak)
    probabilities = weights / lax.optimization_barrier(jnp.sum(weights, axis=-1, keepdims=True))
    mixture = jnp.einsum('hqk,khe->qhe', low(probabilities), value_rows, precision=lax.Precision.HIGHEST)
    return low_back(low(mixture))

def forward_block(hidden, segments, onehot, frozen, adapters):
    w_qkv, w_out, w_up, w_down, ln_gain, ln_bias = frozen
    adapt_a, adapt_b, up_a, up_b, down_a, down_b = adapters
    blocks, length, model_width = hidden.shape
    head_count = model_width // HEAD_DIM
    shaped = []
    for slot_index in range(3):
        projected = adapted(hidden, w_qkv[slot_index], pick_rows(onehot, adapt_a[slot_index]), pick_rows(onehot, adapt_b[slot_index]))
        shaped.append(low_back(low(projected)).reshape(blocks, length, head_count, HEAD_DIM))
    mixture = lax.map(jax.checkpoint(attend_one), (shaped[0], shaped[1], shaped[2], segments))
    attention = mixture.reshape(blocks, length, model_width)
    branch = low_back(adapted(attention, w_out, pick_rows(onehot, adapt_a[3]), pick_rows(onehot, adapt_b[3])))
    middle = layer_norm(hidden + branch, ln_gain[0], ln_bias[0])
    hidden_units = low_back(adapted(low(middle), w_up, pick_rows(onehot, up_a), pick_rows(onehot, up_b)))
    activation = low(jax.nn.gelu(hidden_units, approximate=False))
    feed_out = low_back(adapted(activation, w_down, pick_rows(onehot, down_a), pick_rows(onehot, down_b)))
    return layer_norm(middle + feed_out, ln_gain[1], ln_bias[1])

def reference(hidden_in, segment_ids, adapter_pick, w_qkv, w_out, w_up, w_down, ln_gain, ln_bias, adapt_a, adapt_b, up_a, up_b, down_a, down_b, grad_out):
    per_block = 4
    frozen = tuple((member.astype(jnp.float32) for member in (w_qkv, w_out, w_up, w_down, ln_gain, ln_bias)))
    adapters = tuple((member.astype(jnp.float32) for member in (adapt_a, adapt_b, up_a, up_b, down_a, down_b)))
    block_count = hidden_in.shape[0] // per_block
    onehot = (adapter_pick[:, None] == jnp.arange(ADAPTERS)[None, :]).astype(jnp.float32)
    hidden_blocks = hidden_in.astype(jnp.float32).reshape(block_count, per_block, L, D)
    segment_blocks = segment_ids.reshape(block_count, per_block, L)
    onehot_blocks = onehot.reshape(block_count, per_block, ADAPTERS)
    cotangent_blocks = grad_out.astype(jnp.float32).reshape(block_count, per_block, L, D)

    def block_step(running, bundle):
        hidden, segments, block_hot, cotangent = bundle

        def local_forward(inputs, adapter_set):
            return forward_block(inputs, segments, block_hot, frozen, adapter_set)
        result, pullback = jax.vjp(local_forward, hidden, adapters)
        grad_hidden, grad_adapters = pullback(cotangent)
        running = tuple((old_sum + new_term for old_sum, new_term in zip(running, grad_adapters)))
        return (running, (result.astype(jnp.bfloat16), grad_hidden))
    zero_sums = tuple((jnp.zeros(member.shape, jnp.float32) for member in adapters))
    totals, outputs = lax.scan(block_step, zero_sums, (hidden_blocks, segment_blocks, onehot_blocks, cotangent_blocks))
    layer_out = outputs[0].reshape(SEQS, L, D)
    grad_in = outputs[1].reshape(SEQS, L, D)
    return (layer_out, grad_in, totals[0], totals[1], totals[2], totals[3], totals[4], totals[5])
```

```python
import functools

import jax
import jax.numpy as jnp
from jax import lax
from jax.experimental import pallas as pl
from jax.experimental.pallas import tpu as pltpu
from jax.sharding import PartitionSpec as P

HEAD_DIM = 64
BF = jnp.bfloat16
F32 = jnp.float32
LOG2E = 1.4426950408889634
VMEM = 60 * 2**20


def nn(a, b):
    return lax.dot_general(a, b, (((1,), (0,)), ((), ())), preferred_element_type=F32)


def nt(a, b):
    return lax.dot_general(a, b, (((1,), (1,)), ((), ())), preferred_element_type=F32)


def tn(a, b):
    return lax.dot_general(a, b, (((0,), (0,)), ((), ())), preferred_element_type=F32)


def params(flops, nbytes, limit=VMEM):
    return dict(
        compiler_params=pltpu.CompilerParams(vmem_limit_bytes=limit),
        cost_estimate=pl.CostEstimate(flops=flops, bytes_accessed=nbytes, transcendentals=0),
    )


def load_halves(gathered, scratch, sems, first, width):
    copies = []
    for half in range(2):
        copy = pltpu.make_async_copy(
            gathered.at[:, half, :, pl.ds(first, width)], scratch.at[half], sems.at[half]
        )
        copy.start()
        copies.append(copy)
    return copies


def rows_of(scratch, half, lo, width):
    block = scratch[half, :, :, pl.ds(lo, width)]
    return block.reshape(block.shape[0] * block.shape[1], width)


def qkv_kernel(meta, x_ref, a_ref, b_ref, w_ref, qkv_ref, rank_ref, w_scr, sems):
    @pl.when(pl.program_id(0) == 0)
    def _():
        for copy in load_halves(w_ref, w_scr, sems, 0, w_scr.shape[3]):
            copy.wait()

    x = x_ref[0]
    width = w_scr.shape[3] // 3
    for slot in range(3):
        rank = nt(x, a_ref[slot, 0]).astype(BF)
        rank_ref[0, slot] = rank
        for half in range(2):
            weight = rows_of(w_scr, half, slot * width, width)
            cols = slice(half * width, (half + 1) * width)
            full = nn(x, weight) + nn(rank, b_ref[slot, 0, :, cols])
            qkv_ref[0, slot, :, cols] = full.astype(BF)


def attend_kernel(q_ref, k_ref, v_ref, segc_ref, segr_ref, out_ref, lse_ref):
    q, k, v = q_ref[0, 0], k_ref[0, 0], v_ref[0, 0]
    length, lanes = q.shape
    lane = lax.broadcasted_iota(jnp.int32, (1, lanes), 1)
    zero = jnp.zeros((), BF)
    tile = 256
    stats = []
    for row in range(0, length, tile):
        same = segc_ref[0, row : row + tile, :] == segr_ref[0]
        total = jnp.zeros((tile, lanes), F32)
        for head in range(lanes // HEAD_DIM):
            mine = (lane // HEAD_DIM) == head
            scores = nt(q[row : row + tile], jnp.where(mine, k, zero)) * HEAD_DIM**-0.5
            scores = jnp.where(same, scores, F32(-1000000000.0))
            peak = jnp.max(scores, axis=1, keepdims=True)
            weights = jnp.exp(scores - peak)
            mass = jnp.sum(weights, axis=1, keepdims=True)
            probs = (weights * (1.0 / mass)).astype(BF)
            total += nn(probs, jnp.where(mine, v, zero))
            stats.append(peak + jnp.log(mass))
        out_ref[0, row : row + tile, :] = total.astype(BF)
    heads = lanes // HEAD_DIM
    spread = lax.broadcasted_iota(jnp.int32, (tile, 128), 1)
    for index in range(length // tile):
        table = jnp.zeros((tile, 128), F32)
        for head in range(heads):
            table = jnp.where(spread == head, stats[index * heads + head], table)
        lse_ref[0, 0, :, index * tile : (index + 1) * tile] = table.T[:8, :]


def attend_back_kernel(
    q_ref, k_ref, v_ref, segc_ref, segr_ref, lse_ref, o_ref, do_ref, gq_ref, gk_ref, gv_ref
):
    q, k, v, do = q_ref[0, 0], k_ref[0, 0], v_ref[0, 0], do_ref[0]
    length, lanes = q.shape
    lane = lax.broadcasted_iota(jnp.int32, (1, lanes), 1)
    zero = jnp.zeros((), BF)
    product = do.astype(F32) * o_ref[0].astype(F32)
    high = product.astype(BF)
    low = (product - high.astype(F32)).astype(BF)
    picker = (
        lax.broadcasted_iota(jnp.int32, (8, lanes), 0)
        == lax.broadcasted_iota(jnp.int32, (8, lanes), 1) // HEAD_DIM
    ).astype(BF)
    inner = nt(picker, high) + nt(picker, low)
    tile = 256
    scale = HEAD_DIM**-0.5
    grad_q = jnp.zeros((length, lanes), F32)
    for row in range(0, length, tile):
        same = segc_ref[0, row : row + tile, :] == segr_ref[0]
        grad_k = jnp.zeros((tile, lanes), F32)
        grad_v = jnp.zeros((tile, lanes), F32)
        for head in range(lanes // HEAD_DIM):
            mine = (lane // HEAD_DIM) == head
            k_mine = jnp.where(mine, k[row : row + tile], zero)
            v_mine = jnp.where(mine, v[row : row + tile], zero)
            scores = nt(k_mine, q) * scale
            scores = jnp.where(same, scores, F32(-1000000000.0))
            probs = jnp.exp(scores - lse_ref[0, 0, head : head + 1, :])
            grad_probs = nt(v_mine, do)
            grad_v += nn(probs.astype(BF), jnp.where(mine, do, zero))
            grad_scores = (probs * (grad_probs - inner[head : head + 1, :])).astype(BF)
            grad_k += nn(grad_scores, jnp.where(mine, q, zero))
            grad_q += tn(grad_scores, k_mine)
        gk_ref[0, 0, row : row + tile, :] = (grad_k * scale).astype(BF)
        gv_ref[0, 0, row : row + tile, :] = grad_v.astype(BF)
    gq_ref[0, 0] = (grad_q * scale).astype(BF)


def norm_parts(values):
    mean = jnp.mean(values, axis=-1, keepdims=True)
    centred = values - mean
    inverse = lax.rsqrt(jnp.mean(centred * centred, axis=-1, keepdims=True) + 1e-06)
    return centred * inverse, inverse


def norm_back(scaled, normed, inverse):
    mean_grad = jnp.mean(scaled, axis=-1, keepdims=True)
    mean_proj = jnp.mean(scaled * normed, axis=-1, keepdims=True)
    return (scaled - mean_grad - normed * mean_proj) * inverse


ROWS = 64


def out_kernel(
    meta, att_ref, x_ref, a_ref, b_ref, w_ref, gain_ref, bias_ref,
    normed_ref, inverse_ref, low_ref, rank_ref, w_scr, v_scr, sems,
):
    @pl.when(pl.program_id(0) == 0)
    def _():
        for copy in load_halves(w_ref, w_scr, sems, 3 * w_scr.shape[3], w_scr.shape[3]):
            copy.wait()

    att = att_ref[0]
    rank = nt(att, a_ref[0, 0]).astype(BF)
    rank_ref[0] = rank
    width = w_scr.shape[3]
    v_scr[...] = (
        nt(att[:, :width], rows_of(w_scr, 0, 0, width))
        + nt(att[:, width:], rows_of(w_scr, 1, 0, width))
        + nn(rank, b_ref[0, 0])
    )

    def step(index, carry):
        rows = pl.ds(pl.multiple_of(index * ROWS, ROWS), ROWS)
        normed, inverse = norm_parts(v_scr[rows, :] + x_ref[0, rows, :].astype(F32))
        normed_ref[0, rows, :] = normed
        inverse_ref[0, rows, :] = jnp.broadcast_to(inverse, (ROWS, 128))
        low_ref[0, rows, :] = (normed * gain_ref[0:1, :] + bias_ref[0:1, :]).astype(BF)
        return carry

    lax.fori_loop(0, v_scr.shape[0] // ROWS, step, 0)


def gelu_parts(x):
    density = jnp.exp(-0.5 * x * x)
    t = 1.0 / (1.0 + (0.3275911 * 0.7071067811865476) * jnp.abs(x))
    poly = t * (
        0.127414796
        + t * (-0.142248368 + t * (0.7107068705 + t * (-0.7265760135 + t * 0.5307027145)))
    )
    tail = poly * density
    phi = jnp.where(x > 0, 1.0 - tail, tail)
    return x * phi, phi + x * (density * 0.3989422804014327)


def up_kernel(
    meta, m_ref, a_ref, b_ref, w_ref, act_ref, slope_ref, rank_ref, w_scr, sems, *, first
):
    @pl.when(pl.program_id(0) == 0)
    def _():
        for copy in load_halves(w_ref, w_scr, sems, first, w_scr.shape[3]):
            copy.wait()

    m = m_ref[0]
    rank = nt(m, a_ref[0]).astype(BF)
    rank_ref[0] = rank
    width = w_scr.shape[3]
    chunk = 512
    per = width // chunk

    def step(index, carry):
        half = index // per
        lo = pl.multiple_of((index - half * per) * chunk, chunk)
        cols = pl.ds(pl.multiple_of(index * chunk, chunk), chunk)
        units = nn(m, rows_of(w_scr, half, lo, chunk)) + nn(rank, b_ref[0, :, cols])
        act, slope = gelu_parts(units)
        act_ref[0, :, cols] = act.astype(BF)
        slope_ref[0, :, cols] = slope.astype(BF)
        return carry

    lax.fori_loop(0, 2 * per, step, 0)


def down_kernel(
    meta, act_ref, slope_ref, n1_ref, go_ref, a_ref, b_ref, w_ref, gain_ref, bias_ref,
    out_ref, second_ref, gh_ref, ga_ref, gb_ref, w_scr, v_scr, gf_scr, sems, *, first,
):
    @pl.when(pl.program_id(0) == 0)
    def _():
        for copy in load_halves(w_ref, w_scr, sems, first, w_scr.shape[3]):
            copy.wait()

    act = act_ref[0]
    width = w_scr.shape[3]
    rank = nt(act, a_ref[0]).astype(BF)
    v_scr[...] = (
        nt(act[:, :width], rows_of(w_scr, 0, 0, width))
        + nt(act[:, width:], rows_of(w_scr, 1, 0, width))
        + nn(rank, b_ref[0])
    )

    def step(index, carry):
        rows = pl.ds(pl.multiple_of(index * ROWS, ROWS), ROWS)
        middle = n1_ref[0, rows, :] * gain_ref[0:1, :] + bias_ref[0:1, :]
        normed, inverse = norm_parts(v_scr[rows, :] + middle)
        out_ref[0, rows, :] = (normed * gain_ref[1:2, :] + bias_ref[1:2, :]).astype(BF)
        second = norm_back(go_ref[0, rows, :].astype(F32) * gain_ref[1:2, :], normed, inverse)
        second_ref[0, rows, :] = second
        gf_scr[rows, :] = second.astype(BF)
        return carry

    lax.fori_loop(0, v_scr.shape[0] // ROWS, step, 0)
    grad_feed = gf_scr[...]
    gb_ref[0] = tn(rank, grad_feed)
    grad_rank = nt(grad_feed, b_ref[0]).astype(BF)
    chunk = 512
    per = width // chunk

    def back(index, carry):
        half = index // per
        lo = pl.multiple_of((index - half * per) * chunk, chunk)
        cols = pl.ds(pl.multiple_of(index * chunk, chunk), chunk)
        grad_act = nn(grad_feed, rows_of(w_scr, half, lo, chunk)) + nn(grad_rank, a_ref[0, :, cols])
        gh_ref[0, :, cols] = (grad_act * slope_ref[0, :, cols].astype(F32)).astype(BF)
        ga_ref[0, :, cols] = tn(grad_rank, act_ref[0, :, cols])
        return carry

    lax.fori_loop(0, 2 * per, back, 0)


def mlp_back_kernel(
    meta, gh_ref, m_ref, n1_ref, r1_ref, second_ref, att_ref, ranku_ref, ranko_ref,
    ua_ref, ub_ref, oa_ref, ob_ref, w_ref, gain_ref,
    first_ref, gatt_ref, gua_ref, gub_ref, goa_ref, gob_ref,
    wu_scr, wo_scr, v_scr, gbr_scr, sems, semo, *, up_first, out_first,
):
    @pl.when(pl.program_id(0) == 0)
    def _():
        copies = load_halves(w_ref, wu_scr, sems, up_first, wu_scr.shape[3])
        copies += load_halves(w_ref, wo_scr, semo, out_first, wo_scr.shape[3])
        for copy in copies:
            copy.wait()

    gh = gh_ref[0]
    width = wu_scr.shape[3]
    grad_rank = nt(gh, ub_ref[0]).astype(BF)
    v_scr[...] = (
        nt(gh[:, :width], rows_of(wu_scr, 0, 0, width))
        + nt(gh[:, width:], rows_of(wu_scr, 1, 0, width))
        + nn(grad_rank, ua_ref[0])
    )
    gua_ref[0] = tn(grad_rank, m_ref[0])
    gub_ref[0] = tn(ranku_ref[0], gh)

    def step(index, carry):
        rows = pl.ds(pl.multiple_of(index * ROWS, ROWS), ROWS)
        scaled = (second_ref[0, rows, :] + v_scr[rows, :]) * gain_ref[0:1, :]
        first = norm_back(scaled, n1_ref[0, rows, :], r1_ref[0, rows, 0:1])
        first_ref[0, rows, :] = first
        gbr_scr[rows, :] = first.astype(BF)
        return carry

    lax.fori_loop(0, v_scr.shape[0] // ROWS, step, 0)
    grad_branch = gbr_scr[...]
    grad_rank_out = nt(grad_branch, ob_ref[0, 0]).astype(BF)
    goa_ref[0] = tn(grad_rank_out, att_ref[0])
    gob_ref[0] = tn(ranko_ref[0], grad_branch)
    owidth = wo_scr.shape[3]
    for half in range(2):
        cols = slice(half * owidth, (half + 1) * owidth)
        full = nn(grad_branch, rows_of(wo_scr, half, 0, owidth)) + nn(
            grad_rank_out, oa_ref[0, 0, :, cols]
        )
        gatt_ref[0, :, cols] = full.astype(BF)


def rank_back_kernel(meta, g_ref, x_ref, rank_ref, b_ref, gr_ref, ga_ref, gb_ref):
    grad = g_ref[0, 0]
    grad_rank = nt(b_ref[0, 0], grad).astype(BF)
    gr_ref[0, 0] = grad_rank
    ga_ref[0, 0] = nn(grad_rank, x_ref[0])
    gb_ref[0, 0] = tn(rank_ref[0, 0], grad)


def qkv_back_kernel(
    meta, gq_ref, gk_ref, gv_ref, gr_ref, first_ref, a_ref, w_ref, out_ref, w_scr, sems
):
    @pl.when(pl.program_id(0) == 0)
    def _():
        for copy in load_halves(w_ref, w_scr, sems, 0, w_scr.shape[3]):
            copy.wait()

    width = w_scr.shape[3] // 3
    total = first_ref[0]
    for slot, ref in enumerate((gq_ref, gk_ref, gv_ref)):
        total += tn(gr_ref[slot, 0], a_ref[slot, 0])
        for half in range(2):
            grad = ref[0, 0, :, half * width : (half + 1) * width]
            total += nt(grad, rows_of(w_scr, half, slot * width, width))
    out_ref[0] = total


def call(kernel, meta, grid, ins, outs, scratch, flops, **static):
    nbytes = sum(a.size * a.dtype.itemsize for a, _, _ in ins)
    in_specs = [
        pl.BlockSpec(memory_space=pl.ANY) if block is None else pl.BlockSpec(block, index)
        for _, block, index in ins
    ]
    return pl.pallas_call(
        functools.partial(kernel, **static) if static else kernel,
        grid_spec=pltpu.PrefetchScalarGridSpec(
            num_scalar_prefetch=1,
            grid=grid,
            in_specs=in_specs,
            out_specs=[pl.BlockSpec(block, index) for _, _, block, index in outs],
            scratch_shapes=scratch,
        ),
        out_shape=[jax.ShapeDtypeStruct(shape, dtype) for shape, dtype, _, _ in outs],
        **params(flops, nbytes),
    )(meta, *[a for a, _, _ in ins])


def shards(
    hidden_in, segment_ids, adapter_pick, w_qkv, w_out, w_up, w_down, ln_gain, ln_bias,
    adapt_a, adapt_b, up_a, up_b, down_a, down_b, grad_out,
):
    dp = lax.axis_size("dp")
    t = lax.axis_index("tensor")
    rows, ff_half = w_up.shape
    width = hidden_in.shape[2]
    half = width // 2
    ff = 2 * ff_half
    positions = hidden_in.shape[1]
    length = 2 * positions
    mine = hidden_in.shape[0] // 2
    rank = adapt_b.shape[2]
    adapters = adapt_b.shape[1]

    local = jnp.concatenate([w_qkv[0], w_qkv[1], w_qkv[2], w_out.T, w_up, w_down.T], axis=1)
    weights = lax.all_gather(local, ("dp", "tensor")).reshape(dp, 2, rows, local.shape[1])
    out_first = 3 * half
    up_first = 4 * half
    down_first = up_first + ff_half

    def to_sequences(pieces):
        other = lax.ppermute(
            [lax.dynamic_slice_in_dim(p, mine * (1 - t), mine, 0) for p in pieces], "tensor", [(0, 1), (1, 0)]
        )
        whole = []
        for piece, there in zip(pieces, other):
            here = lax.dynamic_slice_in_dim(piece, mine * t, mine, 0)
            low = jnp.where(t == 0, here, there)
            high = jnp.where(t == 0, there, here)
            whole.append(jnp.concatenate([low, high], axis=1))
        return whole

    def to_positions(value):
        here = lax.dynamic_slice_in_dim(value, positions * t, positions, 1)
        there = lax.ppermute(
            lax.dynamic_slice_in_dim(value, positions * (1 - t), positions, 1), "tensor", [(0, 1), (1, 0)]
        )
        low = jnp.where(t == 0, here, there)
        high = jnp.where(t == 0, there, here)
        return jnp.concatenate([low, high], axis=0)

    x, cotangent = to_sequences([hidden_in, grad_out])
    segs = lax.dynamic_slice_in_dim(segment_ids, mine * t, mine, 0)
    pick = lax.dynamic_slice_in_dim(adapter_pick, mine * t, mine, 0)
    meta = pick
    seg_col = segs.reshape(mine, length, 1)
    seg_row = segs.reshape(mine, 1, length)
    a_t = jnp.swapaxes(adapt_a, 2, 3)
    ua_t = jnp.swapaxes(up_a, 1, 2)
    da_t = jnp.swapaxes(down_a, 1, 2)

    blocks = dp
    tokens = mine * length
    seq3 = lambda s, m: (s, 0, 0)
    fixed2 = lambda s, m: (0, 0)
    picked3 = lambda s, m: (m[s], 0, 0)
    any_space = (None, None)

    def sems():
        return pltpu.SemaphoreType.DMA((2,))

    qkv, rank_qkv = call(
        qkv_kernel, meta, (mine,),
        [(x, (1, length, width), seq3),
         (a_t, (4, 1, rank, width), lambda s, m: (0, m[s], 0, 0)),
         (adapt_b, (4, 1, rank, width), lambda s, m: (0, m[s], 0, 0)),
         (weights, *any_space)],
        [((mine, 3, length, width), BF, (1, 3, length, width), lambda s, m: (s, 0, 0, 0)),
         ((mine, 3, length, rank), BF, (1, 3, length, rank), lambda s, m: (s, 0, 0, 0))],
        [pltpu.VMEM((2, blocks, rows, 3 * half), BF), sems()],
        6 * tokens * width * width,
    )

    pair = 2 * HEAD_DIM
    pairs = width // pair

    def slot_block(slot):
        return ((1, 1, length, pair), lambda s, h: (s, slot, 0, h))

    seg_specs = [
        pl.BlockSpec((1, length, 1), lambda s, h: (s, 0, 0)),
        pl.BlockSpec((1, 1, length), lambda s, h: (s, 0, 0)),
    ]
    attention, lse = pl.pallas_call(
        attend_kernel,
        grid=(mine, pairs),
        in_specs=[pl.BlockSpec(*slot_block(j)) for j in range(3)] + seg_specs,
        out_specs=[
            pl.BlockSpec((1, length, pair), lambda s, h: (s, 0, h)),
            pl.BlockSpec((1, 1, 8, length), lambda s, h: (s, h, 0, 0)),
        ],
        out_shape=[
            jax.ShapeDtypeStruct((mine, length, width), BF),
            jax.ShapeDtypeStruct((mine, pairs, 8, length), F32),
        ],
        **params(4 * tokens * length * width * 4, tokens * width * 8),
    )(qkv, qkv, qkv, seg_col, seg_row)

    normed, inverse, middle_low, rank_out = call(
        out_kernel, meta, (mine,),
        [(attention, (1, length, width), seq3),
         (x, (1, length, width), seq3),
         (a_t, (1, 1, rank, width), lambda s, m: (3, m[s], 0, 0)),
         (adapt_b, (1, 1, rank, width), lambda s, m: (3, m[s], 0, 0)),
         (weights, *any_space),
         (ln_gain, ln_gain.shape, fixed2),
         (ln_bias, ln_bias.shape, fixed2)],
        [((mine, length, width), F32, (1, length, width), seq3),
         ((mine, length, 128), F32, (1, length, 128), seq3),
         ((mine, length, width), BF, (1, length, width), seq3),
         ((mine, length, rank), BF, (1, length, rank), seq3)],
        [pltpu.VMEM((2, blocks, rows, half), BF), pltpu.VMEM((length, width), F32), sems()],
        2 * tokens * width * width,
    )

    act, slope, rank_up = call(
        up_kernel, meta, (mine,),
        [(middle_low, (1, length, width), seq3),
         (ua_t, (1, rank, width), picked3),
         (up_b, (1, rank, ff), picked3),
         (weights, *any_space)],
        [((mine, length, ff), BF, (1, length, ff), seq3),
         ((mine, length, ff), BF, (1, length, ff), seq3),
         ((mine, length, rank), BF, (1, length, rank), seq3)],
        [pltpu.VMEM((2, blocks, rows, ff_half), BF), sems()],
        2 * tokens * width * ff * 2,
        first=up_first,
    )

    layer_out, second, grad_hidden, g_down_a, g_down_b = call(
        down_kernel, meta, (mine,),
        [(act, (1, length, ff), seq3),
         (slope, (1, length, ff), seq3),
         (normed, (1, length, width), seq3),
         (cotangent, (1, length, width), seq3),
         (da_t, (1, rank, ff), picked3),
         (down_b, (1, rank, width), picked3),
         (weights, *any_space),
         (ln_gain, ln_gain.shape, fixed2),
         (ln_bias, ln_bias.shape, fixed2)],
        [((mine, length, width), BF, (1, length, width), seq3),
         ((mine, length, width), F32, (1, length, width), seq3),
         ((mine, length, ff), BF, (1, length, ff), seq3),
         ((mine, rank, ff), F32, (1, rank, ff), seq3),
         ((mine, rank, width), F32, (1, rank, width), seq3)],
        [pltpu.VMEM((2, blocks, rows, ff_half), BF), pltpu.VMEM((length, width), F32),
         pltpu.VMEM((length, width), BF), sems()],
        4 * tokens * width * ff,
        first=down_first,
    )

    grad_first, grad_att, g_up_a, g_up_b, g_out_a, g_out_b = call(
        mlp_back_kernel, meta, (mine,),
        [(grad_hidden, (1, length, ff), seq3),
         (middle_low, (1, length, width), seq3),
         (normed, (1, length, width), seq3),
         (inverse, (1, length, 128), seq3),
         (second, (1, length, width), seq3),
         (attention, (1, length, width), seq3),
         (rank_up, (1, length, rank), seq3),
         (rank_out, (1, length, rank), seq3),
         (ua_t, (1, rank, width), picked3),
         (up_b, (1, rank, ff), picked3),
         (a_t, (1, 1, rank, width), lambda s, m: (3, m[s], 0, 0)),
         (adapt_b, (1, 1, rank, width), lambda s, m: (3, m[s], 0, 0)),
         (weights, *any_space),
         (ln_gain, ln_gain.shape, fixed2)],
        [((mine, length, width), F32, (1, length, width), seq3),
         ((mine, length, width), BF, (1, length, width), seq3),
         ((mine, rank, width), F32, (1, rank, width), seq3),
         ((mine, rank, ff), F32, (1, rank, ff), seq3),
         ((mine, rank, width), F32, (1, rank, width), seq3),
         ((mine, rank, width), F32, (1, rank, width), seq3)],
        [pltpu.VMEM((2, blocks, rows, ff_half), BF), pltpu.VMEM((2, blocks, rows, half), BF),
         pltpu.VMEM((length, width), F32), pltpu.VMEM((length, width), BF), sems(), sems()],
        2 * tokens * width * (ff + width),
        up_first=up_first, out_first=out_first,
    )

    head_out = pl.BlockSpec((1, 1, length, pair), lambda s, h: (0, s, 0, h))
    grads_qkv = pl.pallas_call(
        attend_back_kernel,
        grid=(mine, pairs),
        in_specs=[pl.BlockSpec(*slot_block(j)) for j in range(3)]
        + seg_specs
        + [
            pl.BlockSpec((1, 1, 8, length), lambda s, h: (s, h, 0, 0)),
            pl.BlockSpec((1, length, pair), lambda s, h: (s, 0, h)),
            pl.BlockSpec((1, length, pair), lambda s, h: (s, 0, h)),
        ],
        out_specs=[head_out] * 3,
        out_shape=[jax.ShapeDtypeStruct((1, mine, length, width), BF)] * 3,
        **params(10 * tokens * length * width * 4, tokens * width * 16),
    )(qkv, qkv, qkv, seg_col, seg_row, lse, attention, grad_att)

    ranks, g_a, g_b = [], [], []
    for slot in range(3):
        by_seq = lambda s, m: (0, s, 0, 0)
        gr, ga, gb = call(
            rank_back_kernel, meta, (mine,),
            [(grads_qkv[slot], (1, 1, length, width), by_seq),
             (x, (1, length, width), seq3),
             (rank_qkv, (1, 1, length, rank), lambda s, m, slot=slot: (s, slot, 0, 0)),
             (adapt_b, (1, 1, rank, width), lambda s, m, slot=slot: (slot, m[s], 0, 0))],
            [((1, mine, rank, length), BF, (1, 1, rank, length), by_seq),
             ((1, mine, rank, width), F32, (1, 1, rank, width), by_seq),
             ((1, mine, rank, width), F32, (1, 1, rank, width), by_seq)],
            [],
            6 * tokens * width * rank,
        )
        ranks.append(gr)
        g_a.append(ga[0])
        g_b.append(gb[0])

    by_seq = lambda s, m: (0, s, 0, 0)
    grad_in = call(
        qkv_back_kernel, meta, (mine,),
        [(grads_qkv[0], (1, 1, length, width), by_seq),
         (grads_qkv[1], (1, 1, length, width), by_seq),
         (grads_qkv[2], (1, 1, length, width), by_seq),
         (jnp.concatenate(ranks, axis=0), (3, 1, rank, length), by_seq),
         (grad_first, (1, length, width), seq3),
         (a_t, (4, 1, rank, width), lambda s, m: (0, m[s], 0, 0)),
         (weights, *any_space)],
        [((mine, length, width), F32, (1, length, width), seq3)],
        [pltpu.VMEM((2, blocks, rows, 3 * half), BF), sems()],
        6 * tokens * width * width,
    )[0]

    onehot = (pick[:, None] == jnp.arange(adapters)[None, :]).astype(F32)

    def fold(per_sequence):
        total = onehot[0][:, None, None] * per_sequence[0][None]
        for index in range(1, mine):
            total += onehot[index][:, None, None] * per_sequence[index][None]
        return total.astype(BF)

    sums = lax.psum(
        tuple(fold(g) for g in [*g_a, g_out_a, *g_b, g_out_b, g_up_a, g_up_b, g_down_a, g_down_b]),
        ("dp", "tensor"),
    )
    sums = [s.astype(F32) for s in sums]
    turned = lambda v: jnp.swapaxes(v, -1, -2)
    return (
        to_positions(layer_out),
        to_positions(grad_in),
        turned(jnp.stack(sums[:4])),
        jnp.stack(sums[4:8]),
        turned(sums[8]),
        sums[9],
        turned(sums[10]),
        sums[11],
    )


def solution(mesh):
    placed = (
        P("dp", "tensor", None),
        P("dp", None),
        P("dp"),
        P(None, "dp", "tensor"),
        P("tensor", "dp"),
        P("dp", "tensor"),
        P("tensor", "dp"),
        P(),
        P(),
        P(),
        P(),
        P(),
        P(),
        P(),
        P(),
        P("dp", "tensor", None),
    )
    return jax.shard_map(
        shards,
        mesh=mesh,
        in_specs=placed,
        out_specs=(P("dp", "tensor", None), P("dp", "tensor", None), P(), P(), P(), P(), P(), P()),
        check_vma=False,
    )
```

```python
import functools

import jax
import jax.numpy as jnp
from jax import lax
from jax.experimental import pallas as pl
from jax.experimental.pallas import tpu as pltpu
from jax.sharding import PartitionSpec as P

HEAD_DIM = 64
BF = jnp.bfloat16
F32 = jnp.float32
LOG2E = 1.4426950408889634
VMEM = 60 * 2**20


def nn(a, b):
    return lax.dot_general(a, b, (((1,), (0,)), ((), ())), preferred_element_type=F32)


def nt(a, b):
    return lax.dot_general(a, b, (((1,), (1,)), ((), ())), preferred_element_type=F32)


def tn(a, b):
    return lax.dot_general(a, b, (((0,), (0,)), ((), ())), preferred_element_type=F32)


def params(flops, nbytes, limit=VMEM):
    return dict(
        compiler_params=pltpu.CompilerParams(vmem_limit_bytes=limit),
        cost_estimate=pl.CostEstimate(flops=flops, bytes_accessed=nbytes, transcendentals=0),
    )


class Piece:
    def __init__(self, col, width, rel, row, count, array, at, other):
        self.col, self.width, self.rel, self.row = col, width, rel, row
        self.count, self.array, self.at, self.other = count, array, at, other


class Loader:
    def __init__(self, plan, refs, scratch, sems, me, t):
        self.plan, self.refs, self.scratch, self.sems, self.me, self.t = plan, refs, scratch, sems, me, t

    def start(self):
        for slot, at, count, col, width, other, rel, row, into in self.plan:
            half = self.t ^ other
            if rel is None:
                source = self.refs[slot].at[:, half, :, pl.ds(col, width)]
                target = self.scratch.at[half]
            else:
                source = self.refs[slot].at[pl.ds(at, count), pl.ds(col, width)]
                target = self.scratch.at[half, self.me ^ rel, pl.ds(row, count), pl.ds(into, width)]
            pltpu.make_async_copy(source, target, self.sems.at[other]).start()

    def wait(self, other):
        whole = self.scratch.at[self.t ^ other]
        pltpu.make_async_copy(whole, whole, self.sems.at[other]).wait()

    def first_step(self):
        pl.when(pl.program_id(0) == 0)(self.start)

    def first_wait(self, other):
        pl.when(pl.program_id(0) == 0)(lambda: self.wait(other))

    def first_wait_all(self, index):
        if index == 0:
            self.first_wait(0)
            self.first_wait(1)

    def cols(self, half, lo, width):
        block = self.scratch[half, :, :, pl.ds(lo, width)]
        return block.reshape(block.shape[0] * block.shape[1], width)


def weight_plan(pieces, first, width):
    arrays, plan = [], []
    for p in pieces:
        lo, hi = max(p.col, first), min(p.col + p.width, first + width)
        if lo >= hi:
            continue
        slot = next((i for i, a in enumerate(arrays) if a is p.array), None)
        if slot is None:
            slot = len(arrays)
            arrays.append(p.array)
        plan.append((slot, p.at, p.count, lo - p.col, hi - lo, p.other, p.rel, p.row, lo - first))
    return arrays, plan


def qkv_kernel(meta, ins, outs, weights, scratch):
    x_ref, a_ref, b_ref = ins
    qkv_ref, rank_ref = outs
    (w,) = weights
    w.first_step()
    x = x_ref[0]
    slots, rank_size = rank_ref.shape[2] // a_ref.shape[2], a_ref.shape[2]
    rank = nt(x, a_ref[0:slots, 0].reshape(slots * rank_size, x.shape[1])).astype(BF)
    rank_ref[0] = rank
    width = w.scratch.shape[3] // slots
    for other in range(2):
        w.first_wait(other)
        half = w.t ^ other
        cols = pl.ds(pl.multiple_of(half * width, width), width)
        for slot in range(slots):
            mine = rank[:, slot * rank_size : (slot + 1) * rank_size]
            full = nn(x, w.cols(half, slot * width, width)) + nn(mine, b_ref[slot, 0, :, cols])
            qkv_ref[0, slot, :, cols] = full.astype(BF)


SCALE = HEAD_DIM**-0.5
SCALE2 = SCALE * LOG2E
GROUP = 4 * HEAD_DIM


def one_head(lane, head, value):
    return jnp.where(lane // HEAD_DIM == head, value, jnp.zeros((), value.dtype))


def attend_kernel(q_ref, k_ref, v_ref, segc_ref, segr_ref, out_ref, lse_ref):
    q, k, v = q_ref[0, 0], k_ref[0, 0], v_ref[0, 0]
    length, lanes = q.shape
    heads = lanes // HEAD_DIM
    lane = lax.broadcasted_iota(jnp.int32, (1, lanes), 1)
    same = segc_ref[0] == segr_ref[0]
    v_t = v.T

    def score(head):
        return nt(one_head(lane, head, k), q)

    mixed = []
    scores = score(0)
    for head in range(heads):
        following = score(head + 1) if head + 1 < heads else None
        masked = jnp.where(same, scores, F32(-1000000000.0 / SCALE))
        peak = jnp.max(masked, axis=0, keepdims=True) * SCALE2
        weights = jnp.exp2(masked * SCALE2 - peak)
        mass = jnp.sum(weights, axis=0, keepdims=True)
        rows = slice(head * HEAD_DIM, (head + 1) * HEAD_DIM)
        mixed.append(nn(v_t[rows, :], weights.astype(BF)) * (1.0 / mass))
        lse_ref[0, 0, head : head + 1, :] = peak + jnp.log2(mass)
        scores = following
    out_ref[0] = jnp.concatenate(mixed, axis=0).astype(BF).T
    lse_ref[0, 0, heads:, :] = jnp.zeros((lse_ref.shape[2] - heads, length), F32)


def attend_back_kernel(
    q_ref, k_ref, v_ref, segc_ref, segr_ref, lse_ref, o_ref, do_ref, gq_ref, gk_ref, gv_ref
):
    q, k, v, do = q_ref[0, 0], k_ref[0, 0], v_ref[0, 0], do_ref[0]
    lanes = q.shape[1]
    lane = lax.broadcasted_iota(jnp.int32, (1, lanes), 1)
    product = do.astype(F32) * o_ref[0].astype(F32)
    high = product.astype(BF)
    low = (product - high.astype(F32)).astype(BF)
    picker = (
        lax.broadcasted_iota(jnp.int32, (8, lanes), 0)
        == lax.broadcasted_iota(jnp.int32, (8, lanes), 1) // HEAD_DIM
    ).astype(BF)
    inner = nt(picker, high) + nt(picker, low)
    same = segc_ref[0] == segr_ref[0]
    grad_q = grad_k = grad_v = None
    for head in range(lanes // HEAD_DIM):
        k_mine = one_head(lane, head, k)
        masked = jnp.where(same, nt(k_mine, q), F32(-1000000000.0 / SCALE))
        probs = jnp.exp2(masked * SCALE2 - lse_ref[0, 0, head : head + 1, :])
        grad_probs = nt(one_head(lane, head, v), do)
        grad_scores = (probs * (grad_probs - inner[head : head + 1, :])).astype(BF)
        part_v = nn(probs.astype(BF), one_head(lane, head, do))
        part_k = nn(grad_scores, one_head(lane, head, q))
        part_q = tn(grad_scores, k_mine)
        grad_v = part_v if head == 0 else grad_v + part_v
        grad_k = part_k if head == 0 else grad_k + part_k
        grad_q = part_q if head == 0 else grad_q + part_q
    gq_ref[0] = (grad_q * SCALE).astype(BF)
    gk_ref[0] = (grad_k * SCALE).astype(BF)
    gv_ref[0] = grad_v.astype(BF)


def norm_parts(values):
    mean = jnp.mean(values, axis=-1, keepdims=True)
    centred = values - mean
    inverse = lax.rsqrt(jnp.mean(centred * centred, axis=-1, keepdims=True) + 1e-06)
    return centred * inverse, inverse


def norm_back(scaled, normed, inverse):
    mean_grad = jnp.mean(scaled, axis=-1, keepdims=True)
    mean_proj = jnp.mean(scaled * normed, axis=-1, keepdims=True)
    return (scaled - mean_grad - normed * mean_proj) * inverse


ROWS = 32


def by_rows(count, step):
    for row in range(0, count, ROWS):
        step(slice(row, row + ROWS))


def out_kernel(meta, ins, outs, weights, scratch):
    att_ref, x_ref, a_ref, b_ref, gain_ref, bias_ref = ins
    normed_ref, inverse_ref, low_ref, rank_ref = outs
    (w,) = weights
    (v_scr,) = scratch
    w.first_step()
    att = att_ref[0]
    rank = nt(att, a_ref[0, 0]).astype(BF)
    rank_ref[0] = rank
    width = w.scratch.shape[3]
    w.first_wait(0)
    w.first_wait(1)
    v_scr[...] = (
        nt(att[:, :width], w.cols(0, 0, width))
        + nt(att[:, width:], w.cols(1, 0, width))
        + nn(rank, b_ref[0, 0])
    )

    def step(rows):
        normed, inverse = norm_parts(v_scr[rows, :] + x_ref[0, rows, :].astype(F32))
        normed_ref[0, rows, :] = normed
        inverse_ref[0, rows, :] = jnp.broadcast_to(inverse, (ROWS, 128))
        low_ref[0, rows, :] = (normed * gain_ref[0:1, :] + bias_ref[0:1, :]).astype(BF)

    by_rows(v_scr.shape[0], step)


def gelu_parts(x):
    density = jnp.exp2((-0.5 * LOG2E) * x * x)
    t = 1.0 / (1.0 + (0.3275911 * 0.7071067811865476) * jnp.abs(x))
    poly = t * (
        0.127414796
        + t * (-0.142248368 + t * (0.7107068705 + t * (-0.7265760135 + t * 0.5307027145)))
    )
    tail = poly * density
    phi = jnp.where(x > 0, 1.0 - tail, tail)
    return x * phi, phi + x * (density * 0.3989422804014327)


CHUNK = 512


def up_kernel(meta, ins, outs, weights, scratch):
    m_ref, a_ref = ins[:2]
    b_refs = ins[2:]
    act_ref, slope_ref, rank_ref = outs
    (w,) = weights
    w.first_step()
    m = m_ref[0]
    rank = nt(m, a_ref[0]).astype(BF)
    rank_ref[0] = rank
    width = w.scratch.shape[3]
    for half, b_ref in enumerate(b_refs):
        w.first_wait_all(half)
        for lo in range(0, width, CHUNK):
            cols = slice(half * width + lo, half * width + lo + CHUNK)
            units = nn(m, w.cols(half, lo, CHUNK)) + nn(rank, b_ref[0, :, lo : lo + CHUNK])
            act, slope = gelu_parts(units)
            act_ref[0, :, cols] = act.astype(BF)
            slope_ref[0, :, cols] = slope.astype(BF)


def down_kernel(meta, ins, outs, weights, scratch):
    n1_ref, go_ref, a_ref, b_ref, gain_ref, bias_ref = ins[:6]
    parts = (len(ins) - 6) // 2
    act_refs, slope_refs = ins[6 : 6 + parts], ins[6 + parts :]
    out_ref, second_ref, gh_ref, ga_ref, gb_ref = outs
    (w,) = weights
    v_scr, gf_scr = scratch
    w.first_step()
    size = act_refs[0].shape[2] // 2
    places = [(half, p) for half in range(2) for p in range(parts)]
    start = lambda half, p: (half * parts + p) * size
    rank = sum(
        nt(act_refs[p][0, :, half * size : (half + 1) * size], a_ref[0, :, start(half, p) : start(half, p) + size])
        for half, p in places
    ).astype(BF)
    w.first_wait(0)
    w.first_wait(1)
    v_scr[...] = nn(rank, b_ref[0]) + sum(
        nt(act_refs[p][0, :, half * size : (half + 1) * size], w.cols(half, p * size, size))
        for half, p in places
    )

    def step(rows):
        middle = n1_ref[0, rows, :] * gain_ref[0:1, :] + bias_ref[0:1, :]
        normed, inverse = norm_parts(v_scr[rows, :] + middle)
        out_ref[0, rows, :] = (normed * gain_ref[1:2, :] + bias_ref[1:2, :]).astype(BF)
        second = norm_back(go_ref[0, rows, :].astype(F32) * gain_ref[1:2, :], normed, inverse)
        second_ref[0, rows, :] = second
        gf_scr[rows, :] = second.astype(BF)

    by_rows(v_scr.shape[0], step)
    grad_feed = gf_scr[...]
    gb_ref[0] = tn(rank, grad_feed).astype(BF)
    grad_rank = nt(grad_feed, b_ref[0]).astype(BF)
    for half, p in places:
        local = slice(half * size, (half + 1) * size)
        cols = slice(start(half, p), start(half, p) + size)
        grad_act = nn(grad_feed, w.cols(half, p * size, size)) + nn(grad_rank, a_ref[0, :, cols])
        gh_ref[0, :, cols] = (grad_act * slope_refs[p][0, :, local].astype(F32)).astype(BF)
        ga_ref[0, :, cols] = tn(grad_rank, act_refs[p][0, :, local]).astype(BF)


def mlp_back_kernel(meta, ins, outs, weights, scratch):
    (gh_ref, m_ref, n1_ref, r1_ref, second_ref, att_ref, ranku_ref, ranko_ref,
     ua_ref, ub_ref, oa_ref, ob_ref, gain_ref) = ins
    first_ref, gatt_ref, gua_ref, gub_ref, goa_ref, gob_ref = outs
    up, out = weights
    v_scr, gbr_scr = scratch
    up.first_step()
    out.first_step()
    width = up.scratch.shape[3]
    grad_rank = nt(gh_ref[0], ub_ref[0]).astype(BF)
    for loader in (up, out):
        loader.first_wait(0)
        loader.first_wait(1)
    v_scr[...] = (
        nt(gh_ref[0, :, :width], up.cols(0, 0, width))
        + nt(gh_ref[0, :, width:], up.cols(1, 0, width))
        + nn(grad_rank, ua_ref[0])
    )
    gua_ref[0] = tn(grad_rank, m_ref[0]).astype(BF)
    gub_ref[0] = tn(ranku_ref[0], gh_ref[0]).astype(BF)

    def step(rows):
        scaled = (second_ref[0, rows, :] + v_scr[rows, :]) * gain_ref[0:1, :]
        first = norm_back(scaled, n1_ref[0, rows, :], r1_ref[0, rows, 0:1])
        first_ref[0, rows, :] = first
        gbr_scr[rows, :] = first.astype(BF)

    by_rows(v_scr.shape[0], step)
    grad_branch = gbr_scr[...]
    grad_rank_out = nt(grad_branch, ob_ref[0, 0]).astype(BF)
    goa_ref[0] = tn(grad_rank_out, att_ref[0]).astype(BF)
    gob_ref[0] = tn(ranko_ref[0], grad_branch).astype(BF)
    owidth = out.scratch.shape[3]
    for half in range(2):
        cols = slice(half * owidth, (half + 1) * owidth)
        full = nn(grad_branch, out.cols(half, 0, owidth)) + nn(grad_rank_out, oa_ref[0, 0, :, cols])
        gatt_ref[0, :, cols] = full.astype(BF)


def rank_back_kernel(meta, ins, outs, weights, scratch):
    gq_ref, gk_ref, gv_ref, x_ref, rank_ref, b_ref = ins
    gr_ref, a_refs, b_refs = outs[0], outs[1:4], outs[4:]
    size = b_ref.shape[2]
    ranks = []
    for slot, ref in enumerate((gq_ref, gk_ref, gv_ref)):
        grad = ref[0]
        ranks.append(nt(b_ref[slot, 0], grad))
        b_refs[slot][0] = tn(rank_ref[0, :, slot * size : (slot + 1) * size], grad).astype(BF)
    stacked = jnp.concatenate(ranks, axis=0).astype(BF)
    gr_ref[0] = stacked
    products = nn(stacked, x_ref[0]).astype(BF)
    for slot, ref in enumerate(a_refs):
        ref[0] = products[slot * size : (slot + 1) * size]


def qkv_back_kernel(meta, ins, outs, weights, scratch):
    gq_ref, gk_ref, gv_ref, gr_ref, first_ref, a_ref = ins
    (out_ref,) = outs
    (w,) = weights
    w.first_step()
    slots = 3
    width = w.scratch.shape[3] // slots
    size = a_ref.shape[2]
    total = first_ref[0] + tn(
        gr_ref[0], a_ref[0:slots, 0].reshape(slots * size, out_ref.shape[2])
    )
    for other in range(2):
        w.first_wait(other)
        half = w.t ^ other
        cols = pl.ds(pl.multiple_of(half * width, width), width)
        for slot, ref in enumerate((gq_ref, gk_ref, gv_ref)):
            total += nt(ref[0, :, cols], w.cols(half, slot * width, width))
    out_ref[0] = total


def call(kernel, meta, ins, outs, flops, scratch=(), weights=(), limit=VMEM, after=()):
    plans = [weight_plan(pieces, first, width) for pieces, first, width, _, _ in weights]
    n_in, n_out, n_w = len(ins), len(outs), len(weights)
    counts = [len(arrays) for arrays, _ in plans]
    steps = meta.shape[0] - 2
    after = [a for a in after if a is not None]
    n_after = len(after)

    def body(meta_ref, *refs):
        refs = list(refs)
        take = lambda n: [refs.pop(0) for _ in range(n)]
        in_refs = take(n_in)
        w_refs = [take(n) for n in counts]
        take(n_after)
        out_refs = take(n_out)
        w_scr = take(n_w)
        w_sem = take(n_w)
        me, t = meta_ref[steps], meta_ref[steps + 1]
        loaders = [
            Loader(plan, r, s, m, me, t)
            for (_, plan), r, s, m in zip(plans, w_refs, w_scr, w_sem)
        ]
        kernel(meta_ref, in_refs, out_refs, loaders, refs)

    w_arrays = [a for arrays, _ in plans for a in arrays]
    nbytes = sum(a.size * a.dtype.itemsize for a, _, _ in ins)
    nbytes += sum(2 * dp * rows * width * 2 for _, _, width, dp, rows in weights)
    for shape, dtype, _, _ in outs:
        size = jnp.dtype(dtype).itemsize
        for extent in shape:
            size *= extent
        nbytes += size
    return pl.pallas_call(
        body,
        grid_spec=pltpu.PrefetchScalarGridSpec(
            num_scalar_prefetch=1,
            grid=(steps,),
            in_specs=[pl.BlockSpec(block, index) for _, block, index in ins]
            + [pl.BlockSpec(memory_space=pltpu.HBM) for _ in [*w_arrays, *after]],
            out_specs=[pl.BlockSpec(block, index) for _, _, block, index in outs],
            scratch_shapes=[pltpu.VMEM((2, dp, rows, width), BF) for _, _, width, dp, rows in weights]
            + [pltpu.SemaphoreType.DMA((2,)) for _ in weights]
            + list(scratch),
        ),
        out_shape=[pltpu.HBM(shape, dtype) for shape, dtype, _, _ in outs],
        **params(flops, nbytes, limit),
    )(meta, *[in_hbm(a) for a in [*[a for a, _, _ in ins], *w_arrays, *after]])


def pack(outs, fresh=(), after=()):
    after = [a for a in after if a is not None]
    arrays, plan, heights, widths = [], [], [], []

    def slot(array):
        for index, known in enumerate(arrays):
            if known is array:
                return index
        arrays.append(array)
        return len(arrays) - 1

    for index, parts in enumerate(outs):
        row = 0
        for part in parts:
            array, at, count, col, cols, into, advance = part
            plan.append((slot(array), at, count, col, cols, index, row, into))
            if advance:
                row += count
        heights.append(row)
        widths.append(max(part[4] + part[5] for part in parts))
    for array in after:
        slot(array)
    n_in = len(arrays)

    near = [any(a is f for f in fresh) for a in arrays]

    def kernel(*refs):
        ins, results, sems = refs[:n_in], refs[n_in:-1], refs[-1]
        copies = []
        for number, (a, at, count, col, cols, o, row, into) in enumerate(plan):
            source = ins[a].at[pl.ds(at, count), pl.ds(col, cols)]
            target = results[o].at[pl.ds(row, count), pl.ds(into, cols)]
            if not near[a]:
                copy = pltpu.make_async_copy(source, target, sems.at[number])
                copy.start()
                copies.append(copy)
        for a, at, count, col, cols, o, row, into in plan:
            if near[a]:
                results[o][pl.ds(row, count), pl.ds(into, cols)] = ins[a][pl.ds(at, count), pl.ds(col, cols)]
        for copy in copies:
            copy.wait()

    spaces = [pltpu.VMEM if n else pltpu.HBM for n in near]
    return pl.pallas_call(
        kernel,
        in_specs=[pl.BlockSpec(memory_space=space) for space in spaces],
        out_specs=[pl.BlockSpec(memory_space=pltpu.VMEM)] * len(outs),
        out_shape=[pltpu.VMEM(shape, BF) for shape in zip(heights, widths)],
        scratch_shapes=[pltpu.SemaphoreType.DMA((len(plan),))],
        compiler_params=pltpu.CompilerParams(vmem_limit_bytes=8 * 2**20),
        cost_estimate=pl.CostEstimate(
            flops=0, bytes_accessed=sum(h * w * 4 for h, w in zip(heights, widths)), transcendentals=0
        ),
    )(*[pltpu.with_memory_space_constraint(a, space) for a, space in zip(arrays, spaces)])


def in_hbm(array):
    return pltpu.with_memory_space_constraint(array, pltpu.HBM)


X, Y, Z1, Z2, Z3 = 1, 2, 4, 8, 12
ZS = (Z1, Z2, Z3)


def hop(array, bits):
    return lax.ppermute(array, "dp", [(i, i ^ bits) for i in range(lax.axis_size("dp"))])


def swap(array):
    return lax.ppermute(array, "tensor", [(0, 1), (1, 0)])


class Gather:
    def __init__(self, w_qkv, w_out, w_up, w_down):
        self.n = n = w_up.shape[0]
        self.h = n // 2
        self.pieces = []
        o, u = w_qkv.shape[2], w_up.shape[1]
        self.width = 3 * o
        flat = w_qkv.reshape(3 * n, o)
        wo, wd = w_out.T, w_down.T
        queries = [(flat, slot * n, n, 0, o, slot * o, slot == 2) for slot in range(3)]
        rest = [
            (wo, 0, n, 0, o, 0, False), (w_up, 0, n, 0, 2 * o, o, True),
            (w_up, 0, n, 2 * o, u - 2 * o, 0, False), (wd, 0, n, 0, o, 2 * o, True),
            (wd, 0, n, o, 3 * o, 0, True),
        ]
        self.own, self.q = pack([queries + rest, queries])
        self.e, self.f, self.g = (self.cut(p) for p in (1, 2, 3))

    def cut(self, piece):
        return lax.slice_in_dim(self.own, piece * self.n, (piece + 1) * self.n, axis=0)

    def note(self, array, items, other=0):
        at = 0
        for piece, rel, row, count in items:
            self.pieces.append(Piece(piece * self.width, self.width, rel, row, count, array, at, other))
            at += count

    def part(self, array, at, count):
        return (array, at, count, 0, self.width, 0, True)

    def full(self, piece, *rels):
        return [(piece, rel, 0, self.n) for rel in rels]

    def upper(self, piece, *rels):
        return [(piece, rel, self.h, self.h) for rel in rels]

    def lower(self, piece, *rels):
        return [(piece, rel, 0, self.h) for rel in rels]

    def exchange(self, arrays, after=()):
        fresh = [a for a, _ in arrays if a is not self.own]
        (packed,) = pack([[self.part(a, 0, a.shape[0]) for a, _ in arrays]], fresh=fresh, after=after)
        other = swap(packed)
        self.note(other, [item for _, items in arrays for item in items], 1)
        return packed, other

    def keep(self, got):
        for array, items in got:
            self.note(array, items)
        return got

    def round1(self):
        self.zq = [hop(self.q, k) for k in ZS]
        self.x1, self.y1 = hop(self.own, X), hop(self.own, Y)
        every = range(4)
        got = [(self.own, [i for p in every for i in self.full(p, 0)])]
        got += [(self.x1, [i for p in every for i in self.full(p, X)])]
        got += [(self.y1, [i for p in every for i in self.full(p, Y)])]
        got += [(z, self.full(0, k)) for z, k in zip(self.zq, ZS)]
        self.got1 = self.keep(got)

    def round2(self, after):
        n, h, part = self.n, self.h, self.part
        along = [part(z, 0, n) for z in self.zq]
        xin, yin, e = pack(
            [along + [part(self.y1, h, h)], along + [part(self.x1, 0, h)], [part(self.own, n, n)]],
            fresh=[*self.zq, self.x1, self.y1],
            after=after,
        )
        x, y, self.ze2 = hop(xin, X), hop(yin, Y), hop(e, Z2)
        self.x, self.y = x, y
        self.got2 = self.keep([
            (x, self.full(0, *(X | k for k in ZS)) + self.upper(0, X | Y)),
            (y, self.full(0, *(Y | k for k in ZS)) + self.lower(0, X | Y)),
            (self.ze2, self.full(1, Z2)),
        ])
        return self.exchange(self.got1, [xin])

    def round3(self, after):
        n, h, part = self.n, self.h, self.part
        xin, yin, e, f = pack(
            [
                [part(self.y, i * n + h, h) for i in range(3)] + [part(self.y1, p * n + h, h) for p in (1, 2)],
                [part(self.x, i * n, h) for i in range(3)] + [part(self.x1, p * n, h) for p in (1, 2)],
                [part(self.own, n, n), part(self.ze2, 0, n)],
                [part(self.own, 2 * n, n)],
            ],
            fresh=[self.x, self.y, self.ze2],
            after=after,
        )
        x, y, self.ze1, self.zf2 = hop(xin, X), hop(yin, Y), hop(e, Z1), hop(f, Z2)
        self.x, self.y = x, y
        both = [X | Y | k for k in ZS]
        self.got3 = self.keep([
            (x, self.upper(0, *both) + self.upper(1, X | Y) + self.upper(2, X | Y)),
            (y, self.lower(0, *both) + self.lower(1, X | Y) + self.lower(2, X | Y)),
        ])
        self.late3 = self.keep([(self.ze1, self.full(1, Z1, Z3)), (self.zf2, self.full(2, Z2))])
        return self.exchange(self.got2, [xin])

    def round4(self, after):
        n, h, part = self.n, self.h, self.part
        along = [part(self.ze1, 0, n), part(self.ze2, 0, n), part(self.ze1, n, n)]
        xin, yin, f, g = pack(
            [
                along + [part(self.y1, 3 * n + h, h)],
                along + [part(self.x1, 3 * n, h)],
                [part(self.own, 2 * n, n), part(self.zf2, 0, n)],
                [part(self.own, 3 * n, n)],
            ],
            fresh=[self.ze1, self.zf2],
            after=after,
        )
        x, y, self.zf1, self.zg2 = hop(xin, X), hop(yin, Y), hop(f, Z1), hop(g, Z2)
        self.x, self.y = x, y
        self.got4 = self.keep([
            (x, self.full(1, *(X | k for k in ZS)) + self.upper(3, X | Y)),
            (y, self.full(1, *(Y | k for k in ZS)) + self.lower(3, X | Y)),
            (self.zf1, self.full(2, Z1, Z3)),
            (self.zg2, self.full(3, Z2)),
        ])
        return self.exchange(self.got3, [xin])

    def round5(self, after):
        n, h, part = self.n, self.h, self.part
        along = [part(self.zf1, 0, n), part(self.zf2, 0, n), part(self.zf1, n, n)]
        xin, yin, g, d = pack(
            [
                [part(self.y, i * n + h, h) for i in range(3)] + along,
                [part(self.x, i * n, h) for i in range(3)] + along,
                [part(self.own, 3 * n, n), part(self.zg2, 0, n)],
                [part(self.y, 3 * n, h), part(self.x, 3 * n, h)],
            ],
            fresh=[self.x, self.y, self.zf1, self.zg2],
            after=after,
        )
        self.d = d
        x, y, self.zg1, self.zd2 = hop(xin, X), hop(yin, Y), hop(g, Z1), hop(d, Z2)
        self.x, self.y = x, y
        both = [X | Y | k for k in ZS]
        self.got5 = self.keep([
            (x, self.upper(1, *both) + self.full(2, *(X | k for k in ZS))),
            (y, self.lower(1, *both) + self.full(2, *(Y | k for k in ZS))),
            (self.zg1, self.full(3, Z1, Z3)),
            (self.zd2, self.full(3, X | Y | Z2)),
        ])
        return self.exchange(self.late3 + self.got4, [xin])

    def round6(self, after):
        n, h, part = self.n, self.h, self.part
        along = [part(self.zg1, 0, n), part(self.zg2, 0, n), part(self.zg1, n, n)]
        xin, yin, d = pack(
            [
                [part(self.y, 3 * h + i * n + h, h) for i in range(3)] + along,
                [part(self.x, 3 * h + i * n, h) for i in range(3)] + along,
                [part(self.d, 0, n), part(self.zd2, 0, n)],
            ],
            fresh=[self.x, self.y, self.zg1, self.zd2],
            after=after,
        )
        x, y, zd1 = hop(xin, X), hop(yin, Y), hop(d, Z1)
        both = [X | Y | k for k in ZS]
        self.got6 = self.keep([
            (x, self.upper(2, *both) + self.full(3, *(X | k for k in ZS))),
            (y, self.lower(2, *both) + self.full(3, *(Y | k for k in ZS))),
            (zd1, self.full(3, X | Y | Z1, X | Y | Z3)),
        ])
        return self.exchange(self.got5, [xin])

    def last(self, after):
        return self.exchange(self.got6, after)


class GatherPlain:
    def __init__(self, w_qkv, w_out, w_up, w_down):
        local = jnp.concatenate([w_qkv[0], w_qkv[1], w_qkv[2], w_out.T, w_up, w_down.T], axis=1)
        rows, width = local.shape
        whole = lax.all_gather(local, ("dp", "tensor")).reshape(lax.axis_size("dp"), 2, rows, width)
        self.pieces = [Piece(0, width, None, 0, 0, whole, 0, other) for other in range(2)]

    def round1(self):
        return None

    def round2(self, after):
        return None, None

    round3 = round4 = round5 = round6 = last = round2


class Spot:
    def __init__(self, array, row, rows, col, cols):
        self.array, self.row, self.rows, self.col, self.cols = array, row, rows, col, cols

    def of(self, ref, me, t):
        at = lambda v, unit: pl.multiple_of(v(me, t), unit) if callable(v) else v
        return ref.at[pl.ds(at(self.row, 16), self.rows), pl.ds(at(self.col, 128), self.cols)]


def arrange(where, shapes, moves, fresh=(), after=()):
    arrays = []
    for source, _, _ in moves:
        if not any(a is source.array for a in arrays):
            arrays.append(source.array)
    used = len(arrays)
    arrays += [a for a in after if a is not None]
    near = [any(a is f for f in fresh) for a in arrays]
    number = lambda array: next(i for i, a in enumerate(arrays) if a is array)
    plan = [(number(source.array), source, out, target) for source, out, target in moves]

    def kernel(where_ref, *refs):
        ins, results, sems = refs[: len(arrays)], refs[len(arrays) : -1], refs[-1]
        me, t = where_ref[0], where_ref[1]
        copies = []
        for index, (slot, source, out, target) in enumerate(plan):
            copy = pltpu.make_async_copy(
                source.of(ins[slot], me, t), target.of(results[out], me, t), sems.at[index]
            )
            copy.start()
            copies.append(copy)
        for copy in copies:
            copy.wait()

    spaces = [pltpu.VMEM if n else pltpu.HBM for n in near]
    return pl.pallas_call(
        kernel,
        in_specs=[pl.BlockSpec(memory_space=pltpu.SMEM)] + [pl.BlockSpec(memory_space=m) for m in spaces],
        out_specs=[pl.BlockSpec(memory_space=pltpu.VMEM)] * len(shapes),
        out_shape=[pltpu.VMEM(shape, BF) for shape in shapes],
        scratch_shapes=[pltpu.SemaphoreType.DMA((len(plan),))],
        compiler_params=pltpu.CompilerParams(vmem_limit_bytes=8 * 2**20),
        cost_estimate=pl.CostEstimate(
            flops=0, bytes_accessed=sum(h * w * 4 for h, w in shapes), transcendentals=0
        ),
    )(where, *[pltpu.with_memory_space_constraint(a, m) for a, m in zip(arrays, spaces)])


class GradientSum:
    def __init__(self, where, arrays, mine, rank, adapters):
        self.where, self.arrays = where, arrays
        self.mine, self.rank, self.adapters = mine, rank, adapters
        self.rows = mine * rank
        self.widths = [a.shape[1] for a in arrays]
        self.starts = [sum(self.widths[:i]) for i in range(len(arrays))]
        self.total = sum(self.widths)
        self.chunk = self.total // 8

    def cores(self, after=()):
        half = self.total // 2
        moves = [
            (
                Spot(a, 0, self.rows, lambda me, t, w=w: (1 - t) * (w // 2), w // 2),
                0,
                Spot(None, 0, self.rows, s // 2, w // 2),
            )
            for a, w, s in zip(self.arrays, self.widths, self.starts)
        ]
        (out,) = arrange(self.where, [(self.rows, half)], moves, after=after)
        self.other = swap(out)
        return out

    def plane(self, after=()):
        moves = []
        for k in range(4):
            for a, w, s in zip(self.arrays, self.widths, self.starts):
                e = w // 8
                moves.append((
                    Spot(a, 0, self.rows, lambda me, t, e=e, k=k: (t * 4 + ((me & 3) ^ k)) * e, e),
                    k,
                    Spot(None, 0, self.rows, s // 8, e),
                ))
                moves.append((
                    Spot(self.other, 0, self.rows, lambda me, t, e=e, s=s, k=k: s // 2 + ((me & 3) ^ k) * e, e),
                    k,
                    Spot(None, self.rows, self.rows, s // 8, e),
                ))
        outs = arrange(self.where, [(2 * self.rows, self.chunk)] * 4, moves, fresh=[self.other], after=after)
        self.parts = [outs[0], hop(outs[1], X), hop(outs[2], Y), hop(outs[3], X | Y)]
        return outs[0]

    def fold(self, after=()):
        rank, chunk, count = self.rank, self.chunk, 2 * self.mine
        quarter = self.adapters * rank // 4
        after = [a for a in after if a is not None]

        def kernel(where_ref, *refs):
            ins, outs, total = refs[:4], refs[4 + len(after) : 8 + len(after)], refs[-1]
            z = where_ref[0] // 4
            total[...] = jnp.zeros_like(total)
            for k in range(4):
                for index in range(count):
                    pick = where_ref[2 + k * count + index]
                    into = pl.ds(pl.multiple_of(pick * rank, rank), rank)
                    total[into, :] += ins[k][index * rank : (index + 1) * rank, :].astype(F32)
            for k in range(4):
                rows = pl.ds(pl.multiple_of((z ^ k) * quarter, quarter), quarter)
                outs[k][...] = total[rows, :].astype(BF)

        outs = self.local(kernel, self.parts, after, [(quarter, chunk)] * 4, [(self.adapters * rank, chunk)])
        self.parts = [outs[0]] + [hop(outs[k], 4 * k) for k in (1, 2, 3)]
        return outs[0]

    def local(self, kernel, arrays, after, shapes, scratch):
        vmem = pl.BlockSpec(memory_space=pltpu.VMEM)
        return pl.pallas_call(
            kernel,
            in_specs=[pl.BlockSpec(memory_space=pltpu.SMEM)]
            + [vmem] * len(arrays)
            + [pl.BlockSpec(memory_space=pltpu.HBM)] * len(after),
            out_specs=[vmem] * len(shapes),
            out_shape=[pltpu.VMEM(shape, BF) for shape in shapes],
            scratch_shapes=[pltpu.VMEM(shape, F32) for shape in scratch],
            compiler_params=pltpu.CompilerParams(vmem_limit_bytes=12 * 2**20),
            cost_estimate=pl.CostEstimate(
                flops=0, bytes_accessed=sum(h * w * 8 for h, w in shapes), transcendentals=0
            ),
        )(
            self.where,
            *[pltpu.with_memory_space_constraint(a, pltpu.VMEM) for a in arrays],
            *[in_hbm(a) for a in after],
        )

    def depth(self, after=()):
        after = [a for a in after if a is not None]

        def kernel(where_ref, *refs):
            total = refs[0][...].astype(F32)
            for ref in refs[1:4]:
                total += ref[...].astype(F32)
            refs[-1][...] = total.astype(BF)

        (out,) = self.local(kernel, self.parts, after, [self.parts[0].shape], [])
        self.parts = [out] + [hop(out, 4 * k) for k in (1, 2, 3)]
        return out

    def back(self, after=()):
        quarter = self.adapters * self.rank // 4
        moves = [
            (
                Spot(self.parts[k], 0, quarter, 0, self.chunk),
                0,
                Spot(None, lambda me, t, k=k: ((me >> 2) ^ k) * quarter, quarter, 0, self.chunk),
            )
            for k in range(4)
        ]
        tall = self.adapters * self.rank
        (out,) = arrange(self.where, [(tall, self.chunk)], moves, fresh=self.parts, after=after)
        self.parts = [out, hop(out, X), hop(out, Y), hop(out, X | Y)]
        return out

    def give(self, after=()):
        tall = self.adapters * self.rank
        moves = [
            (Spot(part, 0, tall, 0, self.chunk), 0, Spot(None, k * tall, tall, 0, self.chunk))
            for k, part in enumerate(self.parts)
        ]
        (out,) = arrange(self.where, [(4 * tall, self.chunk)], moves, fresh=self.parts, after=after)
        self.theirs = swap(out)
        self.ours = out
        return out


def finish(where, sums, results, after=()):
    tall = sums[0].adapters * sums[0].rank
    after = [a for a in after if a is not None]
    inputs = [a for s in sums for a in (s.ours, s.theirs)]

    def kernel(where_ref, *refs):
        outs = refs[len(inputs) + len(after) :]
        me, t = where_ref[0], where_ref[1]
        for out, parts in zip(outs, results):
            for place, (number, which) in enumerate(parts):
                total = sums[number]
                start, width = total.starts[which] // 8, total.widths[which] // 8
                for core in range(2):
                    for k in range(4):
                        column = ((t ^ core) * 4 + ((me & 3) ^ k)) * width
                        out[place * tall : (place + 1) * tall, pl.ds(pl.multiple_of(column, 128), width)] = refs[
                            2 * number + core
                        ][k * tall : (k + 1) * tall, start : start + width].astype(F32)

    vmem = pl.BlockSpec(memory_space=pltpu.VMEM)
    shapes = [(len(parts) * tall, sums[parts[0][0]].widths[parts[0][1]]) for parts in results]
    return pl.pallas_call(
        kernel,
        in_specs=[pl.BlockSpec(memory_space=pltpu.SMEM)]
        + [vmem] * len(inputs)
        + [pl.BlockSpec(memory_space=pltpu.HBM)] * len(after),
        out_specs=[vmem] * len(results),
        out_shape=[jax.ShapeDtypeStruct(shape, F32) for shape in shapes],
        compiler_params=pltpu.CompilerParams(vmem_limit_bytes=32 * 2**20),
        cost_estimate=pl.CostEstimate(
            flops=0, bytes_accessed=sum(h * w * 6 for h, w in shapes), transcendentals=0
        ),
    )(where, *inputs, *[in_hbm(a) for a in after])


def shards(
    hidden_in, segment_ids, adapter_pick, w_qkv, w_out, w_up, w_down, ln_gain, ln_bias,
    adapt_a, adapt_b, up_a, up_b, down_a, down_b, grad_out,
):
    dp = lax.axis_size("dp")
    t = lax.axis_index("tensor")
    block, ff_half = w_up.shape
    width = hidden_in.shape[2]
    half = width // 2
    ff = 2 * ff_half
    positions = hidden_in.shape[1]
    length = 2 * positions
    mine = hidden_in.shape[0] // 2
    rank = adapt_b.shape[2]
    adapters = adapt_b.shape[1]

    def to_sequences(piece):
        there = swap(lax.dynamic_slice_in_dim(piece, mine * (1 - t), mine, 0))
        here = lax.dynamic_slice_in_dim(piece, mine * t, mine, 0)
        low = jnp.where(t == 0, here, there)
        high = jnp.where(t == 0, there, here)
        return jnp.concatenate([low, high], axis=1)

    def to_positions(value):
        here = lax.dynamic_slice_in_dim(value, positions * t, positions, 1)
        there = swap(lax.dynamic_slice_in_dim(value, positions * (1 - t), positions, 1))
        low = jnp.where(t == 0, here, there)
        high = jnp.where(t == 0, there, here)
        return jnp.concatenate([low, high], axis=0)

    gather = (Gather if dp == 16 else GatherPlain)(w_qkv, w_out, w_up, w_down)
    gather.round1()
    x, cotangent = to_sequences(hidden_in), to_sequences(grad_out)
    def columns(first, count):
        return (gather.pieces, first, count, dp, block)

    qkv_w = columns(0, 3 * half)
    out_w = columns(3 * half, half)
    part = 2 * half
    up_parts = [columns(4 * half + p, part) for p in range(0, ff_half, part)]
    up_w = columns(4 * half, ff_half)
    down_w = columns(4 * half + ff_half, ff_half)

    segs = lax.dynamic_slice_in_dim(segment_ids, mine * t, mine, 0)
    pick = lax.dynamic_slice_in_dim(adapter_pick, mine * t, mine, 0)
    meta = jnp.concatenate([pick, jnp.stack([lax.axis_index("dp"), t]).astype(pick.dtype)])
    if dp == 16:
        ordered = jnp.where(t == 0, adapter_pick, jnp.roll(adapter_pick, -mine))
        plane = [ordered, hop(ordered, X), hop(ordered, Y), hop(ordered, X | Y)]
        where = jnp.concatenate([meta[mine:], *plane])
    seg_col = segs.reshape(mine, length, 1)
    seg_row = segs.reshape(mine, 1, length)
    a_t = jnp.swapaxes(adapt_a, 2, 3)
    ua_t = jnp.swapaxes(up_a, 1, 2)
    da_t = jnp.swapaxes(down_a, 1, 2)

    _, met = gather.round2([x, cotangent, meta, seg_col, seg_row])
    _, met = gather.round3([met])
    gate, _ = gather.round4([met])
    tokens = mine * length
    seq3 = lambda s, m: (s, 0, 0)
    seq4 = lambda s, m: (s, 0, 0, 0)
    fixed2 = lambda s, m: (0, 0)
    picked3 = lambda s, m: (m[s], 0, 0)
    slots4 = lambda s, m: (0, m[s], 0, 0)
    last4 = lambda s, m: (3, m[s], 0, 0)
    row = lambda a: (a, (1, *a.shape[1:]), seq3 if a.ndim == 3 else seq4)
    whole = lambda a: (a, a.shape, fixed2)
    factor = lambda a: (a, (1, *a.shape[1:]), picked3)
    slots = lambda a: (a, (a.shape[0], 1, *a.shape[2:]), slots4)
    last = lambda a: (a, (1, 1, *a.shape[2:]), last4)
    made = lambda dtype, *shape: ((mine, *shape), dtype, (1, *shape), seq3 if len(shape) == 2 else seq4)

    qkv, rank_qkv = call(
        qkv_kernel, meta,
        [row(x), slots(a_t), slots(adapt_b)],
        [made(BF, 3, length, width), made(BF, length, 3 * rank)],
        6 * tokens * width * width,
        weights=[qkv_w],
        after=[gate],
        limit=28 * 2**20,
    )
    gate, met = gather.round5([qkv])

    groups = width // GROUP

    def heads_of(slot, first=0):
        return pl.BlockSpec((1, 1, length, GROUP), lambda s, h: (s + first, slot, 0, h))

    def seg_specs(first=0):
        return [
            pl.BlockSpec((1, length, 1), lambda s, h: (s + first, 0, 0)),
            pl.BlockSpec((1, 1, length), lambda s, h: (s + first, 0, 0)),
        ]

    lse_spec = pl.BlockSpec((1, 1, 8, length), lambda s, h: (s, h, 0, 0))
    heads_spec = pl.BlockSpec((1, length, GROUP), lambda s, h: (s, 0, h))

    def attend(first, after):
        after = [a for a in after if a is not None]

        def body(q, k, v, sc, sr, *refs):
            attend_kernel(q, k, v, sc, sr, *refs[len(after) :])

        return pl.pallas_call(
            body,
            grid=(1, groups),
            in_specs=[heads_of(j, first) for j in range(3)]
            + seg_specs(first)
            + [pl.BlockSpec(memory_space=pltpu.HBM) for _ in after],
            out_specs=[heads_spec, lse_spec],
            out_shape=[
                pltpu.HBM((1, length, width), BF),
                pltpu.HBM((1, groups, 8, length), F32),
            ],
            **params(16 * length * length * width, length * width * 8, 24 * 2**20),
        )(*[in_hbm(a) for a in [qkv, qkv, qkv, seg_col, seg_row, *after]])

    attended = []
    for index in range(mine):
        attended.append(attend(index, [gate]))
        gate = attended[-1][1]
    gate, _ = gather.round6([gate, met])
    attention = jnp.concatenate([a for a, _ in attended], axis=0)
    lse = jnp.concatenate([a for _, a in attended], axis=0)

    normed, inverse, middle_low, rank_out = call(
        out_kernel, meta,
        [row(attention), row(x), last(a_t), last(adapt_b), whole(ln_gain), whole(ln_bias)],
        [made(F32, length, width), made(F32, length, 128), made(BF, length, width), made(BF, length, rank)],
        2 * tokens * width * width,
        scratch=[pltpu.VMEM((length, width), F32)],
        weights=[out_w],
        limit=28 * 2**20,
        after=[gate],
    )

    gate, _ = gather.last([rank_out])
    acts, slopes, rank_up = [], [], None
    for index, weight in enumerate(up_parts):
        blocks = ff_half // part
        up_cols = [
            (up_b, (1, rank, part), lambda s, m, at=h * blocks + index: (m[s], 0, at)) for h in range(2)
        ]
        act, slope, rank_up = call(
            up_kernel, meta,
            [row(middle_low), factor(ua_t), *up_cols],
            [made(BF, length, 2 * part), made(BF, length, 2 * part), made(BF, length, rank)],
            4 * tokens * width * part * 2,
            weights=[weight],
            limit=36 * 2**20,
            after=[gate],
        )
        gate = rank_up
        acts.append(act)
        slopes.append(slope)

    layer_out, second, grad_hidden, g_down_a, g_down_b = call(
        down_kernel, meta,
        [row(normed), row(cotangent), factor(da_t), factor(down_b), whole(ln_gain), whole(ln_bias),
         *[row(a) for a in acts], *[row(a) for a in slopes]],
        [made(BF, length, width), made(F32, length, width), made(BF, length, ff),
         made(BF, rank, ff), made(BF, rank, width)],
        4 * tokens * width * ff,
        scratch=[pltpu.VMEM((length, width), F32), pltpu.VMEM((length, width), BF)],
        weights=[down_w],
    )

    grad_first, grad_att, g_up_a, g_up_b, g_out_a, g_out_b = call(
        mlp_back_kernel, meta,
        [row(grad_hidden), row(middle_low), row(normed), row(inverse), row(second), row(attention),
         row(rank_up), row(rank_out), factor(ua_t), factor(up_b), last(a_t), last(adapt_b),
         whole(ln_gain)],
        [made(F32, length, width), made(BF, length, width), made(BF, rank, width),
         made(BF, rank, ff), made(BF, rank, width), made(BF, rank, width)],
        2 * tokens * width * (ff + width),
        scratch=[pltpu.VMEM((length, width), F32), pltpu.VMEM((length, width), BF)],
        weights=[up_w, out_w],
    )

    flat = lambda g: g.reshape(mine * rank, g.shape[-1])
    seqs = [g_down_a, g_down_b, g_up_a, g_up_b, g_out_a, g_out_b]
    fast = dp == 16
    if fast:
        first_sum = GradientSum(where, [flat(g) for g in seqs], mine, rank, adapters)
        gate = first_sum.cores()
    else:
        gate = None

    def attend_back(first, after):
        after = [a for a in after if a is not None]

        def body(q, k, v, sc, sr, l, o, do, *refs):
            attend_back_kernel(q, k, v, sc, sr, l, o, do, *refs[len(after) :])

        from_seq = pl.BlockSpec((1, length, GROUP), lambda s, h: (s + first, 0, h))
        args = [qkv, qkv, qkv, seg_col, seg_row, attended[first][1], attended[first][0], grad_att, *after]
        return pl.pallas_call(
            body,
            grid=(1, groups),
            in_specs=[heads_of(j, first) for j in range(3)]
            + seg_specs(first)
            + [lse_spec, heads_spec, from_seq]
            + [pl.BlockSpec(memory_space=pltpu.HBM) for _ in after],
            out_specs=[heads_spec] * 3,
            out_shape=[pltpu.HBM((1, length, width), BF)] * 3,
            **params(40 * length * length * width, length * width * 16, 32 * 2**20),
        )(*[in_hbm(a) for a in args])

    grads_qkv = []
    for index in range(mine):
        grads_qkv.append(attend_back(index, [gate]))
        gate = grads_qkv[-1][0]
        if fast and index == 0:
            gate = first_sum.plane([gate])
    if fast:
        gate = first_sum.fold([gate])

    one3 = lambda s, m: (0, 0, 0)

    def per_sequence(index, meta_at):
        own = [(g, (1, length, width), one3) for g in grads_qkv[index]]
        pick_row = lambda a: (a, (1, *a.shape[1:]), lambda s, m: (index, *([0] * (a.ndim - 1))))
        pick_slots = lambda a: (a, (a.shape[0], 1, *a.shape[2:]), lambda s, m: (0, m[s], 0, 0))
        return own, pick_row, pick_slots

    def one(dtype, *shape):
        return ((1, *shape), dtype, (1, *shape), one3)

    metas = [jnp.concatenate([meta[i : i + 1], meta[mine:]]) for i in range(mine)]
    ranked = []
    for index in range(mine):
        own, pick_row, pick_slots = per_sequence(index, metas[index])
        ranked.append(call(
            rank_back_kernel, metas[index],
            own + [pick_row(x), pick_row(rank_qkv), pick_slots(adapt_b)],
            [one(BF, 3 * rank, length)] + [one(BF, rank, width)] * 6,
            18 * length * width * rank,
            after=[gate],
            limit=32 * 2**20,
        ))
        gate = ranked[-1][0]
    later = [jnp.concatenate([r[1 + j] for r in ranked], axis=0) for j in range(6)]
    if fast:
        second_sum = GradientSum(where, [flat(g) for g in later], mine, rank, adapters)
        gate = second_sum.cores([gate])
        gate = first_sum.depth([gate])

    grad_ins = []
    for index in range(mine):
        own, pick_row, pick_slots = per_sequence(index, metas[index])
        (piece,) = call(
            qkv_back_kernel, metas[index],
            own + [(ranked[index][0], (1, 3 * rank, length), one3), pick_row(grad_first), pick_slots(a_t)],
            [one(F32, length, width)],
            6 * length * width * width,
            weights=[qkv_w],
            after=[gate],
            limit=32 * 2**20,
        )
        grad_ins.append(piece)
        gate = piece
        if fast and index == 0:
            gate = second_sum.plane([gate])
            gate = first_sum.back([gate])
    grad_in = jnp.concatenate(grad_ins, axis=0)
    turned = lambda v: jnp.swapaxes(v, -1, -2)
    if fast:
        gate = second_sum.fold([gate])
        gate = first_sum.give([gate])
        gate = second_sum.depth([gate])
        done1 = finish(where, [first_sum], [[(0, 0)], [(0, 1)], [(0, 2)], [(0, 3)]], [gate])
        gate = second_sum.back([done1[0]])
        second_sum.give([gate])
        all_a, all_b = finish(
            where, [second_sum, first_sum],
            [[(0, 0), (0, 1), (0, 2), (1, 4)], [(0, 3), (0, 4), (0, 5), (1, 5)]],
        )
        shaped = lambda v: v.reshape(-1, adapters, rank, v.shape[1])
        da, db, ua, ub = (shaped(v)[0] for v in done1)
        return (
            to_positions(layer_out), to_positions(grad_in),
            turned(shaped(all_a)), shaped(all_b), turned(ua), ub, turned(da), db,
        )

    onehot = (pick[:, None] == jnp.arange(adapters)[None, :]).astype(F32)

    def fold(per_sequence):
        total = onehot[0][:, None, None] * per_sequence[0][None].astype(F32)
        for index in range(1, mine):
            total += onehot[index][:, None, None] * per_sequence[index][None].astype(F32)
        return total

    sums = lax.psum(
        tuple(fold(g) for g in [*later[:3], g_out_a, *later[3:], g_out_b, g_up_a, g_up_b, g_down_a, g_down_b]),
        ("dp", "tensor"),
    )
    return (
        to_positions(layer_out),
        to_positions(grad_in),
        turned(jnp.stack(sums[:4])),
        jnp.stack(sums[4:8]),
        turned(sums[8]),
        sums[9],
        turned(sums[10]),
        sums[11],
    )


def solution(mesh):
    placed = (
        P("dp", "tensor", None),
        P("dp", None),
        P("dp"),
        P(None, "dp", "tensor"),
        P("tensor", "dp"),
        P("dp", "tensor"),
        P("tensor", "dp"),
        P(),
        P(),
        P(),
        P(),
        P(),
        P(),
        P(),
        P(),
        P("dp", "tensor", None),
    )
    return jax.shard_map(
        shards,
        mesh=mesh,
        in_specs=placed,
        out_specs=(P("dp", "tensor", None), P("dp", "tensor", None), P(), P(), P(), P(), P(), P()),
        check_vma=False,
    )
```

```python
import functools

import jax
import jax.numpy as jnp
from jax import lax
from jax.experimental import pallas as pl
from jax.experimental.pallas import tpu as pltpu
from jax.sharding import PartitionSpec as P

HEAD_DIM = 64
BF = jnp.bfloat16
F32 = jnp.float32
LOG2E = 1.4426950408889634
VMEM = 60 * 2**20


def nn(a, b):
    return lax.dot_general(a, b, (((1,), (0,)), ((), ())), preferred_element_type=F32)


def nt(a, b):
    return lax.dot_general(a, b, (((1,), (1,)), ((), ())), preferred_element_type=F32)


def tn(a, b):
    return lax.dot_general(a, b, (((0,), (0,)), ((), ())), preferred_element_type=F32)


def params(flops, nbytes, limit=VMEM):
    return dict(
        compiler_params=pltpu.CompilerParams(vmem_limit_bytes=limit),
        cost_estimate=pl.CostEstimate(flops=flops, bytes_accessed=nbytes, transcendentals=0),
    )


class Piece:
    def __init__(self, col, width, rel, row, count, array, at, other):
        self.col, self.width, self.rel, self.row = col, width, rel, row
        self.count, self.array, self.at, self.other = count, array, at, other


def first_tile():
    return jnp.logical_and(pl.program_id(0) == 0, pl.program_id(1) == 0)


class Loader:
    def __init__(self, plan, refs, scratch, sems, me, t, dp):
        self.plan, self.refs, self.scratch, self.sems = plan, refs, scratch, sems
        self.me, self.t, self.dp = me, t, dp
        self.width = scratch.shape[1] // 2
        self.block = scratch.shape[0] // dp

    def start(self):
        def copy(source, block, row, count, into, width, other):
            rows = pl.ds(pl.multiple_of(block * self.block + row, 16), count)
            cols = pl.ds(pl.multiple_of((self.t ^ other) * self.width + into, 128), width)
            pltpu.make_async_copy(source, self.scratch.at[rows, cols], self.sems.at[other]).start()

        for slot, at, count, col, width, other, rel, row, into in self.plan:
            cols = pl.ds(col, width)
            if rel is None:
                for block in range(self.dp):
                    source = self.refs[slot].at[block, self.t ^ other, :, cols]
                    copy(source, block, 0, self.block, into, width, other)
            else:
                copy(self.refs[slot].at[pl.ds(at, count), cols], self.me ^ rel, row, count, into, width, other)

    def wait(self, other):
        cols = pl.ds(pl.multiple_of((self.t ^ other) * self.width, 128), self.width)
        whole = self.scratch.at[:, cols]
        pltpu.make_async_copy(whole, whole, self.sems.at[other]).wait()

    def first_step(self):
        pl.when(first_tile())(self.start)

    def first_wait(self, other):
        pl.when(first_tile())(lambda: self.wait(other))

    def first_wait_all(self):
        self.first_wait(0)
        self.first_wait(1)

    def cols(self, half, lo, width):
        at = half * self.width + lo
        return self.scratch[:, pl.ds(at if isinstance(at, int) else pl.multiple_of(at, 128), width)]


def weight_plan(pieces, first, width):
    arrays, plan = [], []
    for p in pieces:
        lo, hi = max(p.col, first), min(p.col + p.width, first + width)
        if lo >= hi:
            continue
        slot = next((i for i, a in enumerate(arrays) if a is p.array), None)
        if slot is None:
            slot = len(arrays)
            arrays.append(p.array)
        plan.append((slot, p.at, p.count, lo - p.col, hi - lo, p.other, p.rel, p.row, lo - first))
    return arrays, plan


def qkv_kernel(meta, ins, outs, weights, scratch):
    x_ref, a_ref, b_ref = ins
    qkv_ref, rank_ref = outs
    (w,) = weights
    w.first_step()
    w.first_wait_all()
    x = x_ref[0]
    slots, rank_size = rank_ref.shape[1] // a_ref.shape[2], a_ref.shape[2]
    factors = a_ref[0:slots, 0].reshape(slots * rank_size, x.shape[1])
    rank = nt(x, factors).astype(BF)
    rank_ref[0] = nt(factors, x).astype(BF)
    width = w.width // slots
    for half in range(2):
        cols = slice(half * width, (half + 1) * width)
        for slot in range(slots):
            mine = rank[:, slot * rank_size : (slot + 1) * rank_size]
            full = nn(x, w.cols(half, slot * width, width)) + nn(mine, b_ref[slot, 0, :, cols])
            qkv_ref[0, slot, :, cols] = full.astype(BF)


SCALE = HEAD_DIM**-0.5
SCALE2 = SCALE * LOG2E
GROUP = 4 * HEAD_DIM


def one_head(lane, head, value):
    return jnp.where(lane // HEAD_DIM == head, value, jnp.zeros((), value.dtype))


def attend_kernel(q_ref, k_ref, v_ref, segc_ref, segr_ref, out_ref, lse_ref):
    q, k, v = q_ref[0, 0], k_ref[0, 0], v_ref[0, 0]
    length, lanes = q.shape
    heads = lanes // HEAD_DIM
    lane = lax.broadcasted_iota(jnp.int32, (1, lanes), 1)
    same = segc_ref[0] == segr_ref[0]
    v_t = v.T

    def score(head):
        return nt(one_head(lane, head, k), q)

    mixed = []
    scores = score(0)
    for head in range(heads):
        following = score(head + 1) if head + 1 < heads else None
        masked = jnp.where(same, scores, F32(-1000000000.0 / SCALE))
        peak = jnp.max(masked, axis=0, keepdims=True) * SCALE2
        weights = jnp.exp2(masked * SCALE2 - peak)
        mass = jnp.sum(weights, axis=0, keepdims=True)
        rows = slice(head * HEAD_DIM, (head + 1) * HEAD_DIM)
        mixed.append(nn(v_t[rows, :], weights.astype(BF)) * (1.0 / mass))
        lse_ref[0, 0, head : head + 1, :] = peak + jnp.log2(mass)
        scores = following
    out_ref[0] = jnp.concatenate(mixed, axis=0).astype(BF).T
    lse_ref[0, 0, heads:, :] = jnp.zeros((lse_ref.shape[2] - heads, length), F32)


def attend_back_kernel(
    q_ref, k_ref, v_ref, segc_ref, segr_ref, lse_ref, o_ref, do_ref, gq_ref, gk_ref, gv_ref
):
    q, k, v, do = q_ref[0, 0], k_ref[0, 0], v_ref[0, 0], do_ref[0]
    lanes = q.shape[1]
    lane = lax.broadcasted_iota(jnp.int32, (1, lanes), 1)
    product = do.astype(F32) * o_ref[0].astype(F32)
    high = product.astype(BF)
    low = (product - high.astype(F32)).astype(BF)
    picker = (
        lax.broadcasted_iota(jnp.int32, (8, lanes), 0)
        == lax.broadcasted_iota(jnp.int32, (8, lanes), 1) // HEAD_DIM
    ).astype(BF)
    inner = nt(picker, high) + nt(picker, low)
    same = segc_ref[0] == segr_ref[0]
    grad_q = grad_k = grad_v = None
    for head in range(lanes // HEAD_DIM):
        k_mine = one_head(lane, head, k)
        masked = jnp.where(same, nt(k_mine, q), F32(-1000000000.0 / SCALE))
        probs = jnp.exp2(masked * SCALE2 - lse_ref[0, 0, head : head + 1, :])
        grad_probs = nt(one_head(lane, head, v), do)
        grad_scores = (probs * (grad_probs - inner[head : head + 1, :])).astype(BF)
        part_v = nn(probs.astype(BF), one_head(lane, head, do))
        part_k = nn(grad_scores, one_head(lane, head, q))
        part_q = tn(grad_scores, k_mine)
        grad_v = part_v if head == 0 else grad_v + part_v
        grad_k = part_k if head == 0 else grad_k + part_k
        grad_q = part_q if head == 0 else grad_q + part_q
    gq_ref[0] = (grad_q * SCALE).astype(BF)
    gk_ref[0] = (grad_k * SCALE).astype(BF)
    gv_ref[0] = grad_v.astype(BF)


def norm_parts(values):
    mean = jnp.mean(values, axis=-1, keepdims=True)
    centred = values - mean
    inverse = lax.rsqrt(jnp.mean(centred * centred, axis=-1, keepdims=True) + 1e-06)
    return centred * inverse, inverse


def norm_back(scaled, normed, inverse):
    mean_grad = jnp.mean(scaled, axis=-1, keepdims=True)
    mean_proj = jnp.mean(scaled * normed, axis=-1, keepdims=True)
    return (scaled - mean_grad - normed * mean_proj) * inverse


ROWS = 64


def by_rows(count, step):
    for row in range(0, count, ROWS):
        step(slice(row, row + ROWS))


def out_kernel(meta, ins, outs, weights, scratch):
    att_ref, x_ref, a_ref, b_ref, gain_ref, bias_ref = ins
    normed_ref, inverse_ref, low_ref, rank_ref = outs
    (w,) = weights
    (v_scr,) = scratch
    w.first_step()
    w.first_wait_all()
    att = att_ref[0]
    rank = nt(att, a_ref[0, 0]).astype(BF)
    rank_ref[0] = nt(a_ref[0, 0], att).astype(BF)
    width = w.width
    v_scr[...] = (
        nt(att[:, :width], w.cols(0, 0, width))
        + nt(att[:, width:], w.cols(1, 0, width))
        + nn(rank, b_ref[0, 0])
    )

    def step(rows):
        normed, inverse = norm_parts(v_scr[rows, :] + x_ref[0, rows, :].astype(F32))
        normed_ref[0, rows, :] = normed
        inverse_ref[0, rows, :] = jnp.broadcast_to(inverse, (ROWS, 128))
        low_ref[0, rows, :] = (normed * gain_ref[0:1, :] + bias_ref[0:1, :]).astype(BF)

    by_rows(v_scr.shape[0], step)


def gelu_parts(x):
    phi = 0.5 + 0.5 * lax.erf(x * 0.7071067811865476)
    density = jnp.exp2((-0.5 * LOG2E) * x * x)
    return x * phi, phi + x * (density * 0.3989422804014327)


CHUNK = 512


def up_kernel(meta, ins, outs, weights, scratch):
    m_ref, a_ref = ins[:2]
    b_refs = ins[2:]
    act_ref, slope_ref, rank_ref = outs
    (w,) = weights
    w.first_step()
    w.first_wait_all()
    m = m_ref[0]
    rank = nt(m, a_ref[0]).astype(BF)
    rank_ref[0] = nt(a_ref[0], m).astype(BF)
    width = w.width
    for half, b_ref in enumerate(b_refs):
        for lo in range(0, width, CHUNK):
            cols = slice(lo, lo + CHUNK)
            units = nn(m, w.cols(half, lo, CHUNK)) + nn(rank, b_ref[0, :, cols])
            act, slope = gelu_parts(units)
            act_ref[0, half, :, cols] = act.astype(BF)
            slope_ref[0, half, :, cols] = slope.astype(BF)


def add_up(total, part, fresh):
    total[...] = jnp.where(fresh, part, total[...] + part)


def keep_or_send(t, value, kept_ref, sent_ref):
    @pl.when(pl.program_id(1) == t)
    def _():
        kept_ref[0] = value

    @pl.when(pl.program_id(1) != t)
    def _():
        sent_ref[0] = value


def middle_kernel(meta, ins, outs, weights, scratch):
    (act_ref, slope_ref, n1_ref, r1_ref, go_ref, m_ref, att_ref, ranku_ref, ranko_ref,
     da_ref, db_ref, ua_ref, ub_ref, oa_ref, ob_ref, gain_ref, bias_ref) = ins
    kept_ref, sent_ref, first_ref, gatt_ref = outs[:4]
    down, up, out = weights
    v_scr, second_scr, gf_scr, gh_scr, out_scr = scratch[:5]
    sums = scratch[5:]
    sum_da, sum_db, sum_ua, sum_ub, sum_oa, sum_ob = sums
    tile = pl.program_id(1)
    fresh = tile == 0
    for loader in (down, up, out):
        loader.first_step()
    for loader in (down, up, out):
        loader.first_wait_all()
    width = down.width
    halves = [slice(0, width), slice(width, 2 * width)]

    rank = sum(nt(act_ref[0, h], da_ref[0, :, halves[h]]) for h in range(2)).astype(BF)
    model = v_scr.shape[1]
    for at in range(0, model, CHUNK):
        cols = slice(at, at + CHUNK)
        v_scr[:, cols] = (
            nt(act_ref[0, 0], down.scratch[cols, halves[0]])
            + nt(act_ref[0, 1], down.scratch[cols, halves[1]])
            + nn(rank, db_ref[0, :, cols])
        )

    def second_norm(rows):
        middle = n1_ref[0, rows, :] * gain_ref[0:1, :] + bias_ref[0:1, :]
        normed, inverse = norm_parts(v_scr[rows, :] + middle)
        out_scr[rows, :] = (normed * gain_ref[1:2, :] + bias_ref[1:2, :]).astype(BF)
        second = norm_back(go_ref[0, rows, :].astype(F32) * gain_ref[1:2, :], normed, inverse)
        second_scr[rows, :] = second
        gf_scr[rows, :] = second.astype(BF)

    by_rows(v_scr.shape[0], second_norm)
    grad_feed = gf_scr[...]
    add_up(sum_db, tn(rank, grad_feed), fresh)
    grad_rank = nt(grad_feed, db_ref[0]).astype(BF)
    chunk = 2 * CHUNK
    for half in range(2):
        for lo in range(0, width, chunk):
            cols = slice(half * width + lo, half * width + lo + chunk)
            grad_act = nn(grad_feed, down.cols(half, lo, chunk)) + nn(grad_rank, da_ref[0, :, cols])
            local = slice(lo, lo + chunk)
            gh_scr[:, cols] = (grad_act * slope_ref[0, half, :, local].astype(F32)).astype(BF)
    grad_rank_down = grad_rank

    grad_rank = nt(gh_scr[...], ub_ref[0]).astype(BF)
    for at in range(0, model, CHUNK):
        cols = slice(at, at + CHUNK)
        v_scr[:, cols] = (
            nt(gh_scr[:, halves[0]], up.scratch[cols, halves[0]])
            + nt(gh_scr[:, halves[1]], up.scratch[cols, halves[1]])
            + nn(grad_rank, ua_ref[0, :, cols])
        )
    add_up(sum_ua, tn(grad_rank, m_ref[0]), fresh)
    add_up(sum_ub, nn(ranku_ref[0], gh_scr[...]), fresh)
    for half in range(2):
        add_up(sum_da.at[:, halves[half]], tn(grad_rank_down, act_ref[0, half]), fresh)

    def first_norm(rows):
        scaled = (second_scr[rows, :] + v_scr[rows, :]) * gain_ref[0:1, :]
        first = norm_back(scaled, n1_ref[0, rows, :], r1_ref[0, rows, 0:1])
        first_ref[0, rows, :] = first
        gf_scr[rows, :] = first.astype(BF)

    by_rows(v_scr.shape[0], first_norm)
    grad_branch = gf_scr[...]
    grad_rank = nt(grad_branch, ob_ref[0, 0]).astype(BF)
    add_up(sum_oa, tn(grad_rank, att_ref[0]), fresh)
    add_up(sum_ob, nn(ranko_ref[0], grad_branch), fresh)
    owidth = out.width
    for half in range(2):
        cols = slice(half * owidth, (half + 1) * owidth)
        full = nn(grad_branch, out.cols(half, 0, owidth)) + nn(grad_rank, oa_ref[0, 0, :, cols])
        gatt_ref[0, :, cols] = full.astype(BF)

    keep_or_send(down.t, out_scr[...], kept_ref, sent_ref)

    @pl.when(tile == pl.num_programs(1) - 1)
    def _():
        for total, ref in zip(sums, outs[4:]):
            ref[0] = total[...].astype(BF)


def rank_back_kernel(meta, ins, outs, weights, scratch):
    gq_ref, gk_ref, gv_ref, x_ref, rank_ref, b_ref = ins
    gr_ref, a_refs, b_refs = outs[0], outs[1:4], outs[4:]
    size = b_ref.shape[2]
    ranks = []
    for slot, ref in enumerate((gq_ref, gk_ref, gv_ref)):
        grad = ref[0]
        ranks.append(nt(b_ref[slot, 0], grad))
        b_refs[slot][0] = nn(rank_ref[0, slot * size : (slot + 1) * size, :], grad).astype(BF)
    stacked = jnp.concatenate(ranks, axis=0).astype(BF)
    gr_ref[0] = stacked
    products = nn(stacked, x_ref[0]).astype(BF)
    for slot, ref in enumerate(a_refs):
        ref[0] = products[slot * size : (slot + 1) * size]


def qkv_back_kernel(meta, ins, outs, weights, scratch):
    gq_ref, gk_ref, gv_ref, gr_ref, first_ref, a_ref = ins
    kept_ref, sent_ref = outs
    (w,) = weights
    w.first_step()
    w.first_wait_all()
    slots = 3
    width = w.width // slots
    size = a_ref.shape[2]
    total = first_ref[0] + tn(
        gr_ref[0], a_ref[0:slots, 0].reshape(slots * size, kept_ref.shape[2])
    )
    for half in range(2):
        cols = slice(half * width, (half + 1) * width)
        for slot, ref in enumerate((gq_ref, gk_ref, gv_ref)):
            total += nt(ref[0, :, cols], w.cols(half, slot * width, width))
    keep_or_send(w.t, total, kept_ref, sent_ref)


NEAR = []


def made_near(arrays):
    NEAR.extend(arrays)
    return arrays


def waits(arrays):
    arrays = [a for a in arrays if a is not None]
    near = [any(a is n for n in NEAR) for a in arrays]
    specs = [pl.BlockSpec(memory_space=pl.ANY if n else pltpu.HBM) for n in near]
    return specs, [a if n else in_hbm(a) for a, n in zip(arrays, near)]


def call(kernel, meta, ins, outs, flops, scratch=(), weights=(), limit=VMEM, after=(), tiles=1, filled=()):
    plans = [weight_plan(pieces, first, width) for pieces, first, width, _, _ in weights]
    n_in, n_out, n_w = len(ins), len(outs), len(weights)
    counts = [len(arrays) for arrays, _ in plans]
    steps = meta.shape[0] - 2
    after_specs, after = waits(after)
    n_after = len(after)

    def body(meta_ref, *refs):
        refs = list(refs)
        take = lambda n: [refs.pop(0) for _ in range(n)]
        in_refs = take(n_in)
        w_refs = [take(n) for n in counts]
        take(n_after + len(filled))
        out_refs = take(n_out)
        w_scr = take(n_w)
        w_sem = take(n_w)
        me, t = meta_ref[steps], meta_ref[steps + 1]
        loaders = [
            Loader(plan, r, s, m, me, t, w[3])
            for (_, plan), r, s, m, w in zip(plans, w_refs, w_scr, w_sem, weights)
        ]
        kernel(meta_ref, in_refs, out_refs, loaders, refs)

    w_arrays = [a for arrays, _ in plans for a in arrays]
    nbytes = sum(a.size * a.dtype.itemsize for a, _, _ in ins)
    nbytes += sum(2 * dp * rows * width * 2 for _, _, width, dp, rows in weights)
    for shape, dtype, _, _ in outs:
        size = jnp.dtype(dtype).itemsize
        for extent in shape:
            size *= extent
        nbytes += size
    return pl.pallas_call(
        body,
        grid_spec=pltpu.PrefetchScalarGridSpec(
            num_scalar_prefetch=1,
            grid=(steps, tiles),
            in_specs=[pl.BlockSpec(block, index) for _, block, index in ins]
            + [pl.BlockSpec(memory_space=pltpu.HBM) for _ in w_arrays]
            + after_specs
            + [pl.BlockSpec(memory_space=pltpu.HBM) for _ in filled],
            out_specs=[pl.BlockSpec(block, index) for _, _, block, index in outs],
            scratch_shapes=[pltpu.VMEM((dp * rows, 2 * width), BF) for _, _, width, dp, rows in weights]
            + [pltpu.SemaphoreType.DMA((2,)) for _ in weights]
            + list(scratch),
        ),
        out_shape=[pltpu.HBM(shape, dtype) for shape, dtype, _, _ in outs],
        input_output_aliases={1 + n_in + len(w_arrays) + n_after + i: i for i in range(len(filled))},
        **params(flops, nbytes, limit),
    )(meta, *[in_hbm(a) for a in [*[a for a, _, _ in ins], *w_arrays]], *after, *[in_hbm(a) for a in filled])


def pack(outs, fresh=(), after=()):
    after_specs, after = waits(after)
    arrays, plan, heights, widths = [], [], [], []

    def slot(array):
        for index, known in enumerate(arrays):
            if known is array:
                return index
        arrays.append(array)
        return len(arrays) - 1

    for index, parts in enumerate(outs):
        row = 0
        for part in parts:
            array, at, count, col, cols, into, advance = part
            plan.append((slot(array), at, count, col, cols, index, row, into))
            if advance:
                row += count
        heights.append(row)
        widths.append(max(part[4] + part[5] for part in parts))
    used, n_in = len(arrays), len(arrays) + len(after)
    near = [any(a is f for f in fresh) for a in arrays]

    def kernel(*refs):
        ins, results, sems = refs[:n_in], refs[n_in:-1], refs[-1]
        copies = []
        for number, (a, at, count, col, cols, o, row, into) in enumerate(plan):
            source = ins[a].at[pl.ds(at, count), pl.ds(col, cols)]
            target = results[o].at[pl.ds(row, count), pl.ds(into, cols)]
            if not near[a]:
                copy = pltpu.make_async_copy(source, target, sems.at[number])
                copy.start()
                copies.append(copy)
        for a, at, count, col, cols, o, row, into in plan:
            if near[a]:
                results[o][pl.ds(row, count), pl.ds(into, cols)] = ins[a][pl.ds(at, count), pl.ds(col, cols)]
        for copy in copies:
            copy.wait()

    spaces = [pltpu.VMEM if n else pltpu.HBM for n in near]
    return made_near(pl.pallas_call(
        kernel,
        in_specs=[pl.BlockSpec(memory_space=space) for space in spaces] + after_specs,
        out_specs=[pl.BlockSpec(memory_space=pltpu.VMEM)] * len(outs),
        out_shape=[pltpu.VMEM(shape, BF) for shape in zip(heights, widths)],
        scratch_shapes=[pltpu.SemaphoreType.DMA((len(plan),))],
        compiler_params=pltpu.CompilerParams(vmem_limit_bytes=8 * 2**20),
        cost_estimate=pl.CostEstimate(
            flops=0, bytes_accessed=sum(h * w * 4 for h, w in zip(heights, widths)), transcendentals=0
        ),
    )(*[pltpu.with_memory_space_constraint(a, space) for a, space in zip(arrays, spaces)], *after))


def in_hbm(array):
    return pltpu.with_memory_space_constraint(array, pltpu.HBM)


X, Y, Z1, Z2, Z3 = 1, 2, 4, 8, 12
ZS = (Z1, Z2, Z3)


def hop(array, bits):
    return lax.ppermute(array, "dp", [(i, i ^ bits) for i in range(lax.axis_size("dp"))])


def swap(array):
    return lax.ppermute(array, "tensor", [(0, 1), (1, 0)])


class Gather:
    def __init__(self, w_qkv, w_out, w_up, w_down):
        self.n = n = w_up.shape[0]
        self.h = n // 2
        self.pieces = []
        o, u = w_qkv.shape[2], w_up.shape[1]
        self.width = 3 * o
        flat = w_qkv.reshape(3 * n, o)
        wo, wd = w_out.T, w_down.T
        queries = [(flat, slot * n, n, 0, o, slot * o, slot == 2) for slot in range(3)]
        rest = [
            (wo, 0, n, 0, o, 0, False), (w_up, 0, n, 0, 2 * o, o, True),
            (w_up, 0, n, 2 * o, u - 2 * o, 0, False), (wd, 0, n, 0, o, 2 * o, True),
            (wd, 0, n, o, 3 * o, 0, True),
        ]
        self.own, self.q = pack([queries + rest, queries])
        self.e, self.f, self.g = (self.cut(p) for p in (1, 2, 3))

    def cut(self, piece):
        return lax.slice_in_dim(self.own, piece * self.n, (piece + 1) * self.n, axis=0)

    def note(self, array, items, other=0):
        at = 0
        for piece, rel, row, count in items:
            self.pieces.append(Piece(piece * self.width, self.width, rel, row, count, array, at, other))
            at += count

    def part(self, array, at, count):
        return (array, at, count, 0, self.width, 0, True)

    def full(self, piece, *rels):
        return [(piece, rel, 0, self.n) for rel in rels]

    def upper(self, piece, *rels):
        return [(piece, rel, self.h, self.h) for rel in rels]

    def lower(self, piece, *rels):
        return [(piece, rel, 0, self.h) for rel in rels]

    def exchange(self, arrays, after=()):
        fresh = [a for a, _ in arrays if a is not self.own]
        (packed,) = pack([[self.part(a, 0, a.shape[0]) for a, _ in arrays]], fresh=fresh, after=after)
        other = swap(packed)
        self.note(other, [item for _, items in arrays for item in items], 1)
        return packed, other

    def keep(self, got):
        for array, items in got:
            self.note(array, items)
        return got

    def round1(self):
        self.zq = [hop(self.q, k) for k in ZS]
        self.x1, self.y1 = hop(self.own, X), hop(self.own, Y)
        every = range(4)
        got = [(self.own, [i for p in every for i in self.full(p, 0)])]
        got += [(self.x1, [i for p in every for i in self.full(p, X)])]
        got += [(self.y1, [i for p in every for i in self.full(p, Y)])]
        got += [(z, self.full(0, k)) for z, k in zip(self.zq, ZS)]
        self.got1 = self.keep(got)

    def round2(self, after):
        n, h, part = self.n, self.h, self.part
        along = [part(z, 0, n) for z in self.zq]
        xin, yin, e = pack(
            [along + [part(self.y1, h, h)], along + [part(self.x1, 0, h)], [part(self.own, n, n)]],
            fresh=[*self.zq, self.x1, self.y1],
            after=after,
        )
        x, y, self.ze2 = hop(xin, X), hop(yin, Y), hop(e, Z2)
        self.x, self.y = x, y
        self.got2 = self.keep([
            (x, self.full(0, *(X | k for k in ZS)) + self.upper(0, X | Y)),
            (y, self.full(0, *(Y | k for k in ZS)) + self.lower(0, X | Y)),
            (self.ze2, self.full(1, Z2)),
        ])
        return self.exchange(self.got1, [xin])

    def round3(self, after):
        n, h, part = self.n, self.h, self.part
        xin, yin, e, f = pack(
            [
                [part(self.y, i * n + h, h) for i in range(3)] + [part(self.y1, p * n + h, h) for p in (1, 2)],
                [part(self.x, i * n, h) for i in range(3)] + [part(self.x1, p * n, h) for p in (1, 2)],
                [part(self.own, n, n), part(self.ze2, 0, n)],
                [part(self.own, 2 * n, n)],
            ],
            fresh=[self.x, self.y, self.ze2],
            after=after,
        )
        x, y, self.ze1, self.zf2 = hop(xin, X), hop(yin, Y), hop(e, Z1), hop(f, Z2)
        self.x, self.y = x, y
        both = [X | Y | k for k in ZS]
        self.got3 = self.keep([
            (x, self.upper(0, *both) + self.upper(1, X | Y) + self.upper(2, X | Y)),
            (y, self.lower(0, *both) + self.lower(1, X | Y) + self.lower(2, X | Y)),
        ])
        self.late3 = self.keep([(self.ze1, self.full(1, Z1, Z3)), (self.zf2, self.full(2, Z2))])
        return self.exchange(self.got2, [xin])

    def round4(self, after):
        n, h, part = self.n, self.h, self.part
        along = [part(self.ze1, 0, n), part(self.ze2, 0, n), part(self.ze1, n, n)]
        xin, yin, f, g = pack(
            [
                along + [part(self.y1, 3 * n + h, h)],
                along + [part(self.x1, 3 * n, h)],
                [part(self.own, 2 * n, n), part(self.zf2, 0, n)],
                [part(self.own, 3 * n, n)],
            ],
            fresh=[self.ze1, self.zf2],
            after=after,
        )
        x, y, self.zf1, self.zg2 = hop(xin, X), hop(yin, Y), hop(f, Z1), hop(g, Z2)
        self.x, self.y = x, y
        self.got4 = self.keep([
            (x, self.full(1, *(X | k for k in ZS)) + self.upper(3, X | Y)),
            (y, self.full(1, *(Y | k for k in ZS)) + self.lower(3, X | Y)),
            (self.zf1, self.full(2, Z1, Z3)),
            (self.zg2, self.full(3, Z2)),
        ])
        return self.exchange(self.got3, [xin])

    def round5(self, after):
        n, h, part = self.n, self.h, self.part
        along = [part(self.zf1, 0, n), part(self.zf2, 0, n), part(self.zf1, n, n)]
        xin, yin, g, d = pack(
            [
                [part(self.y, i * n + h, h) for i in range(3)] + along,
                [part(self.x, i * n, h) for i in range(3)] + along,
                [part(self.own, 3 * n, n), part(self.zg2, 0, n)],
                [part(self.y, 3 * n, h), part(self.x, 3 * n, h)],
            ],
            fresh=[self.x, self.y, self.zf1, self.zg2],
            after=after,
        )
        self.d = d
        x, y, self.zg1, self.zd2 = hop(xin, X), hop(yin, Y), hop(g, Z1), hop(d, Z2)
        self.x, self.y = x, y
        both = [X | Y | k for k in ZS]
        self.got5 = self.keep([
            (x, self.upper(1, *both) + self.full(2, *(X | k for k in ZS))),
            (y, self.lower(1, *both) + self.full(2, *(Y | k for k in ZS))),
            (self.zg1, self.full(3, Z1, Z3)),
            (self.zd2, self.full(3, X | Y | Z2)),
        ])
        return self.exchange(self.late3 + self.got4, [xin])

    def round6(self, after):
        n, h, part = self.n, self.h, self.part
        along = [part(self.zg1, 0, n), part(self.zg2, 0, n), part(self.zg1, n, n)]
        xin, yin, d = pack(
            [
                [part(self.y, 3 * h + i * n + h, h) for i in range(3)] + along,
                [part(self.x, 3 * h + i * n, h) for i in range(3)] + along,
                [part(self.d, 0, n), part(self.zd2, 0, n)],
            ],
            fresh=[self.x, self.y, self.zg1, self.zd2],
            after=after,
        )
        x, y, zd1 = hop(xin, X), hop(yin, Y), hop(d, Z1)
        both = [X | Y | k for k in ZS]
        self.got6 = self.keep([
            (x, self.upper(2, *both) + self.full(3, *(X | k for k in ZS))),
            (y, self.lower(2, *both) + self.full(3, *(Y | k for k in ZS))),
            (zd1, self.full(3, X | Y | Z1, X | Y | Z3)),
        ])
        return self.exchange(self.got5, [xin])

    def last(self, after):
        return self.exchange(self.got6, after)


class GatherPlain:
    def __init__(self, w_qkv, w_out, w_up, w_down):
        local = jnp.concatenate([w_qkv[0], w_qkv[1], w_qkv[2], w_out.T, w_up, w_down.T], axis=1)
        rows, width = local.shape
        whole = lax.all_gather(local, ("dp", "tensor")).reshape(lax.axis_size("dp"), 2, rows, width)
        self.pieces = [Piece(0, width, None, 0, 0, whole, 0, other) for other in range(2)]

    def round1(self):
        return None

    def round2(self, after):
        return None, None

    round3 = round4 = round5 = round6 = last = round2


class Spot:
    def __init__(self, array, row, rows, col, cols):
        self.array, self.row, self.rows, self.col, self.cols = array, row, rows, col, cols

    def of(self, ref, me, t):
        at = lambda v, unit: pl.multiple_of(v(me, t), unit) if callable(v) else v
        return ref.at[pl.ds(at(self.row, 16), self.rows), pl.ds(at(self.col, 128), self.cols)]


def arrange(where, shapes, moves, fresh=(), after=()):
    after_specs, after = waits(after)
    arrays = []
    for source, _, _ in moves:
        if not any(a is source.array for a in arrays):
            arrays.append(source.array)
    near = [any(a is f for f in fresh) for a in arrays]
    number = lambda array: next(i for i, a in enumerate(arrays) if a is array)
    plan = [(number(source.array), source, out, target) for source, out, target in moves]

    def kernel(where_ref, *refs):
        ins, results, sems = refs[: len(arrays)], refs[len(arrays) + len(after) : -1], refs[-1]
        me, t = where_ref[0], where_ref[1]
        copies = []
        for index, (slot, source, out, target) in enumerate(plan):
            copy = pltpu.make_async_copy(
                source.of(ins[slot], me, t), target.of(results[out], me, t), sems.at[index]
            )
            copy.start()
            copies.append(copy)
        for copy in copies:
            copy.wait()

    spaces = [pltpu.VMEM if n else pltpu.HBM for n in near]
    return made_near(pl.pallas_call(
        kernel,
        in_specs=[pl.BlockSpec(memory_space=pltpu.SMEM)]
        + [pl.BlockSpec(memory_space=m) for m in spaces]
        + after_specs,
        out_specs=[pl.BlockSpec(memory_space=pltpu.VMEM)] * len(shapes),
        out_shape=[pltpu.VMEM(shape, BF) for shape in shapes],
        scratch_shapes=[pltpu.SemaphoreType.DMA((len(plan),))],
        compiler_params=pltpu.CompilerParams(vmem_limit_bytes=8 * 2**20),
        cost_estimate=pl.CostEstimate(
            flops=0, bytes_accessed=sum(h * w * 4 for h, w in shapes), transcendentals=0
        ),
    )(where, *[pltpu.with_memory_space_constraint(a, m) for a, m in zip(arrays, spaces)], *after))


class GradientSum:
    def __init__(self, where, arrays, mine, rank, adapters, picks):
        self.where, self.arrays, self.picks = where, arrays, picks
        self.mine, self.rank, self.adapters = mine, rank, adapters
        self.rows = mine * rank
        self.widths = [a.shape[1] for a in arrays]
        self.starts = [sum(self.widths[:i]) for i in range(len(arrays))]
        self.total = sum(self.widths)
        self.chunk = self.total // 8

    def cores(self, after=()):
        half = self.total // 2
        moves = [
            (
                Spot(a, 0, self.rows, lambda me, t, w=w: (1 - t) * (w // 2), w // 2),
                0,
                Spot(None, 0, self.rows, s // 2, w // 2),
            )
            for a, w, s in zip(self.arrays, self.widths, self.starts)
        ]
        (out,) = arrange(self.where, [(self.rows, half)], moves, after=after)
        self.other = swap(out)
        return out

    def plane(self, after=()):
        moves = []
        for k in range(4):
            for a, w, s in zip(self.arrays, self.widths, self.starts):
                e = w // 8
                moves.append((
                    Spot(a, 0, self.rows, lambda me, t, e=e, k=k: (t * 4 + ((me & 3) ^ k)) * e, e),
                    k,
                    Spot(None, 0, self.rows, s // 8, e),
                ))
                moves.append((
                    Spot(self.other, 0, self.rows, lambda me, t, e=e, s=s, k=k: s // 2 + ((me & 3) ^ k) * e, e),
                    k,
                    Spot(None, self.rows, self.rows, s // 8, e),
                ))
            moves.append((
                Spot(self.picks, 0, self.rank, 0, self.chunk), k, Spot(None, 2 * self.rows, self.rank, 0, self.chunk)
            ))
        shape = (2 * self.rows + self.rank, self.chunk)
        outs = arrange(self.where, [shape] * 4, moves, fresh=[self.other], after=after)
        self.parts = [outs[0], hop(outs[1], X), hop(outs[2], Y), hop(outs[3], X | Y)]
        return outs[0]

    def fold(self, after=()):
        rank, chunk, data = self.rank, self.chunk, 2 * self.rows
        tall = self.adapters * rank
        quarter = tall // 4

        def kernel(where_ref, *refs):
            ins, outs, total = refs[:4], refs[-5:-1], refs[-1]
            z = where_ref[0] // 4
            row = lax.broadcasted_iota(jnp.int32, (tall, data), 0)
            col = lax.broadcasted_iota(jnp.int32, (tall, data), 1)
            adapter = (row // rank).astype(F32)
            same_row = row % rank == col % rank
            for k in range(4):
                picks = ins[k][data : data + 1, 0:data].astype(F32)
                chosen = jnp.logical_and(adapter == picks, same_row).astype(F32).astype(BF)
                part = nn(chosen, ins[k][0:data, :])
                total[...] = part if k == 0 else total[...] + part
            for k in range(4):
                rows = pl.ds(pl.multiple_of((z ^ k) * quarter, quarter), quarter)
                outs[k][...] = total[rows, :].astype(BF)

        outs = self.local(kernel, self.parts, after, [(quarter, chunk)] * 4, [(tall, chunk)])
        self.parts = [outs[0]] + [hop(outs[k], 4 * k) for k in (1, 2, 3)]
        return outs[0]

    def local(self, kernel, arrays, after, shapes, scratch):
        after_specs, after = waits(after)
        vmem = pl.BlockSpec(memory_space=pltpu.VMEM)
        return made_near(pl.pallas_call(
            kernel,
            in_specs=[pl.BlockSpec(memory_space=pltpu.SMEM)] + [vmem] * len(arrays) + after_specs,
            out_specs=[vmem] * len(shapes),
            out_shape=[pltpu.VMEM(shape, BF) for shape in shapes],
            scratch_shapes=[pltpu.VMEM(shape, F32) for shape in scratch],
            compiler_params=pltpu.CompilerParams(vmem_limit_bytes=12 * 2**20),
            cost_estimate=pl.CostEstimate(
                flops=0, bytes_accessed=sum(h * w * 8 for h, w in shapes), transcendentals=0
            ),
        )(
            self.where,
            *[pltpu.with_memory_space_constraint(a, pltpu.VMEM) for a in arrays],
            *after,
        ))

    def depth(self, after=()):
        def kernel(where_ref, *refs):
            total = refs[0][...].astype(F32)
            for ref in refs[1:4]:
                total += ref[...].astype(F32)
            refs[-1][...] = total.astype(BF)

        (out,) = self.local(kernel, self.parts, after, [self.parts[0].shape], [])
        self.parts = [out] + [hop(out, 4 * k) for k in (1, 2, 3)]
        return out

    def back(self, after=()):
        tall = self.adapters * self.rank
        quarter, side = tall // 4, self.chunk // 2
        moves = [
            (
                Spot(self.parts[k], 0, quarter, part * side, side),
                part,
                Spot(None, lambda me, t, k=k: ((me >> 2) ^ k) * quarter, quarter, 0, side),
            )
            for k in range(4)
            for part in range(2)
        ]
        self.a, self.b = arrange(self.where, [(tall, side)] * 2, moves, fresh=self.parts, after=after)
        self.xa, self.yb = hop(self.a, X), hop(self.b, Y)
        return self.a

    def spread(self, after=()):
        tall, side = self.adapters * self.rank, self.chunk // 2
        moves = [
            (Spot(source, 0, tall, 0, side), out, Spot(None, row * tall, tall, 0, side))
            for out, pair in enumerate(((self.a, self.xa), (self.b, self.yb)))
            for row, source in enumerate(pair)
        ]
        fresh = [self.a, self.b, self.xa, self.yb]
        up, down = arrange(self.where, [(2 * tall, side)] * 2, moves, fresh=fresh, after=after)
        self.ya, self.xb = hop(up, Y), hop(down, X)
        return up

    def give(self, after=()):
        tall, side = self.adapters * self.rank, self.chunk // 2
        sources = [
            ((self.a, 0), (self.b, 0)),
            ((self.xa, 0), (self.xb, 0)),
            ((self.ya, 0), (self.yb, 0)),
            ((self.ya, tall), (self.xb, tall)),
        ]
        moves = [
            (Spot(source, row, tall, 0, side), 0, Spot(None, k * tall, tall, part * side, side))
            for k, both in enumerate(sources)
            for part, (source, row) in enumerate(both)
        ]
        fresh = [self.a, self.b, self.xa, self.yb, self.ya, self.xb]
        (out,) = arrange(self.where, [(4 * tall, self.chunk)], moves, fresh=fresh, after=after)
        self.theirs = swap(out)
        self.ours = out
        return out


def finish(where, sums, results, after=()):
    tall = sums[0].adapters * sums[0].rank
    after_specs, after = waits(after)
    inputs = [a for s in sums for a in (s.ours, s.theirs)]

    def kernel(where_ref, *refs):
        outs = refs[len(inputs) + len(after) :]
        me, t = where_ref[0], where_ref[1]
        for out, parts in zip(outs, results):
            for place, (number, which) in enumerate(parts):
                total = sums[number]
                start, width = total.starts[which] // 8, total.widths[which] // 8
                for core in range(2):
                    for k in range(4):
                        column = ((t ^ core) * 4 + ((me & 3) ^ k)) * width
                        out[place * tall : (place + 1) * tall, pl.ds(pl.multiple_of(column, 128), width)] = refs[
                            2 * number + core
                        ][k * tall : (k + 1) * tall, start : start + width].astype(F32)

    vmem = pl.BlockSpec(memory_space=pltpu.VMEM)
    shapes = [(len(parts) * tall, sums[parts[0][0]].widths[parts[0][1]]) for parts in results]
    return pl.pallas_call(
        kernel,
        in_specs=[pl.BlockSpec(memory_space=pltpu.SMEM)]
        + [vmem] * len(inputs)
        + after_specs,
        out_specs=[vmem] * len(results),
        out_shape=[pltpu.HBM(shape, F32) for shape in shapes],
        compiler_params=pltpu.CompilerParams(vmem_limit_bytes=32 * 2**20),
        cost_estimate=pl.CostEstimate(
            flops=0, bytes_accessed=sum(h * w * 6 for h, w in shapes), transcendentals=0
        ),
    )(where, *inputs, *after)


def hold(array, after):
    after_specs, after = waits(after)
    return pl.pallas_call(
        lambda *refs: None,
        in_specs=after_specs + [pl.BlockSpec(memory_space=pltpu.HBM)],
        out_specs=pl.BlockSpec(memory_space=pltpu.HBM),
        out_shape=pltpu.HBM(array.shape, array.dtype),
        input_output_aliases={len(after): 0},
        cost_estimate=pl.CostEstimate(flops=0, bytes_accessed=0, transcendentals=0),
    )(*after, in_hbm(array))


def place(where, filled, arrived, after=()):
    after_specs, after = waits(after)
    mine, rows, width = arrived.shape

    def kernel(where_ref, arrived_ref, *refs):
        refs[-1][...] = arrived_ref[...]

    return pl.pallas_call(
        kernel,
        grid_spec=pltpu.PrefetchScalarGridSpec(
            num_scalar_prefetch=1,
            grid=(mine,),
            in_specs=[pl.BlockSpec((1, rows, width), lambda s, w: (s, 0, 0))]
            + after_specs
            + [pl.BlockSpec(memory_space=pltpu.HBM)],
            out_specs=pl.BlockSpec((1, rows, width), lambda s, w: ((1 - w[1]) * mine + s, 0, 0)),
        ),
        out_shape=pltpu.HBM(filled.shape, filled.dtype),
        input_output_aliases={2 + len(after): 0},
        **params(1, 2 * arrived.size * arrived.dtype.itemsize, 16 * 2**20),
    )(where, in_hbm(arrived), *after, in_hbm(filled))


def shards(
    hidden_in, segment_ids, adapter_pick, w_qkv, w_out, w_up, w_down, ln_gain, ln_bias,
    adapt_a, adapt_b, up_a, up_b, down_a, down_b, grad_out,
):
    dp = lax.axis_size("dp")
    t = lax.axis_index("tensor")
    block, ff_half = w_up.shape
    width = hidden_in.shape[2]
    half = width // 2
    ff = 2 * ff_half
    positions = hidden_in.shape[1]
    length = 2 * positions
    mine = hidden_in.shape[0] // 2
    rank = adapt_b.shape[2]
    adapters = adapt_b.shape[1]

    NEAR.clear()
    pick = lax.dynamic_slice_in_dim(adapter_pick, mine * t, mine, 0)
    where = jnp.stack([lax.axis_index("dp"), t]).astype(pick.dtype)
    meta = jnp.concatenate([pick, where])
    ordered = jnp.where(t == 0, adapter_pick, jnp.roll(adapter_pick, -mine))
    picks = jnp.repeat(ordered, rank).astype(BF)
    picks = jnp.broadcast_to(jnp.pad(picks, (0, 3 * half - picks.shape[0]))[None], (rank, 3 * half))
    segs = lax.dynamic_slice_in_dim(segment_ids, mine * t, mine, 0)
    seg_col = segs.reshape(mine, length, 1)
    seg_row = segs.reshape(mine, 1, length)

    sent_rows = mine * positions

    def send_half(value, after):
        flat = value.reshape(2 * sent_rows, width)
        spot = Spot(flat, lambda me, t: (1 - t) * sent_rows, sent_rows, 0, width)
        (out,) = arrange(where, [(sent_rows, width)], [(spot, 0, Spot(None, 0, sent_rows, 0, width))], after=after)
        return flat, out, swap(out)

    def join(flat, there, after):
        moves = []
        for s in range(mine):
            moves.append((
                Spot(flat, lambda me, t, s=s: (t * mine + s) * positions, positions, 0, width), 0,
                Spot(None, lambda me, t, s=s: s * length + t * positions, positions, 0, width),
            ))
            moves.append((
                Spot(there, s * positions, positions, 0, width), 0,
                Spot(None, lambda me, t, s=s: s * length + (1 - t) * positions, positions, 0, width),
            ))
        (out,) = arrange(where, [(mine * length, width)], moves, fresh=[there], after=after)
        return out.reshape(mine, length, width), out

    gather = (Gather if dp == 16 else GatherPlain)(w_qkv, w_out, w_up, w_down)
    gather.round1()
    def columns(first, count):
        return (gather.pieces, first, count, dp, block)

    qkv_w = columns(0, 3 * half)
    out_w = columns(3 * half, half)
    part = 2 * half
    up_parts = [columns(4 * half + p, part) for p in range(0, ff_half, part)]
    up_w = columns(4 * half, ff_half)
    down_w = columns(4 * half + ff_half, ff_half)

    a_t = jnp.swapaxes(adapt_a, 2, 3)
    ua_t = jnp.swapaxes(up_a, 1, 2)
    da_t = jnp.swapaxes(down_a, 1, 2)

    gate, met = gather.round2([meta, seg_col, seg_row, picks])
    flat_x, gate, there = send_half(hidden_in, [gate])
    x, gate = join(flat_x, there, [])
    _, met = gather.round3([met, gate])
    gate, _ = gather.round4([met])
    tokens = mine * length
    tiles = 2
    tile = length // tiles
    seq3 = lambda s, i, m: (s, 0, 0)
    row3 = lambda s, i, m: (s, i, 0)
    fixed2 = lambda s, i, m: (0, 0)
    picked3 = lambda s, i, m: (m[s], 0, 0)
    slots4 = lambda s, i, m: (0, m[s], 0, 0)
    last4 = lambda s, i, m: (3, m[s], 0, 0)
    full = lambda a: (a, (1, *a.shape[1:]), seq3)
    row = lambda a: (a, (1, tile, a.shape[2]), row3)
    across = lambda a: (a, (1, a.shape[1], tile), lambda s, i, m: (s, 0, i))
    whole = lambda a: (a, a.shape, fixed2)
    factor = lambda a: (a, (1, *a.shape[1:]), picked3)
    slots = lambda a: (a, (a.shape[0], 1, *a.shape[2:]), slots4)
    last = lambda a: (a, (1, 1, *a.shape[2:]), last4)
    rows_made = lambda dtype, cols: ((mine, length, cols), dtype, (1, tile, cols), row3)
    across_made = lambda rows: ((mine, rows, length), BF, (1, rows, tile), lambda s, i, m: (s, 0, i))
    def kept_made(dtype):
        block = (1, positions, width)
        return [
            ((2 * mine, positions, width), dtype, block, lambda s, i, m: (m[mine + 1] * mine + s, 0, 0)),
            ((mine, positions, width), dtype, block, seq3),
        ]

    sum_made = lambda rows, cols: ((mine, rows, cols), BF, (1, rows, cols), seq3)

    qkv, rank_qkv = call(
        qkv_kernel, meta,
        [row(x), slots(a_t), slots(adapt_b)],
        [((mine, 3, length, width), BF, (1, 3, tile, width), lambda s, i, m: (s, 0, i, 0)),
         across_made(3 * rank)],
        6 * tokens * width * width,
        weights=[qkv_w],
        after=[gate],
        limit=28 * 2**20,
        tiles=tiles,
    )
    gate, met = gather.round5([qkv])

    groups = width // GROUP

    def heads_of(slot, first, group=0):
        return pl.BlockSpec((1, 1, length, GROUP), lambda s, h: (s + first, slot, 0, h + group))

    def seg_specs(first):
        return [
            pl.BlockSpec((1, length, 1), lambda s, h: (s + first, 0, 0)),
            pl.BlockSpec((1, 1, length), lambda s, h: (s + first, 0, 0)),
        ]

    def lse_at(first, group=0):
        return pl.BlockSpec((1, 1, 8, length), lambda s, h: (s + first, h + group, 0, 0))

    def heads_at(first, group=0):
        return pl.BlockSpec((1, length, GROUP), lambda s, h: (s + first, 0, h + group))

    def attend(first, made, after):
        after_specs, after = waits(after)
        extra = len(made) + len(after)

        def body(q, k, v, sc, sr, *refs):
            attend_kernel(q, k, v, sc, sr, *refs[extra:])

        return pl.pallas_call(
            body,
            grid=(1, groups),
            in_specs=[heads_of(j, first) for j in range(3)]
            + seg_specs(first)
            + [pl.BlockSpec(memory_space=pltpu.HBM) for _ in made]
            + after_specs,
            out_specs=[heads_at(first), lse_at(first)],
            out_shape=[
                pltpu.HBM((mine, length, width), BF),
                pltpu.HBM((mine, groups, 8, length), F32),
            ],
            input_output_aliases={5 + i: i for i in range(len(made))},
            **params(16 * length * length * width, length * width * 8, 24 * 2**20),
        )(*[in_hbm(a) for a in [qkv, qkv, qkv, seg_col, seg_row, *made]], *after)

    attended = []
    for index in range(mine):
        attended = attend(index, attended, [] if index else [gate])
    attention, lse = attended
    gate, _ = gather.round6([lse, met])
    flat_c, gate, there = send_half(grad_out, [gate])

    normed, inverse, middle_low, rank_out = call(
        out_kernel, meta,
        [row(attention), row(x), last(a_t), last(adapt_b), whole(ln_gain), whole(ln_bias)],
        [rows_made(F32, width), rows_made(F32, 128), rows_made(BF, width), across_made(rank)],
        2 * tokens * width * width,
        scratch=[pltpu.VMEM((tile, width), F32)],
        weights=[out_w],
        limit=28 * 2**20,
        after=[gate],
        tiles=tiles,
    )

    cotangent, gate = join(flat_c, there, [rank_out])
    gate, _ = gather.last([gate])
    blocks = ff_half // part
    made_up = []
    for index, weight in enumerate(up_parts):
        up_cols = [
            (up_b, (1, rank, part), lambda s, i, m, at=h * blocks + index: (m[s], 0, at)) for h in range(2)
        ]
        units_made = (
            (mine, 2, length, ff_half), BF, (1, 2, tile, part), lambda s, i, m, index=index: (s, 0, i, index)
        )
        *made_up, rank_up = call(
            up_kernel, meta,
            [row(middle_low), factor(ua_t), *up_cols],
            [units_made, units_made, across_made(rank)],
            4 * tokens * width * part * 2,
            weights=[weight],
            limit=36 * 2**20,
            after=[gate],
            tiles=tiles,
            filled=made_up,
        )
        gate = rank_up
    units = lambda a: (a, (1, 2, tile, ff_half), lambda s, i, m: (s, 0, i, 0))
    act, slope = made_up

    layer_out, layer_sent, grad_first, grad_att, g_down_a, g_down_b, g_up_a, g_up_b, g_out_a, g_out_b = call(
        middle_kernel, meta,
        [units(act), units(slope), row(normed), row(inverse), row(cotangent), row(middle_low), row(attention),
         across(rank_up), across(rank_out), factor(da_t), factor(down_b), factor(ua_t), factor(up_b),
         last(a_t), last(adapt_b), whole(ln_gain), whole(ln_bias)],
        [*kept_made(BF), rows_made(F32, width), rows_made(BF, width),
         sum_made(rank, ff), sum_made(rank, width), sum_made(rank, width), sum_made(rank, ff),
         sum_made(rank, width), sum_made(rank, width)],
        tokens * width * (6 * ff + 2 * width),
        scratch=[pltpu.VMEM((tile, width), F32), pltpu.VMEM((tile, width), F32), pltpu.VMEM((tile, width), BF),
                 pltpu.VMEM((tile, ff), BF), pltpu.VMEM((tile, width), BF),
                 pltpu.VMEM((rank, ff), F32), pltpu.VMEM((rank, width), F32),
                 pltpu.VMEM((rank, width), F32), pltpu.VMEM((rank, ff), F32),
                 pltpu.VMEM((rank, width), F32), pltpu.VMEM((rank, width), F32)],
        weights=[down_w, up_w, out_w],
        tiles=tiles,
    )

    layer_there = swap(layer_sent)
    flat = lambda g: g.reshape(mine * rank, g.shape[-1])
    seqs = [g_down_a, g_down_b, g_up_a, g_up_b, g_out_a, g_out_b]
    fast = dp == 16
    gate = None
    if fast:
        first_sum = GradientSum(where, [flat(g) for g in seqs], mine, rank, adapters, picks)
        gate = first_sum.cores()

    halves = 2
    span = groups // halves

    def attend_back(first, group, made, after):
        after_specs, after = waits(after)
        extra = len(made) + len(after)

        def body(q, k, v, sc, sr, l, o, do, *refs):
            attend_back_kernel(q, k, v, sc, sr, l, o, do, *refs[extra:])

        args = [qkv, qkv, qkv, seg_col, seg_row, lse, attention, grad_att, *made]
        return pl.pallas_call(
            body,
            grid=(1, span),
            in_specs=[heads_of(j, first, group) for j in range(3)]
            + seg_specs(first)
            + [lse_at(first, group), heads_at(first, group), heads_at(first, group)]
            + [pl.BlockSpec(memory_space=pltpu.HBM) for _ in made]
            + after_specs,
            out_specs=[heads_at(first, group)] * 3,
            out_shape=[pltpu.HBM((mine, length, width), BF)] * 3,
            input_output_aliases={8 + i: i for i in range(len(made))},
            **params(40 * length * length * width // halves, length * width * 16, 32 * 2**20),
        )(*[in_hbm(a) for a in args], *after)

    grads_qkv = []
    between = iter([first_sum.plane, first_sum.fold, first_sum.depth, first_sum.back] if fast else [])
    for index in range(mine):
        for group in range(0, groups, span):
            grads_qkv = attend_back(index, group, grads_qkv, [gate])
            gate = None
            phase = next(between, None)
            if phase is not None and (index, group) != (mine - 1, groups - span):
                gate = phase([grads_qkv[0]])
    gate = first_sum.back([grads_qkv[0]]) if fast else None

    grad_rank, *later = call(
        rank_back_kernel, meta,
        [full(g) for g in grads_qkv] + [full(x), full(rank_qkv), slots(adapt_b)],
        [sum_made(3 * rank, length)] + [sum_made(rank, width)] * 6,
        18 * tokens * width * rank,
        after=[gate],
        limit=32 * 2**20,
    )
    gate = grad_rank
    if fast:
        second_sum = GradientSum(where, [flat(g) for g in later], mine, rank, adapters, picks)
        gate = second_sum.cores([gate])
        gate = first_sum.spread([gate])
        layer_out = place(where, layer_out, layer_there, [gate])
        gate = second_sum.plane([layer_out])

    grad_in, grad_sent = call(
        qkv_back_kernel, meta,
        [row(g) for g in grads_qkv] + [across(grad_rank), row(grad_first), slots(a_t)],
        kept_made(F32),
        6 * tokens * width * width,
        weights=[qkv_w],
        after=[gate],
        limit=40 * 2**20,
        tiles=tiles,
    )
    turned = lambda v: jnp.swapaxes(v, -1, -2)
    if fast:
        gate = second_sum.fold([grad_in])
        gate = first_sum.give([gate])
        gate = second_sum.depth([gate])
        there = swap(hold(grad_sent, [gate]))
        done1 = finish(where, [first_sum], [[(0, 0)], [(0, 1)], [(0, 2)], [(0, 3)]], [gate])
        gate = second_sum.back([done1[0]])
        grad_in = place(where, grad_in, there, [gate])
        gate = second_sum.spread([grad_in])
        second_sum.give([gate])
        all_a, all_b = finish(
            where, [second_sum, first_sum],
            [[(0, 0), (0, 1), (0, 2), (1, 4)], [(0, 3), (0, 4), (0, 5), (1, 5)]],
        )
        shaped = lambda v: v.reshape(-1, adapters, rank, v.shape[1])
        da, db, ua, ub = (shaped(v)[0] for v in done1)
        return (layer_out, grad_in, turned(shaped(all_a)), shaped(all_b), turned(ua), ub, turned(da), db)

    layer_out = place(where, layer_out, layer_there)
    grad_in = place(where, grad_in, swap(grad_sent))
    onehot = (pick[:, None] == jnp.arange(adapters)[None, :]).astype(F32)

    def fold(per_sequence):
        total = onehot[0][:, None, None] * per_sequence[0][None].astype(F32)
        for index in range(1, mine):
            total += onehot[index][:, None, None] * per_sequence[index][None].astype(F32)
        return total

    sums = lax.psum(
        tuple(fold(g) for g in [*later[:3], g_out_a, *later[3:], g_out_b, g_up_a, g_up_b, g_down_a, g_down_b]),
        ("dp", "tensor"),
    )
    return (
        layer_out,
        grad_in,
        turned(jnp.stack(sums[:4])),
        jnp.stack(sums[4:8]),
        turned(sums[8]),
        sums[9],
        turned(sums[10]),
        sums[11],
    )


def solution(mesh):
    placed = (
        P("dp", "tensor", None),
        P("dp", None),
        P("dp"),
        P(None, "dp", "tensor"),
        P("tensor", "dp"),
        P("dp", "tensor"),
        P("tensor", "dp"),
        P(),
        P(),
        P(),
        P(),
        P(),
        P(),
        P(),
        P(),
        P("dp", "tensor", None),
    )
    return jax.shard_map(
        shards,
        mesh=mesh,
        in_specs=placed,
        out_specs=(P("dp", "tensor", None), P("dp", "tensor", None), P(), P(), P(), P(), P(), P()),
        check_vma=False,
    )
```

```python
import functools

import jax
import jax.numpy as jnp
from jax import lax
from jax.experimental import pallas as pl
from jax.experimental.pallas import tpu as pltpu
from jax.sharding import PartitionSpec as P

HEAD_DIM = 64
BF = jnp.bfloat16
F32 = jnp.float32
LOG2E = 1.4426950408889634
VMEM = 60 * 2**20


def nn(a, b):
    return lax.dot_general(a, b, (((1,), (0,)), ((), ())), preferred_element_type=F32)


def nt(a, b):
    return lax.dot_general(a, b, (((1,), (1,)), ((), ())), preferred_element_type=F32)


def tn(a, b):
    return lax.dot_general(a, b, (((0,), (0,)), ((), ())), preferred_element_type=F32)


def params(flops, nbytes, limit=VMEM):
    return dict(
        compiler_params=pltpu.CompilerParams(vmem_limit_bytes=limit),
        cost_estimate=pl.CostEstimate(flops=flops, bytes_accessed=nbytes, transcendentals=0),
    )


class Piece:
    def __init__(self, col, width, rel, row, count, array, at, other):
        self.col, self.width, self.rel, self.row = col, width, rel, row
        self.count, self.array, self.at, self.other = count, array, at, other


def first_tile():
    return jnp.logical_and(pl.program_id(0) == 0, pl.program_id(1) == 0)


class Loader:
    def __init__(self, plan, refs, scratch, sems, me, t, dp):
        self.plan, self.refs, self.scratch, self.sems = plan, refs, scratch, sems
        self.me, self.t, self.dp = me, t, dp
        self.saved = None
        self.width = scratch.shape[1] // 2
        self.block = scratch.shape[0] // dp

    def start(self):
        def copy(source, block, row, count, into, width, other):
            rows = pl.ds(pl.multiple_of(block * self.block + row, 16), count)
            cols = pl.ds(pl.multiple_of((self.t ^ other) * self.width + into, 128), width)
            pltpu.make_async_copy(source, self.scratch.at[rows, cols], self.sems.at[other]).start()

        for slot, at, count, col, width, other, rel, row, into in self.plan:
            cols = pl.ds(col, width)
            if rel is None:
                for block in range(self.dp):
                    source = self.refs[slot].at[block, self.t ^ other, :, cols]
                    copy(source, block, 0, self.block, into, width, other)
            else:
                copy(self.refs[slot].at[pl.ds(at, count), cols], self.me ^ rel, row, count, into, width, other)

    def wait(self, other):
        cols = pl.ds(pl.multiple_of((self.t ^ other) * self.width, 128), self.width)
        whole = self.scratch.at[:, cols]
        pltpu.make_async_copy(whole, whole, self.sems.at[other]).wait()

    def first_step(self):
        pl.when(first_tile())(self.start)

    def first_wait(self, other):
        pl.when(first_tile())(lambda: self.wait(other))

    def first_wait_all(self):
        @pl.when(first_tile())
        def _():
            self.wait(0)
            self.wait(1)
            if self.saved is not None:
                for copy in self.save_copies():
                    copy.start()

    def save_copies(self):
        ref, first, sems = self.saved
        half = ref.shape[1] // 2
        return [
            pltpu.make_async_copy(
                self.scratch.at[:, pl.ds(h * self.width, self.width)],
                ref.at[:, pl.ds(h * half + first, self.width)],
                sems.at[h],
            )
            for h in range(2)
        ]

    def cols(self, half, lo, width):
        at = half * self.width + lo
        return self.scratch[:, pl.ds(at if isinstance(at, int) else pl.multiple_of(at, 128), width)]


class Held:
    def __init__(self, ref):
        self.scratch, self.width = ref, ref.shape[1] // 2

    cols = Loader.cols


def weight_plan(pieces, first, width):
    arrays, plan = [], []
    for p in pieces:
        lo, hi = max(p.col, first), min(p.col + p.width, first + width)
        if lo >= hi:
            continue
        slot = next((i for i, a in enumerate(arrays) if a is p.array), None)
        if slot is None:
            slot = len(arrays)
            arrays.append(p.array)
        plan.append((slot, p.at, p.count, lo - p.col, hi - lo, p.other, p.rel, p.row, lo - first))
    return arrays, plan


def qkv_kernel(meta, ins, outs, weights, scratch):
    x_ref, a_ref, b_ref = ins
    qkv_ref, rank_ref = outs
    (w,) = weights
    w.first_step()
    w.first_wait_all()
    x = x_ref[0]
    slots, rank_size = rank_ref.shape[1] // a_ref.shape[2], a_ref.shape[2]
    factors = a_ref[0:slots, 0].reshape(slots * rank_size, x.shape[1])
    rank = nt(x, factors).astype(BF)
    rank_ref[0] = nt(factors, x).astype(BF)
    width = w.width // slots
    for half in range(2):
        cols = slice(half * width, (half + 1) * width)
        for slot in range(slots):
            mine = rank[:, slot * rank_size : (slot + 1) * rank_size]
            full = nn(x, w.cols(half, slot * width, width)) + nn(mine, b_ref[slot, 0, :, cols])
            qkv_ref[0, slot, :, cols] = full.astype(BF)


SCALE = HEAD_DIM**-0.5
SCALE2 = SCALE * LOG2E
GROUP = 4 * HEAD_DIM


def one_head(lane, head, value):
    return jnp.where(lane // HEAD_DIM == head, value, jnp.zeros((), value.dtype))


def attend_kernel(q_ref, k_ref, v_ref, segc_ref, segr_ref, out_ref, lse_ref):
    q, k, v = q_ref[0, 0], k_ref[0, 0], v_ref[0, 0]
    length, lanes = q.shape
    heads = lanes // HEAD_DIM
    lane = lax.broadcasted_iota(jnp.int32, (1, lanes), 1)
    same = segc_ref[0] == segr_ref[0]
    v_t = v.T

    def score(head):
        return nt(one_head(lane, head, k), q)

    mixed = []
    scores = score(0)
    for head in range(heads):
        following = score(head + 1) if head + 1 < heads else None
        masked = jnp.where(same, scores, F32(-1000000000.0 / SCALE))
        peak = jnp.max(masked, axis=0, keepdims=True) * SCALE2
        weights = jnp.exp2(masked * SCALE2 - peak)
        mass = jnp.sum(weights, axis=0, keepdims=True)
        rows = slice(head * HEAD_DIM, (head + 1) * HEAD_DIM)
        mixed.append(nn(v_t[rows, :], weights.astype(BF)) * (1.0 / mass))
        lse_ref[0, 0, head : head + 1, :] = peak + jnp.log2(mass)
        scores = following
    out_ref[0] = jnp.concatenate(mixed, axis=0).astype(BF).T
    lse_ref[0, 0, heads:, :] = jnp.zeros((lse_ref.shape[2] - heads, length), F32)


def attend_back_kernel(
    q_ref, k_ref, v_ref, segc_ref, segr_ref, lse_ref, o_ref, do_ref, gq_ref, gk_ref, gv_ref
):
    q, k, v, do = q_ref[0, 0], k_ref[0, 0], v_ref[0, 0], do_ref[0]
    lanes = q.shape[1]
    lane = lax.broadcasted_iota(jnp.int32, (1, lanes), 1)
    product = do.astype(F32) * o_ref[0].astype(F32)
    high = product.astype(BF)
    low = (product - high.astype(F32)).astype(BF)
    picker = (
        lax.broadcasted_iota(jnp.int32, (8, lanes), 0)
        == lax.broadcasted_iota(jnp.int32, (8, lanes), 1) // HEAD_DIM
    ).astype(BF)
    inner = nt(picker, high) + nt(picker, low)
    same = segc_ref[0] == segr_ref[0]
    grad_q = grad_k = grad_v = None
    for head in range(lanes // HEAD_DIM):
        k_mine = one_head(lane, head, k)
        masked = jnp.where(same, nt(k_mine, q), F32(-1000000000.0 / SCALE))
        probs = jnp.exp2(masked * SCALE2 - lse_ref[0, 0, head : head + 1, :])
        grad_probs = nt(one_head(lane, head, v), do)
        grad_scores = (probs * (grad_probs - inner[head : head + 1, :])).astype(BF)
        part_v = nn(probs.astype(BF), one_head(lane, head, do))
        part_k = nn(grad_scores, one_head(lane, head, q))
        part_q = tn(grad_scores, k_mine)
        grad_v = part_v if head == 0 else grad_v + part_v
        grad_k = part_k if head == 0 else grad_k + part_k
        grad_q = part_q if head == 0 else grad_q + part_q
    gq_ref[0] = (grad_q * SCALE).astype(BF)
    gk_ref[0] = (grad_k * SCALE).astype(BF)
    gv_ref[0] = grad_v.astype(BF)


def norm_parts(values):
    mean = jnp.mean(values, axis=-1, keepdims=True)
    centred = values - mean
    inverse = lax.rsqrt(jnp.mean(centred * centred, axis=-1, keepdims=True) + 1e-06)
    return centred * inverse, inverse


def norm_back(scaled, normed, inverse):
    mean_grad = jnp.mean(scaled, axis=-1, keepdims=True)
    mean_proj = jnp.mean(scaled * normed, axis=-1, keepdims=True)
    return (scaled - mean_grad - normed * mean_proj) * inverse


ROWS = 64


def by_rows(count, step):
    for row in range(0, count, ROWS):
        step(slice(row, row + ROWS))


def out_kernel(meta, ins, outs, weights, scratch):
    att_ref, x_ref, a_ref, b_ref, gain_ref, bias_ref = ins
    normed_ref, inverse_ref, low_ref, rank_ref = outs
    (w,) = weights
    (v_scr,) = scratch
    w.first_step()
    w.first_wait_all()
    att = att_ref[0]
    rank = nt(att, a_ref[0, 0]).astype(BF)
    rank_ref[0] = nt(a_ref[0, 0], att).astype(BF)
    width = w.width
    v_scr[...] = (
        nt(att[:, :width], w.cols(0, 0, width))
        + nt(att[:, width:], w.cols(1, 0, width))
        + nn(rank, b_ref[0, 0])
    )

    def step(rows):
        normed, inverse = norm_parts(v_scr[rows, :] + x_ref[0, rows, :].astype(F32))
        normed_ref[0, rows, :] = normed
        inverse_ref[0, rows, :] = jnp.broadcast_to(inverse, (ROWS, 128))
        low_ref[0, rows, :] = (normed * gain_ref[0:1, :] + bias_ref[0:1, :]).astype(BF)

    by_rows(v_scr.shape[0], step)


def gelu_parts(x):
    phi = 0.5 + 0.5 * lax.erf(x * 0.7071067811865476)
    density = jnp.exp2((-0.5 * LOG2E) * x * x)
    return x * phi, phi + x * (density * 0.3989422804014327)


CHUNK = 512


def up_kernel(meta, ins, outs, weights, scratch):
    m_ref, a_ref = ins[:2]
    b_refs = ins[2:]
    act_ref, slope_ref, rank_ref = outs
    (w,) = weights
    w.first_step()
    w.first_wait_all()
    m = m_ref[0]
    rank = nt(m, a_ref[0]).astype(BF)
    rank_ref[0] = nt(a_ref[0], m).astype(BF)
    width = w.width
    for half, b_ref in enumerate(b_refs):
        for lo in range(0, width, CHUNK):
            cols = slice(lo, lo + CHUNK)
            units = nn(m, w.cols(half, lo, CHUNK)) + nn(rank, b_ref[0, :, cols])
            act, slope = gelu_parts(units)
            act_ref[0, half, :, cols] = act.astype(BF)
            slope_ref[0, half, :, cols] = slope.astype(BF)


def add_up(total, part, fresh):
    total[...] = jnp.where(fresh, part, total[...] + part)


def keep_or_send(t, value, kept_ref, sent_ref):
    @pl.when(pl.program_id(1) == t)
    def _():
        kept_ref[0] = value

    @pl.when(pl.program_id(1) != t)
    def _():
        sent_ref[0] = value


def middle_kernel(meta, ins, outs, weights, scratch):
    (act_ref, slope_ref, n1_ref, r1_ref, go_ref, m_ref, att_ref, ranku_ref, ranko_ref,
     da_ref, db_ref, ua_ref, ub_ref, oa_ref, ob_ref, gain_ref, bias_ref) = ins
    kept_ref, sent_ref, first_ref, gatt_ref = outs[:4]
    down, late_up, early_up, out = weights
    v_scr, second_scr, gf_scr, gh_scr, out_scr = scratch[:5]
    sums = scratch[5:]
    sum_da, sum_db, sum_ua, sum_ub, sum_oa, sum_ob = sums
    tile = pl.program_id(1)
    fresh = tile == 0
    for loader in (down, late_up):
        loader.first_step()
    for loader in (down, late_up):
        loader.first_wait_all()
    width = down.width
    part = early_up.width
    halves = [slice(0, width), slice(width, 2 * width)]

    rank = sum(nt(act_ref[0, h], da_ref[0, :, halves[h]]) for h in range(2)).astype(BF)
    model = v_scr.shape[1]
    for at in range(0, model, CHUNK):
        cols = slice(at, at + CHUNK)
        v_scr[:, cols] = (
            nt(act_ref[0, 0], down.scratch[cols, halves[0]])
            + nt(act_ref[0, 1], down.scratch[cols, halves[1]])
            + nn(rank, db_ref[0, :, cols])
        )

    def second_norm(rows):
        middle = n1_ref[0, rows, :] * gain_ref[0:1, :] + bias_ref[0:1, :]
        normed, inverse = norm_parts(v_scr[rows, :] + middle)
        out_scr[rows, :] = (normed * gain_ref[1:2, :] + bias_ref[1:2, :]).astype(BF)
        second = norm_back(go_ref[0, rows, :].astype(F32) * gain_ref[1:2, :], normed, inverse)
        second_scr[rows, :] = second
        gf_scr[rows, :] = second.astype(BF)

    by_rows(v_scr.shape[0], second_norm)
    grad_feed = gf_scr[...]
    add_up(sum_db, tn(rank, grad_feed), fresh)
    grad_rank = nt(grad_feed, db_ref[0]).astype(BF)
    chunk = 2 * CHUNK
    for half in range(2):
        for lo in range(0, width, chunk):
            cols = slice(half * width + lo, half * width + lo + chunk)
            grad_act = nn(grad_feed, down.cols(half, lo, chunk)) + nn(grad_rank, da_ref[0, :, cols])
            local = slice(lo, lo + chunk)
            gh_scr[:, cols] = (grad_act * slope_ref[0, half, :, local].astype(F32)).astype(BF)
    grad_rank_down = grad_rank

    grad_rank = nt(gh_scr[...], ub_ref[0]).astype(BF)
    for at in range(0, model, CHUNK):
        cols = slice(at, at + CHUNK)
        total = nn(grad_rank, ua_ref[0, :, cols])
        for half in range(2):
            lo = half * width
            local = slice(half * part, (half + 1) * part)
            total = total + nt(gh_scr[:, lo : lo + part], early_up.scratch[cols, local])
            total = total + nt(gh_scr[:, lo + part : lo + width], late_up.scratch[cols, local])
        v_scr[:, cols] = total
    add_up(sum_ua, tn(grad_rank, m_ref[0]), fresh)
    add_up(sum_ub, nn(ranku_ref[0], gh_scr[...]), fresh)
    for half in range(2):
        add_up(sum_da.at[:, halves[half]], tn(grad_rank_down, act_ref[0, half]), fresh)

    def first_norm(rows):
        scaled = (second_scr[rows, :] + v_scr[rows, :]) * gain_ref[0:1, :]
        first = norm_back(scaled, n1_ref[0, rows, :], r1_ref[0, rows, 0:1])
        first_ref[0, rows, :] = first
        gf_scr[rows, :] = first.astype(BF)

    by_rows(v_scr.shape[0], first_norm)
    grad_branch = gf_scr[...]
    grad_rank = nt(grad_branch, ob_ref[0, 0]).astype(BF)
    add_up(sum_oa, tn(grad_rank, att_ref[0]), fresh)
    add_up(sum_ob, nn(ranko_ref[0], grad_branch), fresh)
    owidth = out.width
    for half in range(2):
        cols = slice(half * owidth, (half + 1) * owidth)
        full = nn(grad_branch, out.cols(half, 0, owidth)) + nn(grad_rank, oa_ref[0, 0, :, cols])
        gatt_ref[0, :, cols] = full.astype(BF)

    keep_or_send(down.t, out_scr[...], kept_ref, sent_ref)

    @pl.when(tile == pl.num_programs(1) - 1)
    def _():
        for total, ref in zip(sums, outs[4:]):
            ref[0] = total[...].astype(BF)


def rank_back_kernel(meta, ins, outs, weights, scratch):
    gq_ref, gk_ref, gv_ref, x_ref, rank_ref, b_ref = ins
    gr_ref, a_refs, b_refs = outs[0], outs[1:4], outs[4:]
    size = b_ref.shape[2]
    ranks = []
    for slot, ref in enumerate((gq_ref, gk_ref, gv_ref)):
        grad = ref[0]
        ranks.append(nt(b_ref[slot, 0], grad))
        b_refs[slot][0] = nn(rank_ref[0, slot * size : (slot + 1) * size, :], grad).astype(BF)
    stacked = jnp.concatenate(ranks, axis=0).astype(BF)
    gr_ref[0] = stacked
    products = nn(stacked, x_ref[0]).astype(BF)
    for slot, ref in enumerate(a_refs):
        ref[0] = products[slot * size : (slot + 1) * size]


def qkv_back_kernel(meta, ins, outs, weights, scratch):
    gq_ref, gk_ref, gv_ref, gr_ref, first_ref, a_ref = ins
    kept_ref, sent_ref = outs
    (w,) = weights
    slots = 3
    width = w.width // slots
    size = a_ref.shape[2]
    total = first_ref[0] + tn(
        gr_ref[0], a_ref[0:slots, 0].reshape(slots * size, kept_ref.shape[2])
    )
    for half in range(2):
        cols = slice(half * width, (half + 1) * width)
        for slot, ref in enumerate((gq_ref, gk_ref, gv_ref)):
            total += nt(ref[0, :, cols], w.cols(half, slot * width, width))
    keep_or_send(meta[meta.shape[0] - 1], total, kept_ref, sent_ref)


NEAR = []


def made_near(arrays):
    NEAR.extend(arrays)
    return arrays


def waits(arrays):
    arrays = [a for a in arrays if a is not None]
    near = [any(a is n for n in NEAR) for a in arrays]
    specs = [pl.BlockSpec(memory_space=pl.ANY if n else pltpu.HBM) for n in near]
    return specs, [a if n else in_hbm(a) for a, n in zip(arrays, near)]


def call(kernel, meta, ins, outs, flops, scratch=(), weights=(), limit=VMEM, after=(), tiles=1, filled=(),
         saves=(), held=()):
    plans = [weight_plan(pieces, first, width) for pieces, first, width, _, _ in weights]
    n_in, n_out, n_w = len(ins), len(outs), len(weights)
    counts = [len(arrays) for arrays, _ in plans]
    steps = meta.shape[0] - 2
    after_specs, after = waits(after)
    n_after = len(after)

    def body(meta_ref, *refs):
        refs = list(refs)
        take = lambda n: [refs.pop(0) for _ in range(n)]
        in_refs = take(n_in)
        w_refs = [take(n) for n in counts]
        take(n_after + len(filled))
        held_refs = take(len(held))
        take(len(started))
        out_refs = take(n_out)
        save_refs = take(len(saves))
        w_scr = take(n_w)
        w_sem = take(n_w)
        save_sems = take(len(saves))
        me, t = meta_ref[steps], meta_ref[steps + 1]
        loaders = [
            Loader(plan, r, s, m, me, t, w[3])
            for (_, plan), r, s, m, w in zip(plans, w_refs, w_scr, w_sem, weights)
        ]
        for (number, _, first, _), ref, sem in zip(saves, save_refs, save_sems):
            loaders[number].saved = (ref, first, sem)
        kernel(meta_ref, in_refs, out_refs, loaders + [Held(ref) for ref in held_refs], refs)
        for number, *_ in saves:

            @pl.when(jnp.logical_and(pl.program_id(0) == steps - 1, pl.program_id(1) == tiles - 1))
            def _(loader=loaders[number]):
                for copy in loader.save_copies():
                    copy.wait()

    started = [array for *_, array in saves if array is not None]
    w_arrays = [a for arrays, _ in plans for a in arrays]
    first_alias = 1 + n_in + len(w_arrays) + n_after
    nbytes = sum(a.size * a.dtype.itemsize for a, _, _ in ins)
    nbytes += sum(2 * dp * rows * width * 2 for _, _, width, dp, rows in weights)
    for shape, dtype, _, _ in outs:
        size = jnp.dtype(dtype).itemsize
        for extent in shape:
            size *= extent
        nbytes += size
    return pl.pallas_call(
        body,
        grid_spec=pltpu.PrefetchScalarGridSpec(
            num_scalar_prefetch=1,
            grid=(steps, tiles),
            in_specs=[pl.BlockSpec(block, index) for _, block, index in ins]
            + [pl.BlockSpec(memory_space=pltpu.HBM) for _ in w_arrays]
            + after_specs
            + [pl.BlockSpec(memory_space=pltpu.HBM) for _ in filled]
            + [pl.BlockSpec(memory_space=pltpu.VMEM) for _ in held]
            + [pl.BlockSpec(memory_space=pltpu.HBM) for _ in started],
            out_specs=[pl.BlockSpec(block, index) for _, _, block, index in outs]
            + [pl.BlockSpec(memory_space=pltpu.HBM) for _ in saves],
            scratch_shapes=[pltpu.VMEM((dp * rows, 2 * width), BF) for _, _, width, dp, rows in weights]
            + [pltpu.SemaphoreType.DMA((2,)) for _ in [*weights, *saves]]
            + list(scratch),
        ),
        out_shape=[pltpu.HBM(shape, dtype) for shape, dtype, _, _ in outs]
        + [pltpu.HBM((weights[n][3] * weights[n][4], 2 * half), BF) for n, half, _, _ in saves],
        input_output_aliases={first_alias + i: i for i in range(len(filled))}
        | {first_alias + len(filled) + len(held) + i: n_out + i for i in range(len(started))},
        **params(flops, nbytes, limit),
    )(
        meta, *[in_hbm(a) for a in [*[a for a, _, _ in ins], *w_arrays]], *after, *[in_hbm(a) for a in filled],
        *[pltpu.with_memory_space_constraint(a, pltpu.VMEM) for a in held], *[in_hbm(a) for a in started],
    )


def pack(outs, fresh=(), after=()):
    after_specs, after = waits(after)
    arrays, plan, heights, widths = [], [], [], []

    def slot(array):
        for index, known in enumerate(arrays):
            if known is array:
                return index
        arrays.append(array)
        return len(arrays) - 1

    for index, parts in enumerate(outs):
        row = 0
        for part in parts:
            array, at, count, col, cols, into, advance = part
            plan.append((slot(array), at, count, col, cols, index, row, into))
            if advance:
                row += count
        heights.append(row)
        widths.append(max(part[4] + part[5] for part in parts))
    used, n_in = len(arrays), len(arrays) + len(after)
    near = [any(a is f for f in fresh) for a in arrays]

    def kernel(*refs):
        ins, results, sems = refs[:n_in], refs[n_in:-1], refs[-1]
        copies = []
        for number, (a, at, count, col, cols, o, row, into) in enumerate(plan):
            source = ins[a].at[pl.ds(at, count), pl.ds(col, cols)]
            target = results[o].at[pl.ds(row, count), pl.ds(into, cols)]
            if not near[a]:
                copy = pltpu.make_async_copy(source, target, sems.at[number])
                copy.start()
                copies.append(copy)
        for a, at, count, col, cols, o, row, into in plan:
            if near[a]:
                results[o][pl.ds(row, count), pl.ds(into, cols)] = ins[a][pl.ds(at, count), pl.ds(col, cols)]
        for copy in copies:
            copy.wait()

    spaces = [pltpu.VMEM if n else pltpu.HBM for n in near]
    return made_near(pl.pallas_call(
        kernel,
        in_specs=[pl.BlockSpec(memory_space=space) for space in spaces] + after_specs,
        out_specs=[pl.BlockSpec(memory_space=pltpu.VMEM)] * len(outs),
        out_shape=[pltpu.VMEM(shape, BF) for shape in zip(heights, widths)],
        scratch_shapes=[pltpu.SemaphoreType.DMA((len(plan),))],
        compiler_params=pltpu.CompilerParams(vmem_limit_bytes=8 * 2**20),
        cost_estimate=pl.CostEstimate(
            flops=0, bytes_accessed=sum(h * w * 4 for h, w in zip(heights, widths)), transcendentals=0
        ),
    )(*[pltpu.with_memory_space_constraint(a, space) for a, space in zip(arrays, spaces)], *after))


def in_hbm(array):
    return pltpu.with_memory_space_constraint(array, pltpu.HBM)


X, Y, Z1, Z2, Z3 = 1, 2, 4, 8, 12
ZS = (Z1, Z2, Z3)


def hop(array, bits):
    return lax.ppermute(array, "dp", [(i, i ^ bits) for i in range(lax.axis_size("dp"))])


def swap(array):
    return lax.ppermute(array, "tensor", [(0, 1), (1, 0)])


class Gather:
    def __init__(self, w_qkv, w_out, w_up, w_down):
        self.n = n = w_up.shape[0]
        self.h = n // 2
        self.pieces = []
        o, u = w_qkv.shape[2], w_up.shape[1]
        self.width = 3 * o
        flat = w_qkv.reshape(3 * n, o)
        wo, wd = w_out.T, w_down.T
        queries = [(flat, slot * n, n, 0, o, slot * o, slot == 2) for slot in range(3)]
        rest = [
            (wo, 0, n, 0, o, 0, False), (w_up, 0, n, 0, 2 * o, o, True),
            (w_up, 0, n, 2 * o, u - 2 * o, 0, False), (wd, 0, n, 0, o, 2 * o, True),
            (wd, 0, n, o, 3 * o, 0, True),
        ]
        self.own, self.q = pack([queries + rest, queries])
        self.gate = self.q
        self.e, self.f, self.g = (self.cut(p) for p in (1, 2, 3))

    def cut(self, piece):
        return lax.slice_in_dim(self.own, piece * self.n, (piece + 1) * self.n, axis=0)

    def note(self, array, items, other=0):
        at = 0
        for piece, rel, row, count in items:
            self.pieces.append(Piece(piece * self.width, self.width, rel, row, count, array, at, other))
            at += count

    def part(self, array, at, count):
        return (array, at, count, 0, self.width, 0, True)

    def full(self, piece, *rels):
        return [(piece, rel, 0, self.n) for rel in rels]

    def upper(self, piece, *rels):
        return [(piece, rel, self.h, self.h) for rel in rels]

    def lower(self, piece, *rels):
        return [(piece, rel, 0, self.h) for rel in rels]

    def exchange(self, arrays, after=()):
        fresh = [a for a, _ in arrays if a is not self.own]
        (packed,) = pack([[self.part(a, 0, a.shape[0]) for a, _ in arrays]], fresh=fresh, after=after)
        (other,) = made_near([swap(packed)])
        self.note(other, [item for _, items in arrays for item in items], 1)
        return packed, other

    def keep(self, got):
        for array, items in got:
            self.note(array, items)
        return got

    def round1(self):
        self.zq = [hop(self.q, k) for k in ZS]
        self.x1, self.y1 = hop(self.own, X), hop(self.own, Y)
        every = range(4)
        got = [(self.own, [i for p in every for i in self.full(p, 0)])]
        got += [(self.x1, [i for p in every for i in self.full(p, X)])]
        got += [(self.y1, [i for p in every for i in self.full(p, Y)])]
        got += [(z, self.full(0, k)) for z, k in zip(self.zq, ZS)]
        self.got1 = self.keep(got)

    def round2(self, after):
        n, h, part = self.n, self.h, self.part
        along = [part(z, 0, n) for z in self.zq]
        xin, yin, e = pack(
            [along + [part(self.y1, h, h)], along + [part(self.x1, 0, h)], [part(self.own, n, n)]],
            fresh=[*self.zq, self.x1, self.y1],
            after=after,
        )
        x, y, self.ze2 = hop(xin, X), hop(yin, Y), hop(e, Z2)
        self.x, self.y = x, y
        self.got2 = self.keep([
            (x, self.full(0, *(X | k for k in ZS)) + self.upper(0, X | Y)),
            (y, self.full(0, *(Y | k for k in ZS)) + self.lower(0, X | Y)),
            (self.ze2, self.full(1, Z2)),
        ])
        return self.exchange(self.got1, [xin])

    def round3(self, after):
        n, h, part = self.n, self.h, self.part
        xin, yin, e, f = pack(
            [
                [part(self.y, i * n + h, h) for i in range(3)] + [part(self.y1, p * n + h, h) for p in (1, 2)],
                [part(self.x, i * n, h) for i in range(3)] + [part(self.x1, p * n, h) for p in (1, 2)],
                [part(self.own, n, n), part(self.ze2, 0, n)],
                [part(self.own, 2 * n, n)],
            ],
            fresh=[self.x, self.y, self.ze2],
            after=after,
        )
        x, y, self.ze1, self.zf2 = hop(xin, X), hop(yin, Y), hop(e, Z1), hop(f, Z2)
        self.x, self.y = x, y
        both = [X | Y | k for k in ZS]
        self.got3 = self.keep([
            (x, self.upper(0, *both) + self.upper(1, X | Y) + self.upper(2, X | Y)),
            (y, self.lower(0, *both) + self.lower(1, X | Y) + self.lower(2, X | Y)),
        ])
        self.late3 = self.keep([(self.ze1, self.full(1, Z1, Z3)), (self.zf2, self.full(2, Z2))])
        return self.exchange(self.got2, [xin])

    def round4(self, after):
        n, h, part = self.n, self.h, self.part
        along = [part(self.ze1, 0, n), part(self.ze2, 0, n), part(self.ze1, n, n)]
        xin, yin, f, g = pack(
            [
                along + [part(self.y1, 3 * n + h, h)],
                along + [part(self.x1, 3 * n, h)],
                [part(self.own, 2 * n, n), part(self.zf2, 0, n)],
                [part(self.own, 3 * n, n)],
            ],
            fresh=[self.ze1, self.zf2],
            after=after,
        )
        x, y, self.zf1, self.zg2 = hop(xin, X), hop(yin, Y), hop(f, Z1), hop(g, Z2)
        self.x, self.y = x, y
        self.got4 = self.keep([
            (x, self.full(1, *(X | k for k in ZS)) + self.upper(3, X | Y)),
            (y, self.full(1, *(Y | k for k in ZS)) + self.lower(3, X | Y)),
            (self.zf1, self.full(2, Z1, Z3)),
            (self.zg2, self.full(3, Z2)),
        ])
        return self.exchange(self.got3, [xin])

    def round5(self, after):
        n, h, part = self.n, self.h, self.part
        along = [part(self.zf1, 0, n), part(self.zf2, 0, n), part(self.zf1, n, n)]
        xin, yin, g, d = pack(
            [
                [part(self.y, i * n + h, h) for i in range(3)] + along,
                [part(self.x, i * n, h) for i in range(3)] + along,
                [part(self.own, 3 * n, n), part(self.zg2, 0, n)],
                [part(self.y, 3 * n, h), part(self.x, 3 * n, h)],
            ],
            fresh=[self.x, self.y, self.zf1, self.zg2],
            after=after,
        )
        self.d = d
        x, y, self.zg1, self.zd2 = hop(xin, X), hop(yin, Y), hop(g, Z1), hop(d, Z2)
        self.x, self.y = x, y
        both = [X | Y | k for k in ZS]
        self.got5 = self.keep([
            (x, self.upper(1, *both) + self.full(2, *(X | k for k in ZS))),
            (y, self.lower(1, *both) + self.full(2, *(Y | k for k in ZS))),
            (self.zg1, self.full(3, Z1, Z3)),
            (self.zd2, self.full(3, X | Y | Z2)),
        ])
        return self.exchange(self.late3 + self.got4, [xin])

    def round6(self, after):
        n, h, part = self.n, self.h, self.part
        along = [part(self.zg1, 0, n), part(self.zg2, 0, n), part(self.zg1, n, n)]
        xin, yin, d = pack(
            [
                [part(self.y, 3 * h + i * n + h, h) for i in range(3)] + along,
                [part(self.x, 3 * h + i * n, h) for i in range(3)] + along,
                [part(self.d, 0, n), part(self.zd2, 0, n)],
            ],
            fresh=[self.x, self.y, self.zg1, self.zd2],
            after=after,
        )
        x, y, zd1 = hop(xin, X), hop(yin, Y), hop(d, Z1)
        both = [X | Y | k for k in ZS]
        self.got6 = self.keep([
            (x, self.upper(2, *both) + self.full(3, *(X | k for k in ZS))),
            (y, self.lower(2, *both) + self.full(3, *(Y | k for k in ZS))),
            (zd1, self.full(3, X | Y | Z1, X | Y | Z3)),
        ])
        return self.exchange(self.got5, [xin])

    def last(self, after):
        return self.exchange(self.got6, after)


class GatherPlain:
    def __init__(self, w_qkv, w_out, w_up, w_down):
        local = jnp.concatenate([w_qkv[0], w_qkv[1], w_qkv[2], w_out.T, w_up, w_down.T], axis=1)
        rows, width = local.shape
        whole = lax.all_gather(local, ("dp", "tensor")).reshape(lax.axis_size("dp"), 2, rows, width)
        self.pieces = [Piece(0, width, None, 0, 0, whole, 0, other) for other in range(2)]
        self.gate = None

    def round1(self):
        return None

    def round2(self, after):
        return None, None

    round3 = round4 = round5 = round6 = last = round2


class Spot:
    def __init__(self, array, row, rows, col, cols):
        self.array, self.row, self.rows, self.col, self.cols = array, row, rows, col, cols

    def of(self, ref, me, t):
        at = lambda v, unit: pl.multiple_of(v(me, t), unit) if callable(v) else v
        return ref.at[pl.ds(at(self.row, 16), self.rows), pl.ds(at(self.col, 128), self.cols)]


def arrange(where, shapes, moves, fresh=(), after=()):
    after_specs, after = waits(after)
    arrays = []
    for source, _, _ in moves:
        if not any(a is source.array for a in arrays):
            arrays.append(source.array)
    near = [any(a is f for f in fresh) for a in arrays]
    number = lambda array: next(i for i, a in enumerate(arrays) if a is array)
    plan = [(number(source.array), source, out, target) for source, out, target in moves]

    def kernel(where_ref, *refs):
        ins, results, sems = refs[: len(arrays)], refs[len(arrays) + len(after) : -1], refs[-1]
        me, t = where_ref[0], where_ref[1]
        copies = []
        for index, (slot, source, out, target) in enumerate(plan):
            copy = pltpu.make_async_copy(
                source.of(ins[slot], me, t), target.of(results[out], me, t), sems.at[index]
            )
            copy.start()
            copies.append(copy)
        for copy in copies:
            copy.wait()

    spaces = [pltpu.VMEM if n else pltpu.HBM for n in near]
    return made_near(pl.pallas_call(
        kernel,
        in_specs=[pl.BlockSpec(memory_space=pltpu.SMEM)]
        + [pl.BlockSpec(memory_space=m) for m in spaces]
        + after_specs,
        out_specs=[pl.BlockSpec(memory_space=pltpu.VMEM)] * len(shapes),
        out_shape=[pltpu.VMEM(shape, BF) for shape in shapes],
        scratch_shapes=[pltpu.SemaphoreType.DMA((len(plan),))],
        compiler_params=pltpu.CompilerParams(vmem_limit_bytes=8 * 2**20),
        cost_estimate=pl.CostEstimate(
            flops=0, bytes_accessed=sum(h * w * 4 for h, w in shapes), transcendentals=0
        ),
    )(where, *[pltpu.with_memory_space_constraint(a, m) for a, m in zip(arrays, spaces)], *after))


class GradientSum:
    def __init__(self, where, arrays, mine, rank, adapters, picks):
        self.where, self.arrays, self.picks = where, arrays, picks
        self.mine, self.rank, self.adapters = mine, rank, adapters
        self.rows = mine * rank
        self.widths = [a.shape[1] for a in arrays]
        self.starts = [sum(self.widths[:i]) for i in range(len(arrays))]
        self.total = sum(self.widths)
        self.chunk = self.total // 8

    def cores(self, after=()):
        half = self.total // 2
        moves = [
            (
                Spot(a, 0, self.rows, lambda me, t, w=w: (1 - t) * (w // 2), w // 2),
                0,
                Spot(None, 0, self.rows, s // 2, w // 2),
            )
            for a, w, s in zip(self.arrays, self.widths, self.starts)
        ]
        (out,) = arrange(self.where, [(self.rows, half)], moves, after=after)
        self.other = swap(out)
        return out

    def plane(self, after=()):
        moves = []
        for k in range(4):
            for a, w, s in zip(self.arrays, self.widths, self.starts):
                e = w // 8
                moves.append((
                    Spot(a, 0, self.rows, lambda me, t, e=e, k=k: (t * 4 + ((me & 3) ^ k)) * e, e),
                    k,
                    Spot(None, 0, self.rows, s // 8, e),
                ))
                moves.append((
                    Spot(self.other, 0, self.rows, lambda me, t, e=e, s=s, k=k: s // 2 + ((me & 3) ^ k) * e, e),
                    k,
                    Spot(None, self.rows, self.rows, s // 8, e),
                ))
            moves.append((
                Spot(self.picks, 0, self.rank, 0, self.chunk), k, Spot(None, 2 * self.rows, self.rank, 0, self.chunk)
            ))
        shape = (2 * self.rows + self.rank, self.chunk)
        outs = arrange(self.where, [shape] * 4, moves, fresh=[self.other], after=after)
        self.parts = [outs[0], hop(outs[1], X), hop(outs[2], Y), hop(outs[3], X | Y)]
        return outs[0]

    def fold(self, after=()):
        rank, chunk, data = self.rank, self.chunk, 2 * self.rows
        tall = self.adapters * rank
        quarter = tall // 4

        def kernel(where_ref, *refs):
            ins, outs, total = refs[:4], refs[-5:-1], refs[-1]
            z = where_ref[0] // 4
            row = lax.broadcasted_iota(jnp.int32, (tall, data), 0)
            col = lax.broadcasted_iota(jnp.int32, (tall, data), 1)
            adapter = (row // rank).astype(F32)
            same_row = row % rank == col % rank
            for k in range(4):
                picks = ins[k][data : data + 1, 0:data].astype(F32)
                chosen = jnp.logical_and(adapter == picks, same_row).astype(F32).astype(BF)
                part = nn(chosen, ins[k][0:data, :])
                total[...] = part if k == 0 else total[...] + part
            for k in range(4):
                rows = pl.ds(pl.multiple_of((z ^ k) * quarter, quarter), quarter)
                outs[k][...] = total[rows, :].astype(BF)

        outs = self.local(kernel, self.parts, after, [(quarter, chunk)] * 4, [(tall, chunk)])
        self.parts = [outs[0]] + [hop(outs[k], 4 * k) for k in (1, 2, 3)]
        return outs[0]

    def local(self, kernel, arrays, after, shapes, scratch):
        after_specs, after = waits(after)
        vmem = pl.BlockSpec(memory_space=pltpu.VMEM)
        return made_near(pl.pallas_call(
            kernel,
            in_specs=[pl.BlockSpec(memory_space=pltpu.SMEM)] + [vmem] * len(arrays) + after_specs,
            out_specs=[vmem] * len(shapes),
            out_shape=[pltpu.VMEM(shape, BF) for shape in shapes],
            scratch_shapes=[pltpu.VMEM(shape, F32) for shape in scratch],
            compiler_params=pltpu.CompilerParams(vmem_limit_bytes=12 * 2**20),
            cost_estimate=pl.CostEstimate(
                flops=0, bytes_accessed=sum(h * w * 8 for h, w in shapes), transcendentals=0
            ),
        )(
            self.where,
            *[pltpu.with_memory_space_constraint(a, pltpu.VMEM) for a in arrays],
            *after,
        ))

    def depth(self, after=()):
        def kernel(where_ref, *refs):
            total = refs[0][...].astype(F32)
            for ref in refs[1:4]:
                total += ref[...].astype(F32)
            refs[-1][...] = total.astype(BF)

        (out,) = self.local(kernel, self.parts, after, [self.parts[0].shape], [])
        self.parts = [out] + [hop(out, 4 * k) for k in (1, 2, 3)]
        return out

    def back(self, after=()):
        tall = self.adapters * self.rank
        quarter, side = tall // 4, self.chunk // 2
        moves = [
            (
                Spot(self.parts[k], 0, quarter, part * side, side),
                part,
                Spot(None, lambda me, t, k=k: ((me >> 2) ^ k) * quarter, quarter, 0, side),
            )
            for k in range(4)
            for part in range(2)
        ]
        self.a, self.b = arrange(self.where, [(tall, side)] * 2, moves, fresh=self.parts, after=after)
        self.xa, self.yb = hop(self.a, X), hop(self.b, Y)
        return self.a

    def spread(self, after=()):
        tall, side = self.adapters * self.rank, self.chunk // 2
        moves = [
            (Spot(source, 0, tall, 0, side), out, Spot(None, row * tall, tall, 0, side))
            for out, pair in enumerate(((self.a, self.xa), (self.b, self.yb)))
            for row, source in enumerate(pair)
        ]
        fresh = [self.a, self.b, self.xa, self.yb]
        up, down = arrange(self.where, [(2 * tall, side)] * 2, moves, fresh=fresh, after=after)
        self.ya, self.xb = hop(up, Y), hop(down, X)
        return up

    def give(self, after=()):
        tall, side = self.adapters * self.rank, self.chunk // 2
        sources = [
            ((self.a, 0), (self.b, 0)),
            ((self.xa, 0), (self.xb, 0)),
            ((self.ya, 0), (self.yb, 0)),
            ((self.ya, tall), (self.xb, tall)),
        ]
        moves = [
            (Spot(source, row, tall, 0, side), 0, Spot(None, k * tall, tall, part * side, side))
            for k, both in enumerate(sources)
            for part, (source, row) in enumerate(both)
        ]
        fresh = [self.a, self.b, self.xa, self.yb, self.ya, self.xb]
        (out,) = arrange(self.where, [(4 * tall, self.chunk)], moves, fresh=fresh, after=after)
        self.theirs = swap(out)
        self.ours = out
        return out


def finish(where, sums, results, after=()):
    tall = sums[0].adapters * sums[0].rank
    after_specs, after = waits(after)
    inputs = [a for s in sums for a in (s.ours, s.theirs)]

    def kernel(where_ref, *refs):
        outs = refs[len(inputs) + len(after) :]
        me, t = where_ref[0], where_ref[1]
        for out, parts in zip(outs, results):
            for place, (number, which) in enumerate(parts):
                total = sums[number]
                start, width = total.starts[which] // 8, total.widths[which] // 8
                for core in range(2):
                    for k in range(4):
                        column = ((t ^ core) * 4 + ((me & 3) ^ k)) * width
                        out[place * tall : (place + 1) * tall, pl.ds(pl.multiple_of(column, 128), width)] = refs[
                            2 * number + core
                        ][k * tall : (k + 1) * tall, start : start + width].astype(F32)

    vmem = pl.BlockSpec(memory_space=pltpu.VMEM)
    shapes = [(len(parts) * tall, sums[parts[0][0]].widths[parts[0][1]]) for parts in results]
    return pl.pallas_call(
        kernel,
        in_specs=[pl.BlockSpec(memory_space=pltpu.SMEM)]
        + [vmem] * len(inputs)
        + after_specs,
        out_specs=[vmem] * len(results),
        out_shape=[pltpu.HBM(shape, F32) for shape in shapes],
        compiler_params=pltpu.CompilerParams(vmem_limit_bytes=32 * 2**20),
        cost_estimate=pl.CostEstimate(
            flops=0, bytes_accessed=sum(h * w * 6 for h, w in shapes), transcendentals=0
        ),
    )(where, *inputs, *after)


def hold(array, after):
    after_specs, after = waits(after)
    return pl.pallas_call(
        lambda *refs: None,
        in_specs=after_specs + [pl.BlockSpec(memory_space=pltpu.HBM)],
        out_specs=pl.BlockSpec(memory_space=pltpu.HBM),
        out_shape=pltpu.HBM(array.shape, array.dtype),
        input_output_aliases={len(after): 0},
        cost_estimate=pl.CostEstimate(flops=0, bytes_accessed=0, transcendentals=0),
    )(*after, in_hbm(array))


def place(where, filled, arrived, after=()):
    after_specs, after = waits(after)
    mine, rows, width = arrived.shape

    def kernel(where_ref, arrived_ref, *refs):
        refs[-1][...] = arrived_ref[...]

    return pl.pallas_call(
        kernel,
        grid_spec=pltpu.PrefetchScalarGridSpec(
            num_scalar_prefetch=1,
            grid=(mine,),
            in_specs=[pl.BlockSpec((1, rows, width), lambda s, w: (s, 0, 0))]
            + after_specs
            + [pl.BlockSpec(memory_space=pltpu.HBM)],
            out_specs=pl.BlockSpec((1, rows, width), lambda s, w: ((1 - w[1]) * mine + s, 0, 0)),
        ),
        out_shape=pltpu.HBM(filled.shape, filled.dtype),
        input_output_aliases={2 + len(after): 0},
        **params(1, 2 * arrived.size * arrived.dtype.itemsize, 16 * 2**20),
    )(where, in_hbm(arrived), *after, in_hbm(filled))


def shards(
    hidden_in, segment_ids, adapter_pick, w_qkv, w_out, w_up, w_down, ln_gain, ln_bias,
    adapt_a, adapt_b, up_a, up_b, down_a, down_b, grad_out,
):
    dp = lax.axis_size("dp")
    t = lax.axis_index("tensor")
    block, ff_half = w_up.shape
    width = hidden_in.shape[2]
    half = width // 2
    ff = 2 * ff_half
    positions = hidden_in.shape[1]
    length = 2 * positions
    mine = hidden_in.shape[0] // 2
    rank = adapt_b.shape[2]
    adapters = adapt_b.shape[1]

    NEAR.clear()
    pick = lax.dynamic_slice_in_dim(adapter_pick, mine * t, mine, 0)
    where = jnp.stack([lax.axis_index("dp"), t]).astype(pick.dtype)
    meta = jnp.concatenate([pick, where])
    ordered = jnp.where(t == 0, adapter_pick, jnp.roll(adapter_pick, -mine))
    picks = jnp.repeat(ordered, rank).astype(BF)
    picks = jnp.broadcast_to(jnp.pad(picks, (0, 3 * half - picks.shape[0]))[None], (rank, 3 * half))
    segs = lax.dynamic_slice_in_dim(segment_ids, mine * t, mine, 0)
    seg_col = segs.reshape(mine, length, 1)
    seg_row = segs.reshape(mine, 1, length)

    sent_rows = mine * positions

    def send_half(value, after):
        flat = value.reshape(2 * sent_rows, width)
        spot = Spot(flat, lambda me, t: (1 - t) * sent_rows, sent_rows, 0, width)
        (out,) = arrange(where, [(sent_rows, width)], [(spot, 0, Spot(None, 0, sent_rows, 0, width))], after=after)
        return flat, out, swap(out)

    def join(flat, there, after):
        moves = []
        for s in range(mine):
            moves.append((
                Spot(flat, lambda me, t, s=s: (t * mine + s) * positions, positions, 0, width), 0,
                Spot(None, lambda me, t, s=s: s * length + t * positions, positions, 0, width),
            ))
            moves.append((
                Spot(there, s * positions, positions, 0, width), 0,
                Spot(None, lambda me, t, s=s: s * length + (1 - t) * positions, positions, 0, width),
            ))
        (out,) = arrange(where, [(mine * length, width)], moves, fresh=[there], after=after)
        return out.reshape(mine, length, width), out

    gather = (Gather if dp == 16 else GatherPlain)(w_qkv, w_out, w_up, w_down)
    gather.round1()
    def columns(first, count):
        return (gather.pieces, first, count, dp, block)

    qkv_w = columns(0, 3 * half)
    out_w = columns(3 * half, half)
    part = 2 * half
    up_parts = [columns(4 * half + p, part) for p in range(0, ff_half, part)]
    up_w = columns(4 * half, ff_half)
    down_w = columns(4 * half + ff_half, ff_half)

    a_t = jnp.swapaxes(adapt_a, 2, 3)
    ua_t = jnp.swapaxes(up_a, 1, 2)
    da_t = jnp.swapaxes(down_a, 1, 2)

    flat_x, gate, there_x = send_half(hidden_in, [gather.gate])
    flat_c, gate, there_c = send_half(grad_out, [gate])
    gate, met = gather.round2([meta, seg_col, seg_row, picks, gate])
    x, gate = join(flat_x, there_x, [gate])
    cotangent, gate = join(flat_c, there_c, [gate])
    _, met = gather.round3([met, gate])
    gate, _ = gather.round4([met])
    tokens = mine * length
    tiles = 2
    tile = length // tiles
    seq3 = lambda s, i, m: (s, 0, 0)
    row3 = lambda s, i, m: (s, i, 0)
    fixed2 = lambda s, i, m: (0, 0)
    picked3 = lambda s, i, m: (m[s], 0, 0)
    slots4 = lambda s, i, m: (0, m[s], 0, 0)
    last4 = lambda s, i, m: (3, m[s], 0, 0)
    full = lambda a: (a, (1, *a.shape[1:]), seq3)
    row = lambda a: (a, (1, tile, a.shape[2]), row3)
    across = lambda a: (a, (1, a.shape[1], tile), lambda s, i, m: (s, 0, i))
    whole = lambda a: (a, a.shape, fixed2)
    factor = lambda a: (a, (1, *a.shape[1:]), picked3)
    slots = lambda a: (a, (a.shape[0], 1, *a.shape[2:]), slots4)
    last = lambda a: (a, (1, 1, *a.shape[2:]), last4)
    rows_made = lambda dtype, cols: ((mine, length, cols), dtype, (1, tile, cols), row3)
    across_made = lambda rows: ((mine, rows, length), BF, (1, rows, tile), lambda s, i, m: (s, 0, i))
    def kept_made(dtype):
        block = (1, positions, width)
        return [
            ((2 * mine, positions, width), dtype, block, lambda s, i, m: (m[mine + 1] * mine + s, 0, 0)),
            ((mine, positions, width), dtype, block, seq3),
        ]

    sum_made = lambda rows, cols: ((mine, rows, cols), BF, (1, rows, cols), seq3)

    qkv, rank_qkv, whole_qkv = call(
        qkv_kernel, meta,
        [row(x), slots(a_t), slots(adapt_b)],
        [((mine, 3, length, width), BF, (1, 3, tile, width), lambda s, i, m: (s, 0, i, 0)),
         across_made(3 * rank)],
        6 * tokens * width * width,
        weights=[qkv_w],
        after=[gate],
        limit=28 * 2**20,
        tiles=tiles,
        saves=[(0, 3 * half, 0, None)],
    )
    gate, met = gather.round5([qkv])

    groups = width // GROUP

    def heads_of(slot, first, group=0):
        return pl.BlockSpec((1, 1, length, GROUP), lambda s, h: (s + first, slot, 0, h + group))

    def seg_specs(first):
        return [
            pl.BlockSpec((1, length, 1), lambda s, h: (s + first, 0, 0)),
            pl.BlockSpec((1, 1, length), lambda s, h: (s + first, 0, 0)),
        ]

    def lse_at(first, group=0):
        return pl.BlockSpec((1, 1, 8, length), lambda s, h: (s + first, h + group, 0, 0))

    def heads_at(first, group=0):
        return pl.BlockSpec((1, length, GROUP), lambda s, h: (s + first, 0, h + group))

    def attend(first, made, after):
        after_specs, after = waits(after)
        extra = len(made) + len(after)

        def body(q, k, v, sc, sr, *refs):
            attend_kernel(q, k, v, sc, sr, *refs[extra:])

        return pl.pallas_call(
            body,
            grid=(1, groups),
            in_specs=[heads_of(j, first) for j in range(3)]
            + seg_specs(first)
            + [pl.BlockSpec(memory_space=pltpu.HBM) for _ in made]
            + after_specs,
            out_specs=[heads_at(first), lse_at(first)],
            out_shape=[
                pltpu.HBM((mine, length, width), BF),
                pltpu.HBM((mine, groups, 8, length), F32),
            ],
            input_output_aliases={5 + i: i for i in range(len(made))},
            **params(16 * length * length * width, length * width * 8, 24 * 2**20),
        )(*[in_hbm(a) for a in [qkv, qkv, qkv, seg_col, seg_row, *made]], *after)

    attended = []
    for index in range(mine):
        attended = attend(index, attended, [] if index else [gate])
    attention, lse = attended
    gate, _ = gather.round6([lse, met])

    normed, inverse, middle_low, rank_out, whole_out = call(
        out_kernel, meta,
        [row(attention), row(x), last(a_t), last(adapt_b), whole(ln_gain), whole(ln_bias)],
        [rows_made(F32, width), rows_made(F32, 128), rows_made(BF, width), across_made(rank)],
        2 * tokens * width * width,
        scratch=[pltpu.VMEM((tile, width), F32)],
        weights=[out_w],
        limit=28 * 2**20,
        after=[gate],
        tiles=tiles,
        saves=[(0, half, 0, None)],
    )

    gate = rank_out
    blocks = ff_half // part
    made_up, whole_up = [], None
    for index, weight in enumerate(up_parts):
        up_cols = [
            (up_b, (1, rank, part), lambda s, i, m, at=h * blocks + index: (m[s], 0, at)) for h in range(2)
        ]
        units_made = (
            (mine, 2, length, ff_half), BF, (1, 2, tile, part), lambda s, i, m, index=index: (s, 0, i, index)
        )
        made = call(
            up_kernel, meta,
            [row(middle_low), factor(ua_t), *up_cols],
            [units_made, units_made, across_made(rank)],
            4 * tokens * width * part * 2,
            weights=[weight],
            limit=36 * 2**20,
            after=[gate],
            tiles=tiles,
            filled=made_up,
            saves=[(0, part, 0, None)] if index == 0 else [],
        )
        *made_up, rank_up = made[:3]
        gate = rank_up
        if index == 0:
            whole_up = made[3]
            gate, _ = gather.last([rank_up])
    units = lambda a: (a, (1, 2, tile, ff_half), lambda s, i, m: (s, 0, i, 0))
    act, slope = made_up

    layer_out, layer_sent, grad_first, grad_att, g_down_a, g_down_b, g_up_a, g_up_b, g_out_a, g_out_b = call(
        middle_kernel, meta,
        [units(act), units(slope), row(normed), row(inverse), row(cotangent), row(middle_low), row(attention),
         across(rank_up), across(rank_out), factor(da_t), factor(down_b), factor(ua_t), factor(up_b),
         last(a_t), last(adapt_b), whole(ln_gain), whole(ln_bias)],
        [*kept_made(BF), rows_made(F32, width), rows_made(BF, width),
         sum_made(rank, ff), sum_made(rank, width), sum_made(rank, width), sum_made(rank, ff),
         sum_made(rank, width), sum_made(rank, width)],
        tokens * width * (6 * ff + 2 * width),
        scratch=[pltpu.VMEM((tile, width), F32), pltpu.VMEM((tile, width), F32), pltpu.VMEM((tile, width), BF),
                 pltpu.VMEM((tile, ff), BF), pltpu.VMEM((tile, width), BF),
                 pltpu.VMEM((rank, ff), F32), pltpu.VMEM((rank, width), F32),
                 pltpu.VMEM((rank, width), F32), pltpu.VMEM((rank, ff), F32),
                 pltpu.VMEM((rank, width), F32), pltpu.VMEM((rank, width), F32)],
        weights=[down_w, up_parts[1]],
        tiles=tiles,
        held=[whole_up, whole_out],
        limit=50 * 2**20,
    )

    layer_there = swap(layer_sent)
    flat = lambda g: g.reshape(mine * rank, g.shape[-1])
    seqs = [g_down_a, g_down_b, g_up_a, g_up_b, g_out_a, g_out_b]
    fast = dp == 16
    gate = None
    if fast:
        first_sum = GradientSum(where, [flat(g) for g in seqs], mine, rank, adapters, picks)
        gate = first_sum.cores()

    halves = 2
    span = groups // halves

    def attend_back(first, group, made, after):
        after_specs, after = waits(after)
        extra = len(made) + len(after)

        def body(q, k, v, sc, sr, l, o, do, *refs):
            attend_back_kernel(q, k, v, sc, sr, l, o, do, *refs[extra:])

        args = [qkv, qkv, qkv, seg_col, seg_row, lse, attention, grad_att, *made]
        return pl.pallas_call(
            body,
            grid=(1, span),
            in_specs=[heads_of(j, first, group) for j in range(3)]
            + seg_specs(first)
            + [lse_at(first, group), heads_at(first, group), heads_at(first, group)]
            + [pl.BlockSpec(memory_space=pltpu.HBM) for _ in made]
            + after_specs,
            out_specs=[heads_at(first, group)] * 3,
            out_shape=[pltpu.HBM((mine, length, width), BF)] * 3,
            input_output_aliases={8 + i: i for i in range(len(made))},
            **params(40 * length * length * width // halves, length * width * 16, 32 * 2**20),
        )(*[in_hbm(a) for a in args], *after)

    grads_qkv = []
    between = iter([first_sum.plane, first_sum.fold, first_sum.depth, first_sum.back] if fast else [])
    for index in range(mine):
        for group in range(0, groups, span):
            grads_qkv = attend_back(index, group, grads_qkv, [gate])
            gate = None
            phase = next(between, None)
            if phase is not None and (index, group) != (mine - 1, groups - span):
                gate = phase([grads_qkv[0]])
    gate = first_sum.back([grads_qkv[0]]) if fast else None

    grad_rank, *later = call(
        rank_back_kernel, meta,
        [full(g) for g in grads_qkv] + [full(x), full(rank_qkv), slots(adapt_b)],
        [sum_made(3 * rank, length)] + [sum_made(rank, width)] * 6,
        18 * tokens * width * rank,
        after=[gate],
        limit=32 * 2**20,
    )
    gate = grad_rank
    if fast:
        second_sum = GradientSum(where, [flat(g) for g in later], mine, rank, adapters, picks)
        gate = second_sum.cores([gate])
        gate = first_sum.spread([gate])
        gate = second_sum.plane([gate])

    grad_in, grad_sent = call(
        qkv_back_kernel, meta,
        [row(g) for g in grads_qkv] + [across(grad_rank), row(grad_first), slots(a_t)],
        kept_made(F32),
        6 * tokens * width * width,
        held=[whole_qkv],
        after=[gate],
        limit=40 * 2**20,
        tiles=tiles,
    )
    turned = lambda v: jnp.swapaxes(v, -1, -2)
    if fast:
        gate = second_sum.fold([grad_in])
        gate = first_sum.give([gate])
        layer_out = place(where, layer_out, layer_there, [gate])
        gate = second_sum.depth([layer_out])
        there = swap(hold(grad_sent, [gate]))
        done1 = finish(where, [first_sum], [[(0, 0)], [(0, 1)], [(0, 2)], [(0, 3)]], [gate])
        gate = second_sum.back([done1[0]])
        grad_in = place(where, grad_in, there, [gate])
        gate = second_sum.spread([grad_in])
        second_sum.give([gate])
        all_a, all_b = finish(
            where, [second_sum, first_sum],
            [[(0, 0), (0, 1), (0, 2), (1, 4)], [(0, 3), (0, 4), (0, 5), (1, 5)]],
        )
        shaped = lambda v: v.reshape(-1, adapters, rank, v.shape[1])
        da, db, ua, ub = (shaped(v)[0] for v in done1)
        return (layer_out, grad_in, turned(shaped(all_a)), shaped(all_b), turned(ua), ub, turned(da), db)

    layer_out = place(where, layer_out, layer_there)
    grad_in = place(where, grad_in, swap(grad_sent))
    onehot = (pick[:, None] == jnp.arange(adapters)[None, :]).astype(F32)

    def fold(per_sequence):
        total = onehot[0][:, None, None] * per_sequence[0][None].astype(F32)
        for index in range(1, mine):
            total += onehot[index][:, None, None] * per_sequence[index][None].astype(F32)
        return total

    sums = lax.psum(
        tuple(fold(g) for g in [*later[:3], g_out_a, *later[3:], g_out_b, g_up_a, g_up_b, g_down_a, g_down_b]),
        ("dp", "tensor"),
    )
    return (
        layer_out,
        grad_in,
        turned(jnp.stack(sums[:4])),
        jnp.stack(sums[4:8]),
        turned(sums[8]),
        sums[9],
        turned(sums[10]),
        sums[11],
    )


def solution(mesh):
    placed = (
        P("dp", "tensor", None),
        P("dp", None),
        P("dp"),
        P(None, "dp", "tensor"),
        P("tensor", "dp"),
        P("dp", "tensor"),
        P("tensor", "dp"),
        P(),
        P(),
        P(),
        P(),
        P(),
        P(),
        P(),
        P(),
        P("dp", "tensor", None),
    )
    return jax.shard_map(
        shards,
        mesh=mesh,
        in_specs=placed,
        out_specs=(P("dp", "tensor", None), P("dp", "tensor", None), P(), P(), P(), P(), P(), P()),
        check_vma=False,
    )
```

```python
import functools

import jax
import jax.numpy as jnp
from jax import lax
from jax.experimental import pallas as pl
from jax.experimental.pallas import tpu as pltpu
from jax.sharding import PartitionSpec as P

HEAD_DIM = 64
BF = jnp.bfloat16
F32 = jnp.float32
LOG2E = 1.4426950408889634
VMEM = 60 * 2**20


def nn(a, b):
    return lax.dot_general(a, b, (((1,), (0,)), ((), ())), preferred_element_type=F32)


def nt(a, b):
    return lax.dot_general(a, b, (((1,), (1,)), ((), ())), preferred_element_type=F32)


def tn(a, b):
    return lax.dot_general(a, b, (((0,), (0,)), ((), ())), preferred_element_type=F32)


def params(flops, nbytes, limit=VMEM):
    return dict(
        compiler_params=pltpu.CompilerParams(vmem_limit_bytes=limit),
        cost_estimate=pl.CostEstimate(flops=flops, bytes_accessed=nbytes, transcendentals=0),
    )


class Piece:
    def __init__(self, col, width, rel, row, count, array, at, other):
        self.col, self.width, self.rel, self.row = col, width, rel, row
        self.count, self.array, self.at, self.other = count, array, at, other


def first_tile():
    return jnp.logical_and(pl.program_id(0) == 0, pl.program_id(1) == 0)


class Loader:
    def __init__(self, plan, refs, scratch, sems, me, t, dp):
        self.plan, self.refs, self.scratch, self.sems = plan, refs, scratch, sems
        self.me, self.t, self.dp = me, t, dp
        self.saved = None
        self.width = scratch.shape[1] // 2
        self.block = scratch.shape[0] // dp

    def start(self):
        def copy(source, block, row, count, into, width, other):
            rows = pl.ds(pl.multiple_of(block * self.block + row, 16), count)
            cols = pl.ds(pl.multiple_of((self.t ^ other) * self.width + into, 128), width)
            pltpu.make_async_copy(source, self.scratch.at[rows, cols], self.sems.at[other]).start()

        for slot, at, count, col, width, other, rel, row, into in self.plan:
            cols = pl.ds(col, width)
            if rel is None:
                for block in range(self.dp):
                    source = self.refs[slot].at[block, self.t ^ other, :, cols]
                    copy(source, block, 0, self.block, into, width, other)
            else:
                copy(self.refs[slot].at[pl.ds(at, count), cols], self.me ^ rel, row, count, into, width, other)

    def wait(self, other):
        cols = pl.ds(pl.multiple_of((self.t ^ other) * self.width, 128), self.width)
        whole = self.scratch.at[:, cols]
        pltpu.make_async_copy(whole, whole, self.sems.at[other]).wait()

    def first_step(self):
        pl.when(first_tile())(self.start)

    def first_wait(self, other):
        pl.when(first_tile())(lambda: self.wait(other))

    def first_wait_all(self):
        @pl.when(first_tile())
        def _():
            self.wait(0)
            self.wait(1)
            if self.saved is not None:
                for copy in self.save_copies():
                    copy.start()

    def save_copies(self):
        ref, first, sems = self.saved
        half = ref.shape[1] // 2
        return [
            pltpu.make_async_copy(
                self.scratch.at[:, pl.ds(h * self.width, self.width)],
                ref.at[:, pl.ds(h * half + first, self.width)],
                sems.at[h],
            )
            for h in range(2)
        ]

    def cols(self, half, lo, width):
        at = half * self.width + lo
        return self.scratch[:, pl.ds(at if isinstance(at, int) else pl.multiple_of(at, 128), width)]


class Held:
    def __init__(self, ref):
        self.scratch, self.width = ref, ref.shape[1] // 2

    cols = Loader.cols


def weight_plan(pieces, first, width):
    arrays, plan = [], []
    for p in pieces:
        lo, hi = max(p.col, first), min(p.col + p.width, first + width)
        if lo >= hi:
            continue
        slot = next((i for i, a in enumerate(arrays) if a is p.array), None)
        if slot is None:
            slot = len(arrays)
            arrays.append(p.array)
        plan.append((slot, p.at, p.count, lo - p.col, hi - lo, p.other, p.rel, p.row, lo - first))
    return arrays, plan


def qkv_kernel(meta, ins, outs, weights, scratch):
    x_ref, a_ref, b_ref = ins
    qkv_ref, rank_ref = outs
    (w,) = weights
    w.first_step()
    w.first_wait_all()
    x = x_ref[0]
    slots, rank_size = rank_ref.shape[1] // a_ref.shape[2], a_ref.shape[2]
    factors = a_ref[0:slots, 0].reshape(slots * rank_size, x.shape[1])
    rank = nt(x, factors)
    rank_ref[0] = rank.T.astype(BF)
    rank = rank.astype(BF)
    width = w.width // slots
    for half in range(2):
        cols = slice(half * width, (half + 1) * width)
        for slot in range(slots):
            mine = rank[:, slot * rank_size : (slot + 1) * rank_size]
            full = nn(x, w.cols(half, slot * width, width)) + nn(mine, b_ref[slot, 0, :, cols])
            qkv_ref[0, slot, :, cols] = full.astype(BF)


SCALE = HEAD_DIM**-0.5
SCALE2 = SCALE * LOG2E
GROUP = 4 * HEAD_DIM


def one_head(lane, head, value):
    return jnp.where(lane // HEAD_DIM == head, value, jnp.zeros((), value.dtype))


def attend_kernel(q_ref, k_ref, v_ref, segc_ref, segr_ref, out_ref, lse_ref):
    q, k, v = q_ref[0, 0], k_ref[0, 0], v_ref[0, 0]
    length, lanes = q.shape
    heads = lanes // HEAD_DIM
    lane = lax.broadcasted_iota(jnp.int32, (1, lanes), 1)
    same = segc_ref[0] == segr_ref[0]
    v_t = v.T

    def score(head):
        return nt(one_head(lane, head, k), q)

    mixed = []
    scores = score(0)
    for head in range(heads):
        following = score(head + 1) if head + 1 < heads else None
        masked = jnp.where(same, scores, F32(-1000000000.0 / SCALE))
        peak = jnp.max(masked, axis=0, keepdims=True) * SCALE2
        weights = jnp.exp2(masked * SCALE2 - peak)
        mass = jnp.sum(weights, axis=0, keepdims=True)
        rows = slice(head * HEAD_DIM, (head + 1) * HEAD_DIM)
        mixed.append(nn(v_t[rows, :], weights.astype(BF)) * (1.0 / mass))
        lse_ref[0, 0, head : head + 1, :] = peak + jnp.log2(mass)
        scores = following
    out_ref[0] = jnp.concatenate(mixed, axis=0).astype(BF).T
    lse_ref[0, 0, heads:, :] = jnp.zeros((lse_ref.shape[2] - heads, length), F32)


def attend_back_kernel(
    q_ref, k_ref, v_ref, segc_ref, segr_ref, lse_ref, o_ref, do_ref, gq_ref, gk_ref, gv_ref
):
    q, k, v, do = q_ref[0, 0], k_ref[0, 0], v_ref[0, 0], do_ref[0]
    lanes = q.shape[1]
    lane = lax.broadcasted_iota(jnp.int32, (1, lanes), 1)
    product = do.astype(F32) * o_ref[0].astype(F32)
    high = product.astype(BF)
    low = (product - high.astype(F32)).astype(BF)
    picker = (
        lax.broadcasted_iota(jnp.int32, (8, lanes), 0)
        == lax.broadcasted_iota(jnp.int32, (8, lanes), 1) // HEAD_DIM
    ).astype(BF)
    inner = nt(picker, high) + nt(picker, low)
    same = segc_ref[0] == segr_ref[0]
    grad_q = grad_k = grad_v = None
    for head in range(lanes // HEAD_DIM):
        k_mine = one_head(lane, head, k)
        masked = jnp.where(same, nt(k_mine, q), F32(-1000000000.0 / SCALE))
        probs = jnp.exp2(masked * SCALE2 - lse_ref[0, 0, head : head + 1, :])
        grad_probs = nt(one_head(lane, head, v), do)
        grad_scores = (probs * (grad_probs - inner[head : head + 1, :])).astype(BF)
        part_v = nn(probs.astype(BF), one_head(lane, head, do))
        part_k = nn(grad_scores, one_head(lane, head, q))
        part_q = tn(grad_scores, k_mine)
        grad_v = part_v if head == 0 else grad_v + part_v
        grad_k = part_k if head == 0 else grad_k + part_k
        grad_q = part_q if head == 0 else grad_q + part_q
    gq_ref[0] = (grad_q * SCALE).astype(BF)
    gk_ref[0] = (grad_k * SCALE).astype(BF)
    gv_ref[0] = grad_v.astype(BF)


def norm_parts(values):
    mean = jnp.mean(values, axis=-1, keepdims=True)
    centred = values - mean
    inverse = lax.rsqrt(jnp.mean(centred * centred, axis=-1, keepdims=True) + 1e-06)
    return centred * inverse, inverse


def norm_back(scaled, normed, inverse):
    mean_grad = jnp.mean(scaled, axis=-1, keepdims=True)
    mean_proj = jnp.mean(scaled * normed, axis=-1, keepdims=True)
    return (scaled - mean_grad - normed * mean_proj) * inverse


ROWS = 64


def by_rows(count, step):
    for row in range(0, count, ROWS):
        step(slice(row, row + ROWS))


def out_kernel(meta, ins, outs, weights, scratch):
    att_ref, x_ref, a_ref, b_ref, gain_ref, bias_ref = ins
    normed_ref, inverse_ref, low_ref, rank_ref = outs
    (w,) = weights
    (v_scr,) = scratch
    w.first_step()
    w.first_wait_all()
    att = att_ref[0]
    rank = nt(att, a_ref[0, 0])
    rank_ref[0] = rank.T.astype(BF)
    rank = rank.astype(BF)
    width = w.width
    v_scr[...] = (
        nt(att[:, :width], w.cols(0, 0, width))
        + nt(att[:, width:], w.cols(1, 0, width))
        + nn(rank, b_ref[0, 0])
    )

    def step(rows):
        normed, inverse = norm_parts(v_scr[rows, :] + x_ref[0, rows, :].astype(F32))
        normed_ref[0, rows, :] = normed
        inverse_ref[0, rows, :] = jnp.broadcast_to(inverse, (ROWS, 128))
        low_ref[0, rows, :] = (normed * gain_ref[0:1, :] + bias_ref[0:1, :]).astype(BF)

    by_rows(v_scr.shape[0], step)


def gelu_parts(x):
    phi = 0.5 + 0.5 * lax.erf(x * 0.7071067811865476)
    density = jnp.exp2((-0.5 * LOG2E) * x * x)
    return x * phi, phi + x * (density * 0.3989422804014327)


CHUNK = 512


def up_kernel(meta, ins, outs, weights, scratch):
    m_ref, a_ref = ins[:2]
    b_refs = ins[2:]
    act_ref, slope_ref, rank_ref = outs
    (w,) = weights
    w.first_step()
    w.first_wait_all()
    m = m_ref[0]
    rank = nt(m, a_ref[0])
    rank_ref[0] = rank.T.astype(BF)
    rank = rank.astype(BF)
    width = w.width
    for half, b_ref in enumerate(b_refs):
        for lo in range(0, width, CHUNK):
            cols = slice(lo, lo + CHUNK)
            units = nn(m, w.cols(half, lo, CHUNK)) + nn(rank, b_ref[0, :, cols])
            act, slope = gelu_parts(units)
            act_ref[0, half, :, cols] = act.astype(BF)
            slope_ref[0, half, :, cols] = slope.astype(BF)


def add_up(total, part, fresh):
    total[...] = jnp.where(fresh, part, total[...] + part)


def by_chunks(ref, parts):
    at = 0
    for chunk in range(8):
        for part in parts:
            width = part.shape[1] // 8
            ref[0, :, at : at + width] = part[:, chunk * width : (chunk + 1) * width].astype(BF)
            at += width


def keep_or_send(t, value, kept_ref, sent_ref):
    @pl.when(pl.program_id(1) == t)
    def _():
        kept_ref[0] = value

    @pl.when(pl.program_id(1) != t)
    def _():
        sent_ref[0] = value


def middle_kernel(meta, ins, outs, weights, scratch):
    (act_ref, slope_ref, n1_ref, r1_ref, go_ref, m_ref, att_ref, ranku_ref, ranko_ref,
     da_ref, db_ref, ua_ref, ub_ref, oa_ref, ob_ref, gain_ref, bias_ref) = ins
    kept_ref, sent_ref, first_ref, gatt_ref = outs[:4]
    down, late_up, early_up, out = weights
    v_scr, second_scr, gf_scr, gh_scr, out_scr = scratch[:5]
    sums = scratch[5:]
    sum_da, sum_db, sum_ua, sum_ub, sum_oa, sum_ob = sums
    tile = pl.program_id(1)
    fresh = tile == 0
    for loader in (down, late_up):
        loader.first_step()
    for loader in (down, late_up):
        loader.first_wait_all()
    width = down.width
    part = early_up.width
    halves = [slice(0, width), slice(width, 2 * width)]

    rank = sum(nt(act_ref[0, h], da_ref[0, :, halves[h]]) for h in range(2)).astype(BF)
    model = v_scr.shape[1]
    for at in range(0, model, CHUNK):
        cols = slice(at, at + CHUNK)
        v_scr[:, cols] = (
            nt(act_ref[0, 0], down.scratch[cols, halves[0]])
            + nt(act_ref[0, 1], down.scratch[cols, halves[1]])
            + nn(rank, db_ref[0, :, cols])
        )

    def second_norm(rows):
        middle = n1_ref[0, rows, :] * gain_ref[0:1, :] + bias_ref[0:1, :]
        normed, inverse = norm_parts(v_scr[rows, :] + middle)
        out_scr[rows, :] = (normed * gain_ref[1:2, :] + bias_ref[1:2, :]).astype(BF)
        second = norm_back(go_ref[0, rows, :].astype(F32) * gain_ref[1:2, :], normed, inverse)
        second_scr[rows, :] = second
        gf_scr[rows, :] = second.astype(BF)

    by_rows(v_scr.shape[0], second_norm)
    grad_feed = gf_scr[...]
    add_up(sum_db, tn(rank, grad_feed), fresh)
    grad_rank = nt(grad_feed, db_ref[0]).astype(BF)
    chunk = 2 * CHUNK
    for half in range(2):
        for lo in range(0, width, chunk):
            cols = slice(half * width + lo, half * width + lo + chunk)
            grad_act = nn(grad_feed, down.cols(half, lo, chunk)) + nn(grad_rank, da_ref[0, :, cols])
            local = slice(lo, lo + chunk)
            gh_scr[:, cols] = (grad_act * slope_ref[0, half, :, local].astype(F32)).astype(BF)
    grad_rank_down = grad_rank

    grad_rank = nt(gh_scr[...], ub_ref[0]).astype(BF)
    for at in range(0, model, CHUNK):
        cols = slice(at, at + CHUNK)
        total = nn(grad_rank, ua_ref[0, :, cols])
        for half in range(2):
            lo = half * width
            local = slice(half * part, (half + 1) * part)
            total = total + nt(gh_scr[:, lo : lo + part], early_up.scratch[cols, local])
            total = total + nt(gh_scr[:, lo + part : lo + width], late_up.scratch[cols, local])
        v_scr[:, cols] = total
    add_up(sum_ua, tn(grad_rank, m_ref[0]), fresh)
    add_up(sum_ub, nn(ranku_ref[0], gh_scr[...]), fresh)
    for half in range(2):
        add_up(sum_da.at[:, halves[half]], tn(grad_rank_down, act_ref[0, half]), fresh)

    def first_norm(rows):
        scaled = (second_scr[rows, :] + v_scr[rows, :]) * gain_ref[0:1, :]
        first = norm_back(scaled, n1_ref[0, rows, :], r1_ref[0, rows, 0:1])
        first_ref[0, rows, :] = first
        gf_scr[rows, :] = first.astype(BF)

    by_rows(v_scr.shape[0], first_norm)
    grad_branch = gf_scr[...]
    grad_rank = nt(grad_branch, ob_ref[0, 0]).astype(BF)
    add_up(sum_oa, tn(grad_rank, att_ref[0]), fresh)
    add_up(sum_ob, nn(ranko_ref[0], grad_branch), fresh)
    owidth = out.width
    for half in range(2):
        cols = slice(half * owidth, (half + 1) * owidth)
        full = nn(grad_branch, out.cols(half, 0, owidth)) + nn(grad_rank, oa_ref[0, 0, :, cols])
        gatt_ref[0, :, cols] = full.astype(BF)

    keep_or_send(down.t, out_scr[...], kept_ref, sent_ref)

    @pl.when(tile == pl.num_programs(1) - 1)
    def _():
        by_chunks(outs[4], sums)


def rank_back_kernel(meta, ins, outs, weights, scratch):
    gq_ref, gk_ref, gv_ref, x_ref, rank_ref, b_ref = ins
    gr_ref, sum_ref = outs
    size = b_ref.shape[2]
    ranks, parts_b = [], []
    for slot, ref in enumerate((gq_ref, gk_ref, gv_ref)):
        grad = ref[0]
        ranks.append(nt(b_ref[slot, 0], grad))
        parts_b.append(nn(rank_ref[0, slot * size : (slot + 1) * size, :], grad))
    stacked = jnp.concatenate(ranks, axis=0).astype(BF)
    gr_ref[0] = stacked
    products = nn(stacked, x_ref[0])
    parts_a = [products[slot * size : (slot + 1) * size] for slot in range(3)]
    by_chunks(sum_ref, parts_a + parts_b)


def qkv_back_kernel(meta, ins, outs, weights, scratch):
    gq_ref, gk_ref, gv_ref, gr_ref, first_ref, a_ref = ins
    kept_ref, sent_ref = outs
    (w,) = weights
    slots = 3
    width = w.width // slots
    size = a_ref.shape[2]
    total = first_ref[0] + tn(
        gr_ref[0], a_ref[0:slots, 0].reshape(slots * size, kept_ref.shape[2])
    )
    for half in range(2):
        cols = slice(half * width, (half + 1) * width)
        for slot, ref in enumerate((gq_ref, gk_ref, gv_ref)):
            total += nt(ref[0, :, cols], w.cols(half, slot * width, width))
    keep_or_send(meta[meta.shape[0] - 1], total, kept_ref, sent_ref)


NEAR = []


def made_near(arrays):
    NEAR.extend(arrays)
    return arrays


def waits(arrays):
    arrays = [a for a in arrays if a is not None]
    near = [any(a is n for n in NEAR) for a in arrays]
    specs = [pl.BlockSpec(memory_space=pl.ANY if n else pltpu.HBM) for n in near]
    return specs, [a if n else in_hbm(a) for a, n in zip(arrays, near)]


def far(arrays):
    return [pl.BlockSpec(memory_space=pltpu.HBM) for _ in arrays], [in_hbm(a) for a in arrays]


def call(kernel, meta, ins, outs, flops, scratch=(), weights=(), limit=VMEM, after=(), tiles=1, filled=(),
         saves=(), held=(), near=True):
    plans = [weight_plan(pieces, first, width) for pieces, first, width, _, _ in weights]
    n_in, n_out, n_w = len(ins), len(outs), len(weights)
    counts = [len(arrays) for arrays, _ in plans]
    steps = meta.shape[0] - 2
    after_specs, after = waits(after)
    n_after = len(after)

    def body(meta_ref, *refs):
        refs = list(refs)
        take = lambda n: [refs.pop(0) for _ in range(n)]
        in_refs = take(n_in)
        w_refs = [take(n) for n in counts]
        take(n_after + len(filled))
        held_refs = take(len(held))
        take(len(started))
        out_refs = take(n_out)
        save_refs = take(len(saves))
        w_scr = take(n_w)
        w_sem = take(n_w)
        save_sems = take(len(saves))
        me, t = meta_ref[steps], meta_ref[steps + 1]
        loaders = [
            Loader(plan, r, s, m, me, t, w[3])
            for (_, plan), r, s, m, w in zip(plans, w_refs, w_scr, w_sem, weights)
        ]
        for (number, _, first, _), ref, sem in zip(saves, save_refs, save_sems):
            loaders[number].saved = (ref, first, sem)
        kernel(meta_ref, in_refs, out_refs, loaders + [Held(ref) for ref in held_refs], refs)
        for number, *_ in saves:

            @pl.when(jnp.logical_and(pl.program_id(0) == steps - 1, pl.program_id(1) == tiles - 1))
            def _(loader=loaders[number]):
                for copy in loader.save_copies():
                    copy.wait()

    started = [array for *_, array in saves if array is not None]
    w_arrays = [a for arrays, _ in plans for a in arrays]
    first_alias = 1 + n_in + len(w_arrays) + n_after
    w_specs, w_arrays = waits(w_arrays) if near else far(w_arrays)
    nbytes = sum(a.size * a.dtype.itemsize for a, _, _ in ins)
    nbytes += sum(2 * dp * rows * width * 2 for _, _, width, dp, rows in weights)
    for shape, dtype, _, _ in outs:
        size = jnp.dtype(dtype).itemsize
        for extent in shape:
            size *= extent
        nbytes += size
    return pl.pallas_call(
        body,
        grid_spec=pltpu.PrefetchScalarGridSpec(
            num_scalar_prefetch=1,
            grid=(steps, tiles),
            in_specs=[pl.BlockSpec(block, index) for _, block, index in ins]
            + w_specs
            + after_specs
            + [pl.BlockSpec(memory_space=pltpu.HBM) for _ in filled]
            + [pl.BlockSpec(memory_space=pltpu.VMEM) for _ in held]
            + [pl.BlockSpec(memory_space=pltpu.HBM) for _ in started],
            out_specs=[pl.BlockSpec(block, index) for _, _, block, index in outs]
            + [pl.BlockSpec(memory_space=pltpu.HBM) for _ in saves],
            scratch_shapes=[pltpu.VMEM((dp * rows, 2 * width), BF) for _, _, width, dp, rows in weights]
            + [pltpu.SemaphoreType.DMA((2,)) for _ in [*weights, *saves]]
            + list(scratch),
        ),
        out_shape=[pltpu.HBM(shape, dtype) for shape, dtype, _, _ in outs]
        + [pltpu.HBM((weights[n][3] * weights[n][4], 2 * half), BF) for n, half, _, _ in saves],
        input_output_aliases={first_alias + i: i for i in range(len(filled))}
        | {first_alias + len(filled) + len(held) + i: n_out + i for i in range(len(started))},
        **params(flops, nbytes, limit),
    )(
        meta, *[in_hbm(a) for a, _, _ in ins], *w_arrays, *after, *[in_hbm(a) for a in filled],
        *[pltpu.with_memory_space_constraint(a, pltpu.VMEM) for a in held], *[in_hbm(a) for a in started],
    )


def pack(outs, fresh=(), after=()):
    after_specs, after = waits(after)
    arrays, plan, heights, widths = [], [], [], []

    def slot(array):
        for index, known in enumerate(arrays):
            if known is array:
                return index
        arrays.append(array)
        return len(arrays) - 1

    for index, parts in enumerate(outs):
        row = 0
        for part in parts:
            array, at, count, col, cols, into, advance = part
            plan.append((slot(array), at, count, col, cols, index, row, into))
            if advance:
                row += count
        heights.append(row)
        widths.append(max(part[4] + part[5] for part in parts))
    used, n_in = len(arrays), len(arrays) + len(after)
    near = [any(a is f for f in fresh) for a in arrays]

    def kernel(*refs):
        ins, results, sems = refs[:n_in], refs[n_in:-1], refs[-1]
        copies = []
        for number, (a, at, count, col, cols, o, row, into) in enumerate(plan):
            source = ins[a].at[pl.ds(at, count), pl.ds(col, cols)]
            target = results[o].at[pl.ds(row, count), pl.ds(into, cols)]
            if not near[a]:
                copy = pltpu.make_async_copy(source, target, sems.at[number])
                copy.start()
                copies.append(copy)
        for a, at, count, col, cols, o, row, into in plan:
            if near[a]:
                results[o][pl.ds(row, count), pl.ds(into, cols)] = ins[a][pl.ds(at, count), pl.ds(col, cols)]
        for copy in copies:
            copy.wait()

    spaces = [pltpu.VMEM if n else pltpu.HBM for n in near]
    return made_near(pl.pallas_call(
        kernel,
        in_specs=[pl.BlockSpec(memory_space=space) for space in spaces] + after_specs,
        out_specs=[pl.BlockSpec(memory_space=pltpu.VMEM)] * len(outs),
        out_shape=[pltpu.VMEM(shape, BF) for shape in zip(heights, widths)],
        scratch_shapes=[pltpu.SemaphoreType.DMA((len(plan),))],
        compiler_params=pltpu.CompilerParams(vmem_limit_bytes=8 * 2**20),
        cost_estimate=pl.CostEstimate(
            flops=0, bytes_accessed=sum(h * w * 4 for h, w in zip(heights, widths)), transcendentals=0
        ),
    )(*[pltpu.with_memory_space_constraint(a, space) for a, space in zip(arrays, spaces)], *after))


def in_hbm(array):
    return pltpu.with_memory_space_constraint(array, pltpu.HBM)


X, Y, Z1, Z2, Z3 = 1, 2, 4, 8, 12
ZS = (Z1, Z2, Z3)


def hop(array, bits):
    return lax.ppermute(array, "dp", [(i, i ^ bits) for i in range(lax.axis_size("dp"))])


def swap(array):
    return lax.ppermute(array, "tensor", [(0, 1), (1, 0)])


class Gather:
    def __init__(self, w_qkv, w_out, w_up, w_down):
        self.n = n = w_up.shape[0]
        self.h = n // 2
        self.pieces = []
        o, u = w_qkv.shape[2], w_up.shape[1]
        self.width = 3 * o
        flat = w_qkv.reshape(3 * n, o)
        wo, wd = w_out.T, w_down.T
        queries = [(flat, slot * n, n, 0, o, slot * o, slot == 2) for slot in range(3)]
        rest = [
            (wo, 0, n, 0, o, 0, False), (w_up, 0, n, 0, 2 * o, o, True),
            (w_up, 0, n, 2 * o, u - 2 * o, 0, False), (wd, 0, n, 0, o, 2 * o, True),
            (wd, 0, n, o, 3 * o, 0, True),
        ]
        self.own, self.q = pack([queries + rest, queries])
        self.gate = self.q
        self.e, self.f, self.g = (self.cut(p) for p in (1, 2, 3))

    def cut(self, piece):
        return lax.slice_in_dim(self.own, piece * self.n, (piece + 1) * self.n, axis=0)

    def note(self, array, items, other=0):
        at = 0
        for piece, rel, row, count in items:
            self.pieces.append(Piece(piece * self.width, self.width, rel, row, count, array, at, other))
            at += count

    def part(self, array, at, count):
        return (array, at, count, 0, self.width, 0, True)

    def full(self, piece, *rels):
        return [(piece, rel, 0, self.n) for rel in rels]

    def upper(self, piece, *rels):
        return [(piece, rel, self.h, self.h) for rel in rels]

    def lower(self, piece, *rels):
        return [(piece, rel, 0, self.h) for rel in rels]

    def exchange(self, arrays, after=()):
        fresh = [a for a, _ in arrays if a is not self.own]
        (packed,) = pack([[self.part(a, 0, a.shape[0]) for a, _ in arrays]], fresh=fresh, after=after)
        (other,) = made_near([swap(packed)])
        self.note(other, [item for _, items in arrays for item in items], 1)
        return packed, other

    def keep(self, got):
        for array, items in got:
            self.note(array, items)
        return got

    def round1(self):
        self.zq = [hop(self.q, k) for k in ZS]
        self.x1, self.y1 = hop(self.own, X), hop(self.own, Y)
        every = range(4)
        got = [(self.own, [i for p in every for i in self.full(p, 0)])]
        got += [(self.x1, [i for p in every for i in self.full(p, X)])]
        got += [(self.y1, [i for p in every for i in self.full(p, Y)])]
        got += [(z, self.full(0, k)) for z, k in zip(self.zq, ZS)]
        self.got1 = self.keep(got)

    def round2(self, after):
        n, h, part = self.n, self.h, self.part
        along = [part(z, 0, n) for z in self.zq]
        xin, yin, e = pack(
            [along + [part(self.y1, h, h)], along + [part(self.x1, 0, h)], [part(self.own, n, n)]],
            fresh=[*self.zq, self.x1, self.y1],
            after=after,
        )
        x, y, self.ze2 = hop(xin, X), hop(yin, Y), hop(e, Z2)
        self.x, self.y = x, y
        self.got2 = self.keep([
            (x, self.full(0, *(X | k for k in ZS)) + self.upper(0, X | Y)),
            (y, self.full(0, *(Y | k for k in ZS)) + self.lower(0, X | Y)),
            (self.ze2, self.full(1, Z2)),
        ])
        return self.exchange(self.got1, [xin])

    def round3(self, after):
        n, h, part = self.n, self.h, self.part
        xin, yin, e, f = pack(
            [
                [part(self.y, i * n + h, h) for i in range(3)] + [part(self.y1, p * n + h, h) for p in (1, 2)],
                [part(self.x, i * n, h) for i in range(3)] + [part(self.x1, p * n, h) for p in (1, 2)],
                [part(self.own, n, n), part(self.ze2, 0, n)],
                [part(self.own, 2 * n, n)],
            ],
            fresh=[self.x, self.y, self.ze2],
            after=after,
        )
        x, y, self.ze1, self.zf2 = hop(xin, X), hop(yin, Y), hop(e, Z1), hop(f, Z2)
        self.x, self.y = x, y
        both = [X | Y | k for k in ZS]
        self.got3 = self.keep([
            (x, self.upper(0, *both) + self.upper(1, X | Y) + self.upper(2, X | Y)),
            (y, self.lower(0, *both) + self.lower(1, X | Y) + self.lower(2, X | Y)),
        ])
        self.late3 = self.keep([(self.ze1, self.full(1, Z1, Z3)), (self.zf2, self.full(2, Z2))])
        return self.exchange(self.got2, [xin])

    def round4(self, after):
        n, h, part = self.n, self.h, self.part
        along = [part(self.ze1, 0, n), part(self.ze2, 0, n), part(self.ze1, n, n)]
        xin, yin, f, g = pack(
            [
                along + [part(self.y1, 3 * n + h, h)],
                along + [part(self.x1, 3 * n, h)],
                [part(self.own, 2 * n, n), part(self.zf2, 0, n)],
                [part(self.own, 3 * n, n)],
            ],
            fresh=[self.ze1, self.zf2],
            after=after,
        )
        x, y, self.zf1, self.zg2 = hop(xin, X), hop(yin, Y), hop(f, Z1), hop(g, Z2)
        self.x, self.y = x, y
        self.got4 = self.keep([
            (x, self.full(1, *(X | k for k in ZS)) + self.upper(3, X | Y)),
            (y, self.full(1, *(Y | k for k in ZS)) + self.lower(3, X | Y)),
            (self.zf1, self.full(2, Z1, Z3)),
            (self.zg2, self.full(3, Z2)),
        ])
        return self.exchange(self.got3, [xin])

    def round5(self, after):
        n, h, part = self.n, self.h, self.part
        along = [part(self.zf1, 0, n), part(self.zf2, 0, n), part(self.zf1, n, n)]
        xin, yin, g, d = pack(
            [
                [part(self.y, i * n + h, h) for i in range(3)] + along,
                [part(self.x, i * n, h) for i in range(3)] + along,
                [part(self.own, 3 * n, n), part(self.zg2, 0, n)],
                [part(self.y, 3 * n, h), part(self.x, 3 * n, h)],
            ],
            fresh=[self.x, self.y, self.zf1, self.zg2],
            after=after,
        )
        self.d = d
        x, y, self.zg1, self.zd2 = hop(xin, X), hop(yin, Y), hop(g, Z1), hop(d, Z2)
        self.x, self.y = x, y
        both = [X | Y | k for k in ZS]
        self.got5 = self.keep([
            (x, self.upper(1, *both) + self.full(2, *(X | k for k in ZS))),
            (y, self.lower(1, *both) + self.full(2, *(Y | k for k in ZS))),
            (self.zg1, self.full(3, Z1, Z3)),
            (self.zd2, self.full(3, X | Y | Z2)),
        ])
        return self.exchange(self.late3 + self.got4, [xin])

    def round6(self, after):
        n, h, part = self.n, self.h, self.part
        along = [part(self.zg1, 0, n), part(self.zg2, 0, n), part(self.zg1, n, n)]
        xin, yin, d = pack(
            [
                [part(self.y, 3 * h + i * n + h, h) for i in range(3)] + along,
                [part(self.x, 3 * h + i * n, h) for i in range(3)] + along,
                [part(self.d, 0, n), part(self.zd2, 0, n)],
            ],
            fresh=[self.x, self.y, self.zg1, self.zd2],
            after=after,
        )
        x, y, zd1 = hop(xin, X), hop(yin, Y), hop(d, Z1)
        both = [X | Y | k for k in ZS]
        self.got6 = self.keep([
            (x, self.upper(2, *both) + self.full(3, *(X | k for k in ZS))),
            (y, self.lower(2, *both) + self.full(3, *(Y | k for k in ZS))),
            (zd1, self.full(3, X | Y | Z1, X | Y | Z3)),
        ])
        return self.exchange(self.got5, [xin])

    def last(self, after):
        return self.exchange(self.got6, after)


class GatherPlain:
    def __init__(self, w_qkv, w_out, w_up, w_down):
        local = jnp.concatenate([w_qkv[0], w_qkv[1], w_qkv[2], w_out.T, w_up, w_down.T], axis=1)
        rows, width = local.shape
        whole = lax.all_gather(local, ("dp", "tensor")).reshape(lax.axis_size("dp"), 2, rows, width)
        self.pieces = [Piece(0, width, None, 0, 0, whole, 0, other) for other in range(2)]
        self.gate = None

    def round1(self):
        return None

    def round2(self, after):
        return None, None

    round3 = round4 = round5 = round6 = last = round2


class Spot:
    def __init__(self, array, row, rows, col, cols):
        self.array, self.row, self.rows, self.col, self.cols = array, row, rows, col, cols

    def of(self, ref, me, t):
        at = lambda v, unit: pl.multiple_of(v(me, t), unit) if callable(v) else v
        return ref.at[pl.ds(at(self.row, 16), self.rows), pl.ds(at(self.col, 128), self.cols)]


def arrange(where, shapes, moves, fresh=(), after=()):
    after_specs, after = waits(after)
    arrays = []
    for source, _, _ in moves:
        if not any(a is source.array for a in arrays):
            arrays.append(source.array)
    near = [any(a is f for f in fresh) for a in arrays]
    number = lambda array: next(i for i, a in enumerate(arrays) if a is array)
    plan = [(number(source.array), source, out, target) for source, out, target in moves]

    def kernel(where_ref, *refs):
        ins, results, sems = refs[: len(arrays)], refs[len(arrays) + len(after) : -1], refs[-1]
        me, t = where_ref[0], where_ref[1]
        copies = []
        for index, (slot, source, out, target) in enumerate(plan):
            copy = pltpu.make_async_copy(
                source.of(ins[slot], me, t), target.of(results[out], me, t), sems.at[index]
            )
            copy.start()
            copies.append(copy)
        for copy in copies:
            copy.wait()

    spaces = [pltpu.VMEM if n else pltpu.HBM for n in near]
    return made_near(pl.pallas_call(
        kernel,
        in_specs=[pl.BlockSpec(memory_space=pltpu.SMEM)]
        + [pl.BlockSpec(memory_space=m) for m in spaces]
        + after_specs,
        out_specs=[pl.BlockSpec(memory_space=pltpu.VMEM)] * len(shapes),
        out_shape=[pltpu.VMEM(shape, BF) for shape in shapes],
        scratch_shapes=[pltpu.SemaphoreType.DMA((len(plan),))],
        compiler_params=pltpu.CompilerParams(vmem_limit_bytes=8 * 2**20),
        cost_estimate=pl.CostEstimate(
            flops=0, bytes_accessed=sum(h * w * 4 for h, w in shapes), transcendentals=0
        ),
    )(where, *[pltpu.with_memory_space_constraint(a, m) for a, m in zip(arrays, spaces)], *after))


class GradientSum:
    def __init__(self, where, array, widths, mine, rank, adapters, picks):
        self.where, self.array, self.picks = where, array, picks
        self.mine, self.rank, self.adapters = mine, rank, adapters
        self.rows = mine * rank
        self.widths = widths
        self.starts = [sum(widths[:i]) for i in range(len(widths))]
        self.chunk = sum(widths) // 8

    def cores(self, after=()):
        half = 4 * self.chunk
        source = Spot(self.array, 0, self.rows, lambda me, t: (1 - t) * half, half)
        moves = [(source, 0, Spot(None, 0, self.rows, 0, half))]
        (out,) = arrange(self.where, [(self.rows, half)], moves, after=after)
        self.other = swap(out)
        return out

    def plane(self, after=()):
        rows, chunk = self.rows, self.chunk
        moves = []
        for k in range(4):
            mine = Spot(self.array, 0, rows, lambda me, t, k=k: (t * 4 + ((me & 3) ^ k)) * chunk, chunk)
            theirs = Spot(self.other, 0, rows, lambda me, t, k=k: ((me & 3) ^ k) * chunk, chunk)
            moves += [
                (mine, k, Spot(None, 0, rows, 0, chunk)),
                (theirs, k, Spot(None, rows, rows, 0, chunk)),
                (Spot(self.picks, 0, self.rank, 0, chunk), k, Spot(None, 2 * rows, self.rank, 0, chunk)),
            ]
        shape = (2 * rows + self.rank, chunk)
        outs = arrange(self.where, [shape] * 4, moves, fresh=[self.other], after=after)
        self.parts = [outs[0], hop(outs[1], X), hop(outs[2], Y), hop(outs[3], X | Y)]
        return outs[0]

    def fold(self, after=()):
        rank, chunk, data = self.rank, self.chunk, 2 * self.rows
        tall = self.adapters * rank
        quarter = tall // 4

        def kernel(where_ref, *refs):
            ins, outs, total = refs[:4], refs[-5:-1], refs[-1]
            z = where_ref[0] // 4
            row = lax.broadcasted_iota(jnp.int32, (tall, data), 0)
            col = lax.broadcasted_iota(jnp.int32, (tall, data), 1)
            adapter = (row // rank).astype(F32)
            same_row = row % rank == col % rank
            for k in range(4):
                picks = ins[k][data : data + 1, 0:data].astype(F32)
                chosen = jnp.logical_and(adapter == picks, same_row).astype(F32).astype(BF)
                part = nn(chosen, ins[k][0:data, :])
                total[...] = part if k == 0 else total[...] + part
            for k in range(4):
                rows = pl.ds(pl.multiple_of((z ^ k) * quarter, quarter), quarter)
                outs[k][...] = total[rows, :].astype(BF)

        outs = self.local(kernel, self.parts, after, [(quarter, chunk)] * 4, [(tall, chunk)])
        self.parts = [outs[0]] + [hop(outs[k], 4 * k) for k in (1, 2, 3)]
        return outs[0]

    def local(self, kernel, arrays, after, shapes, scratch):
        after_specs, after = waits(after)
        vmem = pl.BlockSpec(memory_space=pltpu.VMEM)
        return made_near(pl.pallas_call(
            kernel,
            in_specs=[pl.BlockSpec(memory_space=pltpu.SMEM)] + [vmem] * len(arrays) + after_specs,
            out_specs=[vmem] * len(shapes),
            out_shape=[pltpu.VMEM(shape, BF) for shape in shapes],
            scratch_shapes=[pltpu.VMEM(shape, F32) for shape in scratch],
            compiler_params=pltpu.CompilerParams(vmem_limit_bytes=12 * 2**20),
            cost_estimate=pl.CostEstimate(
                flops=0, bytes_accessed=sum(h * w * 8 for h, w in shapes), transcendentals=0
            ),
        )(
            self.where,
            *[pltpu.with_memory_space_constraint(a, pltpu.VMEM) for a in arrays],
            *after,
        ))

    def depth(self, after=()):
        def kernel(where_ref, *refs):
            total = refs[0][...].astype(F32)
            for ref in refs[1:4]:
                total += ref[...].astype(F32)
            refs[-1][...] = total.astype(BF)

        (out,) = self.local(kernel, self.parts, after, [self.parts[0].shape], [])
        self.parts = [out] + [hop(out, 4 * k) for k in (1, 2, 3)]
        return out

    def back(self, after=()):
        tall = self.adapters * self.rank
        quarter, side = tall // 4, self.chunk // 2
        moves = [
            (
                Spot(self.parts[k], 0, quarter, part * side, side),
                part,
                Spot(None, lambda me, t, k=k: ((me >> 2) ^ k) * quarter, quarter, 0, side),
            )
            for k in range(4)
            for part in range(2)
        ]
        self.a, self.b = arrange(self.where, [(tall, side)] * 2, moves, fresh=self.parts, after=after)
        self.xa, self.yb = hop(self.a, X), hop(self.b, Y)
        return self.a

    def spread(self, after=()):
        tall, side = self.adapters * self.rank, self.chunk // 2
        moves = [
            (Spot(source, 0, tall, 0, side), out, Spot(None, row * tall, tall, 0, side))
            for out, pair in enumerate(((self.a, self.xa), (self.b, self.yb)))
            for row, source in enumerate(pair)
        ]
        fresh = [self.a, self.b, self.xa, self.yb]
        up, down = arrange(self.where, [(2 * tall, side)] * 2, moves, fresh=fresh, after=after)
        self.ya, self.xb = hop(up, Y), hop(down, X)
        return up

    def give(self, after=()):
        tall, side = self.adapters * self.rank, self.chunk // 2
        sources = [
            ((self.a, 0), (self.b, 0)),
            ((self.xa, 0), (self.xb, 0)),
            ((self.ya, 0), (self.yb, 0)),
            ((self.ya, tall), (self.xb, tall)),
        ]
        moves = [
            (Spot(source, row, tall, 0, side), 0, Spot(None, k * tall, tall, part * side, side))
            for k, both in enumerate(sources)
            for part, (source, row) in enumerate(both)
        ]
        fresh = [self.a, self.b, self.xa, self.yb, self.ya, self.xb]
        (out,) = arrange(self.where, [(4 * tall, self.chunk)], moves, fresh=fresh, after=after)
        self.theirs = swap(out)
        self.ours = out
        return out


def finish(where, sums, results, after=()):
    tall = sums[0].adapters * sums[0].rank
    after_specs, after = waits(after)
    inputs = [a for s in sums for a in (s.ours, s.theirs)]

    def kernel(where_ref, *refs):
        outs = refs[len(inputs) + len(after) :]
        me, t = where_ref[0], where_ref[1]
        for out, parts in zip(outs, results):
            for place, (number, which) in enumerate(parts):
                total = sums[number]
                start, width = total.starts[which] // 8, total.widths[which] // 8
                for core in range(2):
                    for k in range(4):
                        column = ((t ^ core) * 4 + ((me & 3) ^ k)) * width
                        out[place * tall : (place + 1) * tall, pl.ds(pl.multiple_of(column, 128), width)] = refs[
                            2 * number + core
                        ][k * tall : (k + 1) * tall, start : start + width].astype(F32)

    vmem = pl.BlockSpec(memory_space=pltpu.VMEM)
    shapes = [(len(parts) * tall, sums[parts[0][0]].widths[parts[0][1]]) for parts in results]
    return pl.pallas_call(
        kernel,
        in_specs=[pl.BlockSpec(memory_space=pltpu.SMEM)]
        + [vmem] * len(inputs)
        + after_specs,
        out_specs=[vmem] * len(results),
        out_shape=[pltpu.HBM(shape, F32) for shape in shapes],
        compiler_params=pltpu.CompilerParams(vmem_limit_bytes=32 * 2**20),
        cost_estimate=pl.CostEstimate(
            flops=0, bytes_accessed=sum(h * w * 6 for h, w in shapes), transcendentals=0
        ),
    )(where, *inputs, *after)


def hold(array, after):
    after_specs, after = waits(after)
    return pl.pallas_call(
        lambda *refs: None,
        in_specs=after_specs + [pl.BlockSpec(memory_space=pltpu.HBM)],
        out_specs=pl.BlockSpec(memory_space=pltpu.HBM),
        out_shape=pltpu.HBM(array.shape, array.dtype),
        input_output_aliases={len(after): 0},
        cost_estimate=pl.CostEstimate(flops=0, bytes_accessed=0, transcendentals=0),
    )(*after, in_hbm(array))


def place(where, filled, arrived, after=()):
    after_specs, after = waits(after)
    mine, rows, width = arrived.shape

    def kernel(where_ref, arrived_ref, *refs):
        refs[-1][...] = arrived_ref[...]

    return pl.pallas_call(
        kernel,
        grid_spec=pltpu.PrefetchScalarGridSpec(
            num_scalar_prefetch=1,
            grid=(mine,),
            in_specs=[pl.BlockSpec((1, rows, width), lambda s, w: (s, 0, 0))]
            + after_specs
            + [pl.BlockSpec(memory_space=pltpu.HBM)],
            out_specs=pl.BlockSpec((1, rows, width), lambda s, w: ((1 - w[1]) * mine + s, 0, 0)),
        ),
        out_shape=pltpu.HBM(filled.shape, filled.dtype),
        input_output_aliases={2 + len(after): 0},
        **params(1, 2 * arrived.size * arrived.dtype.itemsize, 16 * 2**20),
    )(where, in_hbm(arrived), *after, in_hbm(filled))


def shards(
    hidden_in, segment_ids, adapter_pick, w_qkv, w_out, w_up, w_down, ln_gain, ln_bias,
    adapt_a, adapt_b, up_a, up_b, down_a, down_b, grad_out,
):
    dp = lax.axis_size("dp")
    t = lax.axis_index("tensor")
    block, ff_half = w_up.shape
    width = hidden_in.shape[2]
    half = width // 2
    ff = 2 * ff_half
    positions = hidden_in.shape[1]
    length = 2 * positions
    mine = hidden_in.shape[0] // 2
    rank = adapt_b.shape[2]
    adapters = adapt_b.shape[1]

    NEAR.clear()
    pick = lax.dynamic_slice_in_dim(adapter_pick, mine * t, mine, 0)
    where = jnp.stack([lax.axis_index("dp"), t]).astype(pick.dtype)
    meta = jnp.concatenate([pick, where])
    ordered = jnp.where(t == 0, adapter_pick, jnp.roll(adapter_pick, -mine))
    picks = jnp.repeat(ordered, rank).astype(BF)
    picks = jnp.broadcast_to(jnp.pad(picks, (0, 3 * half - picks.shape[0]))[None], (rank, 3 * half))
    segs = lax.dynamic_slice_in_dim(segment_ids, mine * t, mine, 0)
    seg_col = segs.reshape(mine, length, 1)
    seg_row = segs.reshape(mine, 1, length)

    sent_rows = mine * positions

    def send_half(value, after):
        flat = value.reshape(2 * sent_rows, width)
        spot = Spot(flat, lambda me, t: (1 - t) * sent_rows, sent_rows, 0, width)
        (out,) = arrange(where, [(sent_rows, width)], [(spot, 0, Spot(None, 0, sent_rows, 0, width))], after=after)
        return flat, out, swap(out)

    def join(flat, there, after):
        moves = []
        for s in range(mine):
            moves.append((
                Spot(flat, lambda me, t, s=s: (t * mine + s) * positions, positions, 0, width), 0,
                Spot(None, lambda me, t, s=s: s * length + t * positions, positions, 0, width),
            ))
            moves.append((
                Spot(there, s * positions, positions, 0, width), 0,
                Spot(None, lambda me, t, s=s: s * length + (1 - t) * positions, positions, 0, width),
            ))
        (out,) = arrange(where, [(mine * length, width)], moves, fresh=[there], after=after)
        return out.reshape(mine, length, width), out

    gather = (Gather if dp == 16 else GatherPlain)(w_qkv, w_out, w_up, w_down)
    gather.round1()
    def columns(first, count):
        return (gather.pieces, first, count, dp, block)

    qkv_w = columns(0, 3 * half)
    out_w = columns(3 * half, half)
    part = 2 * half
    up_parts = [columns(4 * half + p, part) for p in range(0, ff_half, part)]
    up_w = columns(4 * half, ff_half)
    down_w = columns(4 * half + ff_half, ff_half)

    a_t = jnp.swapaxes(adapt_a, 2, 3)
    ua_t = jnp.swapaxes(up_a, 1, 2)
    da_t = jnp.swapaxes(down_a, 1, 2)

    flat_x, gate, there_x = send_half(hidden_in, [gather.gate])
    flat_c, gate, there_c = send_half(grad_out, [gate])
    gate, met = gather.round2([meta, seg_col, seg_row, picks, gate])
    x, gate = join(flat_x, there_x, [gate])
    cotangent, gate = join(flat_c, there_c, [gate])
    _, met = gather.round3([met, gate])
    gate, _ = gather.round4([met])
    tokens = mine * length
    tiles = 2
    tile = length // tiles
    seq3 = lambda s, i, m: (s, 0, 0)
    row3 = lambda s, i, m: (s, i, 0)
    fixed2 = lambda s, i, m: (0, 0)
    picked3 = lambda s, i, m: (m[s], 0, 0)
    slots4 = lambda s, i, m: (0, m[s], 0, 0)
    last4 = lambda s, i, m: (3, m[s], 0, 0)
    full = lambda a: (a, (1, *a.shape[1:]), seq3)
    row = lambda a: (a, (1, tile, a.shape[2]), row3)
    across = lambda a: (a, (1, a.shape[1], tile), lambda s, i, m: (s, 0, i))
    whole = lambda a: (a, a.shape, fixed2)
    factor = lambda a: (a, (1, *a.shape[1:]), picked3)
    slots = lambda a: (a, (a.shape[0], 1, *a.shape[2:]), slots4)
    last = lambda a: (a, (1, 1, *a.shape[2:]), last4)
    rows_made = lambda dtype, cols: ((mine, length, cols), dtype, (1, tile, cols), row3)
    across_made = lambda rows: ((mine, rows, length), BF, (1, rows, tile), lambda s, i, m: (s, 0, i))
    def kept_made(dtype):
        block = (1, positions, width)
        return [
            ((2 * mine, positions, width), dtype, block, lambda s, i, m: (m[mine + 1] * mine + s, 0, 0)),
            ((mine, positions, width), dtype, block, seq3),
        ]

    sum_made = lambda rows, cols: ((mine, rows, cols), BF, (1, rows, cols), seq3)

    qkv, rank_qkv, whole_qkv = call(
        qkv_kernel, meta,
        [row(x), slots(a_t), slots(adapt_b)],
        [((mine, 3, length, width), BF, (1, 3, tile, width), lambda s, i, m: (s, 0, i, 0)),
         across_made(3 * rank)],
        6 * tokens * width * width,
        weights=[qkv_w],
        after=[gate],
        limit=24 * 2**20,
        tiles=tiles,
        saves=[(0, 3 * half, 0, None)],
    )
    gate, met = gather.round5([qkv])

    groups = width // GROUP

    def heads_of(slot, first, group=0):
        return pl.BlockSpec((1, 1, length, GROUP), lambda s, h: (s + first, slot, 0, h + group))

    def seg_specs(first):
        return [
            pl.BlockSpec((1, length, 1), lambda s, h: (s + first, 0, 0)),
            pl.BlockSpec((1, 1, length), lambda s, h: (s + first, 0, 0)),
        ]

    def lse_at(first, group=0):
        return pl.BlockSpec((1, 1, 8, length), lambda s, h: (s + first, h + group, 0, 0))

    def heads_at(first, group=0):
        return pl.BlockSpec((1, length, GROUP), lambda s, h: (s + first, 0, h + group))

    after_specs, after = waits([gate])
    attention, lse = pl.pallas_call(
        lambda q, k, v, sc, sr, *refs: attend_kernel(q, k, v, sc, sr, *refs[len(after) :]),
        grid=(mine, groups),
        in_specs=[heads_of(j, 0) for j in range(3)] + seg_specs(0) + after_specs,
        out_specs=[heads_at(0), lse_at(0)],
        out_shape=[
            pltpu.HBM((mine, length, width), BF),
            pltpu.HBM((mine, groups, 8, length), F32),
        ],
        **params(16 * tokens * length * width, tokens * width * 8, 16 * 2**20),
    )(*[in_hbm(a) for a in [qkv, qkv, qkv, seg_col, seg_row]], *after)
    gate, _ = gather.round6([lse, met])

    normed, inverse, middle_low, rank_out, whole_out = call(
        out_kernel, meta,
        [row(attention), row(x), last(a_t), last(adapt_b), whole(ln_gain), whole(ln_bias)],
        [rows_made(F32, width), rows_made(F32, 128), rows_made(BF, width), across_made(rank)],
        2 * tokens * width * width,
        scratch=[pltpu.VMEM((tile, width), F32)],
        weights=[out_w],
        limit=24 * 2**20,
        after=[gate],
        tiles=tiles,
        saves=[(0, half, 0, None)],
    )

    gate = rank_out
    blocks = ff_half // part
    made_up, whole_up = [], None
    for index, weight in enumerate(up_parts):
        up_cols = [
            (up_b, (1, rank, part), lambda s, i, m, at=h * blocks + index: (m[s], 0, at)) for h in range(2)
        ]
        units_made = (
            (mine, 2, length, ff_half), BF, (1, 2, tile, part), lambda s, i, m, index=index: (s, 0, i, index)
        )
        made = call(
            up_kernel, meta,
            [row(middle_low), factor(ua_t), *up_cols],
            [units_made, units_made, across_made(rank)],
            4 * tokens * width * part * 2,
            weights=[weight],
            limit=24 * 2**20,
            after=[gate],
            tiles=tiles,
            filled=made_up,
            saves=[(0, part, 0, None)] if index == 0 else [],
        )
        *made_up, rank_up = made[:3]
        gate = rank_up
        if index == 0:
            whole_up = made[3]
            gate, _ = gather.last([rank_up])
    units = lambda a: (a, (1, 2, tile, ff_half), lambda s, i, m: (s, 0, i, 0))
    act, slope = made_up

    layer_out, layer_sent, grad_first, grad_att, sooner = call(
        middle_kernel, meta,
        [units(act), units(slope), row(normed), row(inverse), row(cotangent), row(middle_low), row(attention),
         across(rank_up), across(rank_out), factor(da_t), factor(down_b), factor(ua_t), factor(up_b),
         last(a_t), last(adapt_b), whole(ln_gain), whole(ln_bias)],
        [*kept_made(BF), rows_made(F32, width), rows_made(BF, width),
         sum_made(rank, 2 * ff + 4 * width)],
        tokens * width * (6 * ff + 2 * width),
        scratch=[pltpu.VMEM((tile, width), F32), pltpu.VMEM((tile, width), F32), pltpu.VMEM((tile, width), BF),
                 pltpu.VMEM((tile, ff), BF), pltpu.VMEM((tile, width), BF),
                 pltpu.VMEM((rank, ff), F32), pltpu.VMEM((rank, width), F32),
                 pltpu.VMEM((rank, width), F32), pltpu.VMEM((rank, ff), F32),
                 pltpu.VMEM((rank, width), F32), pltpu.VMEM((rank, width), F32)],
        weights=[down_w, up_parts[1]],
        tiles=tiles,
        held=[whole_up, whole_out],
        near=False,
        limit=46 * 2**20,
    )

    layer_there = swap(layer_sent)
    flat = lambda g: g.reshape(mine * rank, g.shape[-1])
    sooner_widths = [ff, width, width, ff, width, width]
    later_widths = [width] * 6
    fast = dp == 16
    gate = None
    if fast:
        first_sum = GradientSum(where, flat(sooner), sooner_widths, mine, rank, adapters, picks)
        gate = first_sum.cores()

    halves = 2
    span = groups // halves

    def attend_back(first, group, made, after):
        after_specs, after = waits(after)
        extra = len(made) + len(after)

        def body(q, k, v, sc, sr, l, o, do, *refs):
            attend_back_kernel(q, k, v, sc, sr, l, o, do, *refs[extra:])

        args = [qkv, qkv, qkv, seg_col, seg_row, lse, attention, grad_att, *made]
        return pl.pallas_call(
            body,
            grid=(1, span),
            in_specs=[heads_of(j, first, group) for j in range(3)]
            + seg_specs(first)
            + [lse_at(first, group), heads_at(first, group), heads_at(first, group)]
            + [pl.BlockSpec(memory_space=pltpu.HBM) for _ in made]
            + after_specs,
            out_specs=[heads_at(first, group)] * 3,
            out_shape=[pltpu.HBM((mine, length, width), BF)] * 3,
            input_output_aliases={8 + i: i for i in range(len(made))},
            **params(40 * length * length * width // halves, length * width * 16, 32 * 2**20),
        )(*[in_hbm(a) for a in args], *after)

    grads_qkv = []
    between = iter([first_sum.plane, first_sum.fold, first_sum.depth, first_sum.back] if fast else [])
    for index in range(mine):
        for group in range(0, groups, span):
            grads_qkv = attend_back(index, group, grads_qkv, [gate])
            gate = None
            phase = next(between, None)
            if phase is not None and (index, group) != (mine - 1, groups - span):
                gate = phase([grads_qkv[0]])
    gate = first_sum.back([grads_qkv[0]]) if fast else None

    grad_rank, later = call(
        rank_back_kernel, meta,
        [full(g) for g in grads_qkv] + [full(x), full(rank_qkv), slots(adapt_b)],
        [sum_made(3 * rank, length), sum_made(rank, 6 * width)],
        18 * tokens * width * rank,
        after=[gate],
        limit=32 * 2**20,
    )
    gate = grad_rank
    if fast:
        second_sum = GradientSum(where, flat(later), later_widths, mine, rank, adapters, picks)
        gate = second_sum.cores([gate])
        gate = first_sum.spread([gate])
        gate = second_sum.plane([gate])

    grad_in, grad_sent = call(
        qkv_back_kernel, meta,
        [row(g) for g in grads_qkv] + [across(grad_rank), row(grad_first), slots(a_t)],
        kept_made(F32),
        6 * tokens * width * width,
        held=[whole_qkv],
        after=[gate],
        limit=40 * 2**20,
        tiles=tiles,
    )
    turned = lambda v: jnp.swapaxes(v, -1, -2)
    if fast:
        gate = second_sum.fold([grad_in])
        gate = first_sum.give([gate])
        layer_out = place(where, layer_out, layer_there, [gate])
        gate = second_sum.depth([layer_out])
        there = swap(hold(grad_sent, [gate]))
        done1 = finish(where, [first_sum], [[(0, 0)], [(0, 1)], [(0, 2)], [(0, 3)]], [gate])
        gate = second_sum.back([done1[0]])
        grad_in = place(where, grad_in, there, [gate])
        gate = second_sum.spread([grad_in])
        second_sum.give([gate])
        all_a, all_b = finish(
            where, [second_sum, first_sum],
            [[(0, 0), (0, 1), (0, 2), (1, 4)], [(0, 3), (0, 4), (0, 5), (1, 5)]],
        )
        shaped = lambda v: v.reshape(-1, adapters, rank, v.shape[1])
        da, db, ua, ub = (shaped(v)[0] for v in done1)
        return (layer_out, grad_in, turned(shaped(all_a)), shaped(all_b), turned(ua), ub, turned(da), db)

    layer_out = place(where, layer_out, layer_there)
    grad_in = place(where, grad_in, swap(grad_sent))
    onehot = (pick[:, None] == jnp.arange(adapters)[None, :]).astype(F32)

    def fold(per_sequence):
        total = onehot[0][:, None, None] * per_sequence[0][None].astype(F32)
        for index in range(1, mine):
            total += onehot[index][:, None, None] * per_sequence[index][None].astype(F32)
        return total

    def apart(array, widths):
        chunks, at, parts = array.reshape(mine, rank, 8, -1), 0, []
        for columns_of in widths:
            part = chunks[..., at : at + columns_of // 8]
            parts.append(part.reshape(mine, rank, columns_of))
            at += columns_of // 8
        return parts

    g_down_a, g_down_b, g_up_a, g_up_b, g_out_a, g_out_b = apart(sooner, sooner_widths)
    qkv_sums = apart(later, later_widths)
    sums = lax.psum(
        tuple(
            fold(g)
            for g in [*qkv_sums[:3], g_out_a, *qkv_sums[3:], g_out_b, g_up_a, g_up_b, g_down_a, g_down_b]
        ),
        ("dp", "tensor"),
    )
    return (
        layer_out,
        grad_in,
        turned(jnp.stack(sums[:4])),
        jnp.stack(sums[4:8]),
        turned(sums[8]),
        sums[9],
        turned(sums[10]),
        sums[11],
    )


def solution(mesh):
    placed = (
        P("dp", "tensor", None),
        P("dp", None),
        P("dp"),
        P(None, "dp", "tensor"),
        P("tensor", "dp"),
        P("dp", "tensor"),
        P("tensor", "dp"),
        P(),
        P(),
        P(),
        P(),
        P(),
        P(),
        P(),
        P(),
        P("dp", "tensor", None),
    )
    return jax.shard_map(
        shards,
        mesh=mesh,
        in_specs=placed,
        out_specs=(P("dp", "tensor", None), P("dp", "tensor", None), P(), P(), P(), P(), P(), P()),
        check_vma=False,
    )
```

```python
import functools

import jax
import jax.numpy as jnp
from jax import lax
from jax.experimental import pallas as pl
from jax.experimental.pallas import tpu as pltpu
from jax.sharding import PartitionSpec as P

HEAD_DIM = 64
BF = jnp.bfloat16
F32 = jnp.float32
LOG2E = 1.4426950408889634
VMEM = 60 * 2**20


def nn(a, b):
    return lax.dot_general(a, b, (((1,), (0,)), ((), ())), preferred_element_type=F32)


def nt(a, b):
    return lax.dot_general(a, b, (((1,), (1,)), ((), ())), preferred_element_type=F32)


def tn(a, b):
    return lax.dot_general(a, b, (((0,), (0,)), ((), ())), preferred_element_type=F32)


def params(flops, nbytes, limit=VMEM):
    return dict(
        compiler_params=pltpu.CompilerParams(vmem_limit_bytes=limit),
        cost_estimate=pl.CostEstimate(flops=flops, bytes_accessed=nbytes, transcendentals=0),
    )


class Piece:
    def __init__(self, col, width, rel, row, count, array, at, other):
        self.col, self.width, self.rel, self.row = col, width, rel, row
        self.count, self.array, self.at, self.other = count, array, at, other


def first_tile():
    return jnp.logical_and(pl.program_id(0) == 0, pl.program_id(1) == 0)


class Loader:
    def __init__(self, plan, refs, scratch, sems, me, t, dp):
        self.plan, self.refs, self.scratch, self.sems = plan, refs, scratch, sems
        self.me, self.t, self.dp = me, t, dp
        self.saved = None
        self.width = scratch.shape[1] // 2
        self.block = scratch.shape[0] // dp

    def start(self):
        def copy(source, block, row, count, into, width, other):
            rows = pl.ds(pl.multiple_of(block * self.block + row, 16), count)
            cols = pl.ds(pl.multiple_of((self.t ^ other) * self.width + into, 128), width)
            pltpu.make_async_copy(source, self.scratch.at[rows, cols], self.sems.at[other]).start()

        for slot, at, count, col, width, other, rel, row, into in self.plan:
            cols = pl.ds(col, width)
            if rel is None:
                for block in range(self.dp):
                    source = self.refs[slot].at[block, self.t ^ other, :, cols]
                    copy(source, block, 0, self.block, into, width, other)
            else:
                copy(self.refs[slot].at[pl.ds(at, count), cols], self.me ^ rel, row, count, into, width, other)

    def wait(self, other):
        cols = pl.ds(pl.multiple_of((self.t ^ other) * self.width, 128), self.width)
        whole = self.scratch.at[:, cols]
        pltpu.make_async_copy(whole, whole, self.sems.at[other]).wait()

    def first_step(self):
        pl.when(first_tile())(self.start)

    def first_wait(self, other):
        pl.when(first_tile())(lambda: self.wait(other))

    def first_wait_all(self):
        @pl.when(first_tile())
        def _():
            self.wait(0)
            self.wait(1)
            if self.saved is not None:
                for copy in self.save_copies():
                    copy.start()

    def save_copies(self):
        ref, first, sems = self.saved
        half = ref.shape[1] // 2
        return [
            pltpu.make_async_copy(
                self.scratch.at[:, pl.ds(h * self.width, self.width)],
                ref.at[:, pl.ds(h * half + first, self.width)],
                sems.at[h],
            )
            for h in range(2)
        ]

    def cols(self, half, lo, width):
        at = half * self.width + lo
        return self.scratch[:, pl.ds(at if isinstance(at, int) else pl.multiple_of(at, 128), width)]


class Held:
    def __init__(self, ref):
        self.scratch, self.width = ref, ref.shape[1] // 2

    cols = Loader.cols


def weight_plan(pieces, first, width):
    arrays, plan = [], []
    for p in pieces:
        lo, hi = max(p.col, first), min(p.col + p.width, first + width)
        if lo >= hi:
            continue
        slot = next((i for i, a in enumerate(arrays) if a is p.array), None)
        if slot is None:
            slot = len(arrays)
            arrays.append(p.array)
        plan.append((slot, p.at, p.count, lo - p.col, hi - lo, p.other, p.rel, p.row, lo - first))
    return arrays, plan


def qkv_kernel(meta, ins, outs, weights, scratch):
    x_ref, a_ref, b_ref = ins
    qkv_ref, rank_ref = outs
    (w,) = weights
    w.first_step()
    w.first_wait_all()
    x = x_ref[0]
    slots, rank_size = rank_ref.shape[1] // a_ref.shape[2], a_ref.shape[2]
    factors = a_ref[0:slots, 0].reshape(slots * rank_size, x.shape[1])
    rank = nt(x, factors)
    rank_ref[0] = rank.T.astype(BF)
    rank = rank.astype(BF)
    width = w.width // slots
    for half in range(2):
        cols = slice(half * width, (half + 1) * width)
        for slot in range(slots):
            mine = rank[:, slot * rank_size : (slot + 1) * rank_size]
            full = nn(x, w.cols(half, slot * width, width)) + nn(mine, b_ref[slot, 0, :, cols])
            qkv_ref[0, slot, :, cols] = full.astype(BF)


SCALE = HEAD_DIM**-0.5
SCALE2 = SCALE * LOG2E
GROUP = 4 * HEAD_DIM


def one_head(lane, head, value):
    return jnp.where(lane // HEAD_DIM == head, value, jnp.zeros((), value.dtype))


def attend_kernel(q_ref, k_ref, v_ref, segc_ref, segr_ref, out_ref, lse_ref):
    q, k, v = q_ref[0, 0], k_ref[0, 0], v_ref[0, 0]
    length, lanes = q.shape
    heads = lanes // HEAD_DIM
    lane = lax.broadcasted_iota(jnp.int32, (1, lanes), 1)
    same = segc_ref[0] == segr_ref[0]
    v_t = v.T

    def score(head):
        return nt(one_head(lane, head, k), q)

    mixed = []
    scores = score(0)
    for head in range(heads):
        following = score(head + 1) if head + 1 < heads else None
        masked = jnp.where(same, scores, F32(-1000000000.0 / SCALE))
        peak = jnp.max(masked, axis=0, keepdims=True) * SCALE2
        weights = jnp.exp2(masked * SCALE2 - peak)
        mass = jnp.sum(weights, axis=0, keepdims=True)
        rows = slice(head * HEAD_DIM, (head + 1) * HEAD_DIM)
        mixed.append(nn(v_t[rows, :], weights.astype(BF)) * (1.0 / mass))
        lse_ref[0, 0, head : head + 1, :] = peak + jnp.log2(mass)
        scores = following
    out_ref[0] = jnp.concatenate(mixed, axis=0).astype(BF).T
    lse_ref[0, 0, heads:, :] = jnp.zeros((lse_ref.shape[2] - heads, length), F32)


def attend_back_kernel(
    q_ref, k_ref, v_ref, segc_ref, segr_ref, lse_ref, o_ref, do_ref, gq_ref, gk_ref, gv_ref
):
    q, k, v, do = q_ref[0, 0], k_ref[0, 0], v_ref[0, 0], do_ref[0]
    lanes = q.shape[1]
    lane = lax.broadcasted_iota(jnp.int32, (1, lanes), 1)
    product = do.astype(F32) * o_ref[0].astype(F32)
    high = product.astype(BF)
    low = (product - high.astype(F32)).astype(BF)
    picker = (
        lax.broadcasted_iota(jnp.int32, (8, lanes), 0)
        == lax.broadcasted_iota(jnp.int32, (8, lanes), 1) // HEAD_DIM
    ).astype(BF)
    inner = nt(picker, high) + nt(picker, low)
    same = segc_ref[0] == segr_ref[0]
    grad_q = grad_k = grad_v = None
    for head in range(lanes // HEAD_DIM):
        k_mine = one_head(lane, head, k)
        masked = jnp.where(same, nt(k_mine, q), F32(-1000000000.0 / SCALE))
        probs = jnp.exp2(masked * SCALE2 - lse_ref[0, 0, head : head + 1, :])
        grad_probs = nt(one_head(lane, head, v), do)
        grad_scores = (probs * (grad_probs - inner[head : head + 1, :])).astype(BF)
        part_v = nn(probs.astype(BF), one_head(lane, head, do))
        part_k = nn(grad_scores, one_head(lane, head, q))
        part_q = tn(grad_scores, k_mine)
        grad_v = part_v if head == 0 else grad_v + part_v
        grad_k = part_k if head == 0 else grad_k + part_k
        grad_q = part_q if head == 0 else grad_q + part_q
    gq_ref[0] = (grad_q * SCALE).astype(BF)
    gk_ref[0] = (grad_k * SCALE).astype(BF)
    gv_ref[0] = grad_v.astype(BF)


def norm_parts(values):
    mean = jnp.mean(values, axis=-1, keepdims=True)
    centred = values - mean
    inverse = lax.rsqrt(jnp.mean(centred * centred, axis=-1, keepdims=True) + 1e-06)
    return centred * inverse, inverse


def norm_back(scaled, normed, inverse):
    mean_grad = jnp.mean(scaled, axis=-1, keepdims=True)
    mean_proj = jnp.mean(scaled * normed, axis=-1, keepdims=True)
    return (scaled - mean_grad - normed * mean_proj) * inverse


ROWS = 64


def by_rows(count, step):
    for row in range(0, count, ROWS):
        step(slice(row, row + ROWS))


def out_kernel(meta, ins, outs, weights, scratch):
    att_ref, x_ref, a_ref, b_ref, gain_ref, bias_ref = ins
    normed_ref, inverse_ref, low_ref, rank_ref = outs
    (w,) = weights
    (v_scr,) = scratch
    w.first_step()
    w.first_wait_all()
    att = att_ref[0]
    rank = nt(att, a_ref[0, 0])
    rank_ref[0] = rank.T.astype(BF)
    rank = rank.astype(BF)
    width = w.width
    v_scr[...] = (
        nt(att[:, :width], w.cols(0, 0, width))
        + nt(att[:, width:], w.cols(1, 0, width))
        + nn(rank, b_ref[0, 0])
    )

    def step(rows):
        normed, inverse = norm_parts(v_scr[rows, :] + x_ref[0, rows, :].astype(F32))
        normed_ref[0, rows, :] = normed
        inverse_ref[0, rows, :] = jnp.broadcast_to(inverse, (ROWS, 128))
        low_ref[0, rows, :] = (normed * gain_ref[0:1, :] + bias_ref[0:1, :]).astype(BF)

    by_rows(v_scr.shape[0], step)


def gelu_parts(x):
    phi = 0.5 + 0.5 * lax.erf(x * 0.7071067811865476)
    density = jnp.exp2((-0.5 * LOG2E) * x * x)
    return x * phi, phi + x * (density * 0.3989422804014327)


CHUNK = 512


def up_kernel(meta, ins, outs, weights, scratch):
    w, *more = weights
    m_ref, a_ref = ins[:2]
    b_refs = ins[2:]
    act_ref, slope_ref, rank_ref = outs
    for loader in weights:
        loader.first_step()
    w.first_wait_all()
    m = m_ref[0]
    rank = nt(m, a_ref[0])
    rank_ref[0] = rank.T.astype(BF)
    rank = rank.astype(BF)
    width = w.width
    for half, b_ref in enumerate(b_refs):
        for lo in range(0, width, CHUNK):
            cols = slice(lo, lo + CHUNK)
            units = nn(m, w.cols(half, lo, CHUNK)) + nn(rank, b_ref[0, :, cols])
            act, slope = gelu_parts(units)
            act_ref[0, half, :, cols] = act.astype(BF)
            slope_ref[0, half, :, cols] = slope.astype(BF)

    last = jnp.logical_and(
        pl.program_id(0) == pl.num_programs(0) - 1, pl.program_id(1) == pl.num_programs(1) - 1
    )

    @pl.when(last)
    def _():
        for loader in more:
            loader.wait(0)
            loader.wait(1)


def add_up(total, part, fresh):
    total[...] = jnp.where(fresh, part, total[...] + part)


def by_chunks(ref, parts):
    at = 0
    for chunk in range(8):
        for part in parts:
            width = part.shape[1] // 8
            ref[0, :, at : at + width] = part[:, chunk * width : (chunk + 1) * width].astype(BF)
            at += width


def keep_or_send(t, value, kept_ref, sent_ref):
    @pl.when(pl.program_id(1) == t)
    def _():
        kept_ref[0] = value

    @pl.when(pl.program_id(1) != t)
    def _():
        sent_ref[0] = value


def middle_kernel(meta, ins, outs, weights, scratch):
    (act_ref, slope_ref, n1_ref, r1_ref, go_ref, m_ref, att_ref, ranku_ref, ranko_ref,
     da_ref, db_ref, ua_ref, ub_ref, oa_ref, ob_ref, gain_ref, bias_ref) = ins
    kept_ref, sent_ref, first_ref, gatt_ref = outs[:4]
    down, early_up, late_up, out = weights
    v_scr, second_scr, gf_scr, gh_scr, out_scr = scratch[:5]
    sums = scratch[5:]
    sum_da, sum_db, sum_ua, sum_ub, sum_oa, sum_ob = sums
    tile = pl.program_id(1)
    fresh = tile == 0
    width = down.width
    part = early_up.width
    halves = [slice(0, width), slice(width, 2 * width)]

    rank = sum(nt(act_ref[0, h], da_ref[0, :, halves[h]]) for h in range(2)).astype(BF)
    model = v_scr.shape[1]
    for at in range(0, model, CHUNK):
        cols = slice(at, at + CHUNK)
        v_scr[:, cols] = (
            nt(act_ref[0, 0], down.scratch[cols, halves[0]])
            + nt(act_ref[0, 1], down.scratch[cols, halves[1]])
            + nn(rank, db_ref[0, :, cols])
        )

    def second_norm(rows):
        middle = n1_ref[0, rows, :] * gain_ref[0:1, :] + bias_ref[0:1, :]
        normed, inverse = norm_parts(v_scr[rows, :] + middle)
        out_scr[rows, :] = (normed * gain_ref[1:2, :] + bias_ref[1:2, :]).astype(BF)
        second = norm_back(go_ref[0, rows, :].astype(F32) * gain_ref[1:2, :], normed, inverse)
        second_scr[rows, :] = second
        gf_scr[rows, :] = second.astype(BF)

    by_rows(v_scr.shape[0], second_norm)
    grad_feed = gf_scr[...]
    add_up(sum_db, tn(rank, grad_feed), fresh)
    grad_rank = nt(grad_feed, db_ref[0]).astype(BF)
    chunk = 2 * CHUNK
    for half in range(2):
        for lo in range(0, width, chunk):
            cols = slice(half * width + lo, half * width + lo + chunk)
            grad_act = nn(grad_feed, down.cols(half, lo, chunk)) + nn(grad_rank, da_ref[0, :, cols])
            local = slice(lo, lo + chunk)
            gh_scr[:, cols] = (grad_act * slope_ref[0, half, :, local].astype(F32)).astype(BF)
    grad_rank_down = grad_rank

    grad_rank = nt(gh_scr[...], ub_ref[0]).astype(BF)
    for at in range(0, model, CHUNK):
        cols = slice(at, at + CHUNK)
        total = nn(grad_rank, ua_ref[0, :, cols])
        for half in range(2):
            lo = half * width
            local = slice(half * part, (half + 1) * part)
            total = total + nt(gh_scr[:, lo : lo + part], early_up.scratch[cols, local])
            total = total + nt(gh_scr[:, lo + part : lo + width], late_up.scratch[cols, local])
        v_scr[:, cols] = total
    add_up(sum_ua, tn(grad_rank, m_ref[0]), fresh)
    add_up(sum_ub, nn(ranku_ref[0], gh_scr[...]), fresh)
    for half in range(2):
        add_up(sum_da.at[:, halves[half]], tn(grad_rank_down, act_ref[0, half]), fresh)

    def first_norm(rows):
        scaled = (second_scr[rows, :] + v_scr[rows, :]) * gain_ref[0:1, :]
        first = norm_back(scaled, n1_ref[0, rows, :], r1_ref[0, rows, 0:1])
        first_ref[0, rows, :] = first
        gf_scr[rows, :] = first.astype(BF)

    by_rows(v_scr.shape[0], first_norm)
    grad_branch = gf_scr[...]
    grad_rank = nt(grad_branch, ob_ref[0, 0]).astype(BF)
    add_up(sum_oa, tn(grad_rank, att_ref[0]), fresh)
    add_up(sum_ob, nn(ranko_ref[0], grad_branch), fresh)
    owidth = out.width
    for half in range(2):
        cols = slice(half * owidth, (half + 1) * owidth)
        full = nn(grad_branch, out.cols(half, 0, owidth)) + nn(grad_rank, oa_ref[0, 0, :, cols])
        gatt_ref[0, :, cols] = full.astype(BF)

    keep_or_send(meta[meta.shape[0] - 1], out_scr[...], kept_ref, sent_ref)

    @pl.when(tile == pl.num_programs(1) - 1)
    def _():
        by_chunks(outs[4], sums)


def rank_back_kernel(meta, ins, outs, weights, scratch):
    gq_ref, gk_ref, gv_ref, x_ref, rank_ref, b_ref = ins
    gr_ref, sum_ref = outs
    size = b_ref.shape[2]
    ranks, parts_b = [], []
    for slot, ref in enumerate((gq_ref, gk_ref, gv_ref)):
        grad = ref[0]
        ranks.append(nt(b_ref[slot, 0], grad))
        parts_b.append(nn(rank_ref[0, slot * size : (slot + 1) * size, :], grad))
    stacked = jnp.concatenate(ranks, axis=0).astype(BF)
    gr_ref[0] = stacked
    products = nn(stacked, x_ref[0])
    parts_a = [products[slot * size : (slot + 1) * size] for slot in range(3)]
    by_chunks(sum_ref, parts_a + parts_b)


def qkv_back_kernel(meta, ins, outs, weights, scratch):
    gq_ref, gk_ref, gv_ref, gr_ref, first_ref, a_ref = ins
    kept_ref, sent_ref = outs
    (w,) = weights
    slots = 3
    width = w.width // slots
    size = a_ref.shape[2]
    total = first_ref[0] + tn(
        gr_ref[0], a_ref[0:slots, 0].reshape(slots * size, kept_ref.shape[2])
    )
    for half in range(2):
        cols = slice(half * width, (half + 1) * width)
        for slot, ref in enumerate((gq_ref, gk_ref, gv_ref)):
            total += nt(ref[0, :, cols], w.cols(half, slot * width, width))
    keep_or_send(meta[meta.shape[0] - 1], total, kept_ref, sent_ref)


NEAR = []


def made_near(arrays):
    NEAR.extend(arrays)
    return arrays


def waits(arrays):
    arrays = [a for a in arrays if a is not None]
    near = [any(a is n for n in NEAR) for a in arrays]
    specs = [pl.BlockSpec(memory_space=pl.ANY if n else pltpu.HBM) for n in near]
    return specs, [a if n else in_hbm(a) for a, n in zip(arrays, near)]


def far(arrays):
    return [pl.BlockSpec(memory_space=pltpu.HBM) for _ in arrays], [in_hbm(a) for a in arrays]


def call(kernel, meta, ins, outs, flops, scratch=(), weights=(), limit=VMEM, after=(), tiles=1, filled=(),
         saves=(), held=(), near=True, stays=()):
    plans = [weight_plan(pieces, first, width) for pieces, first, width, _, _ in weights]
    n_in, n_out, n_w = len(ins), len(outs), len(weights)
    counts = [len(arrays) for arrays, _ in plans]
    steps = meta.shape[0] - 2
    after_specs, after = waits(after)
    n_after = len(after)

    def body(meta_ref, *refs):
        refs = list(refs)
        take = lambda n: [refs.pop(0) for _ in range(n)]
        in_refs = take(n_in)
        w_refs = [take(n) for n in counts]
        take(n_after + len(filled))
        held_refs = take(len(held))
        take(len(started))
        out_refs = take(n_out)
        save_refs = take(len(saves))
        stay_refs = dict(zip(stays, take(len(stays))))
        w_scr = [stay_refs[i] if i in stay_refs else take(1)[0] for i in range(n_w)]
        w_sem = take(n_w)
        save_sems = take(len(saves))
        me, t = meta_ref[steps], meta_ref[steps + 1]
        loaders = [
            Loader(plan, r, s, m, me, t, w[3])
            for (_, plan), r, s, m, w in zip(plans, w_refs, w_scr, w_sem, weights)
        ]
        for (number, _, first, _), ref, sem in zip(saves, save_refs, save_sems):
            loaders[number].saved = (ref, first, sem)
        kernel(meta_ref, in_refs, out_refs, loaders + [Held(ref) for ref in held_refs], refs)
        for number, *_ in saves:

            @pl.when(jnp.logical_and(pl.program_id(0) == steps - 1, pl.program_id(1) == tiles - 1))
            def _(loader=loaders[number]):
                for copy in loader.save_copies():
                    copy.wait()

    started = [array for *_, array in saves if array is not None]
    w_arrays = [a for arrays, _ in plans for a in arrays]
    first_alias = 1 + n_in + len(w_arrays) + n_after
    w_specs, w_arrays = waits(w_arrays) if near else far(w_arrays)
    nbytes = sum(a.size * a.dtype.itemsize for a, _, _ in ins)
    nbytes += sum(2 * dp * rows * width * 2 for _, _, width, dp, rows in weights)
    for shape, dtype, _, _ in outs:
        size = jnp.dtype(dtype).itemsize
        for extent in shape:
            size *= extent
        nbytes += size
    return pl.pallas_call(
        body,
        grid_spec=pltpu.PrefetchScalarGridSpec(
            num_scalar_prefetch=1,
            grid=(steps, tiles),
            in_specs=[pl.BlockSpec(block, index) for _, block, index in ins]
            + w_specs
            + after_specs
            + [pl.BlockSpec(memory_space=pltpu.HBM) for _ in filled]
            + [pl.BlockSpec(memory_space=pltpu.VMEM) for _ in held]
            + [pl.BlockSpec(memory_space=pltpu.HBM) for _ in started],
            out_specs=[pl.BlockSpec(block, index) for _, _, block, index in outs]
            + [pl.BlockSpec(memory_space=pltpu.HBM) for _ in saves]
            + [pl.BlockSpec(memory_space=pltpu.VMEM) for _ in stays],
            scratch_shapes=[
                pltpu.VMEM((dp * rows, 2 * width), BF)
                for i, (_, _, width, dp, rows) in enumerate(weights)
                if i not in stays
            ]
            + [pltpu.SemaphoreType.DMA((2,)) for _ in [*weights, *saves]]
            + list(scratch),
        ),
        out_shape=[pltpu.HBM(shape, dtype) for shape, dtype, _, _ in outs]
        + [pltpu.HBM((weights[n][3] * weights[n][4], 2 * half), BF) for n, half, _, _ in saves]
        + [pltpu.VMEM((weights[n][3] * weights[n][4], 2 * weights[n][2]), BF) for n in stays],
        input_output_aliases={first_alias + i: i for i in range(len(filled))}
        | {first_alias + len(filled) + len(held) + i: n_out + i for i in range(len(started))},
        **params(flops, nbytes, limit),
    )(
        meta, *[in_hbm(a) for a, _, _ in ins], *w_arrays, *after, *[in_hbm(a) for a in filled],
        *[pltpu.with_memory_space_constraint(a, pltpu.VMEM) for a in held], *[in_hbm(a) for a in started],
    )


def pack(outs, fresh=(), after=()):
    after_specs, after = waits(after)
    arrays, plan, heights, widths = [], [], [], []

    def slot(array):
        for index, known in enumerate(arrays):
            if known is array:
                return index
        arrays.append(array)
        return len(arrays) - 1

    for index, parts in enumerate(outs):
        row = 0
        for part in parts:
            array, at, count, col, cols, into, advance = part
            plan.append((slot(array), at, count, col, cols, index, row, into))
            if advance:
                row += count
        heights.append(row)
        widths.append(max(part[4] + part[5] for part in parts))
    used, n_in = len(arrays), len(arrays) + len(after)
    near = [any(a is f for f in fresh) for a in arrays]

    def kernel(*refs):
        ins, results, sems = refs[:n_in], refs[n_in:-1], refs[-1]
        copies = []
        for number, (a, at, count, col, cols, o, row, into) in enumerate(plan):
            source = ins[a].at[pl.ds(at, count), pl.ds(col, cols)]
            target = results[o].at[pl.ds(row, count), pl.ds(into, cols)]
            if not near[a]:
                copy = pltpu.make_async_copy(source, target, sems.at[number])
                copy.start()
                copies.append(copy)
        for a, at, count, col, cols, o, row, into in plan:
            if near[a]:
                results[o][pl.ds(row, count), pl.ds(into, cols)] = ins[a][pl.ds(at, count), pl.ds(col, cols)]
        for copy in copies:
            copy.wait()

    spaces = [pltpu.VMEM if n else pltpu.HBM for n in near]
    return made_near(pl.pallas_call(
        kernel,
        in_specs=[pl.BlockSpec(memory_space=space) for space in spaces] + after_specs,
        out_specs=[pl.BlockSpec(memory_space=pltpu.VMEM)] * len(outs),
        out_shape=[pltpu.VMEM(shape, BF) for shape in zip(heights, widths)],
        scratch_shapes=[pltpu.SemaphoreType.DMA((len(plan),))],
        compiler_params=pltpu.CompilerParams(vmem_limit_bytes=8 * 2**20),
        cost_estimate=pl.CostEstimate(
            flops=0, bytes_accessed=sum(h * w * 4 for h, w in zip(heights, widths)), transcendentals=0
        ),
    )(*[pltpu.with_memory_space_constraint(a, space) for a, space in zip(arrays, spaces)], *after))


def in_hbm(array):
    return pltpu.with_memory_space_constraint(array, pltpu.HBM)


X, Y, Z1, Z2, Z3 = 1, 2, 4, 8, 12
ZS = (Z1, Z2, Z3)


def hop(array, bits):
    return lax.ppermute(array, "dp", [(i, i ^ bits) for i in range(lax.axis_size("dp"))])


def swap(array):
    return lax.ppermute(array, "tensor", [(0, 1), (1, 0)])


class Gather:
    def __init__(self, w_qkv, w_out, w_up, w_down):
        self.n = n = w_up.shape[0]
        self.h = n // 2
        self.pieces = []
        o, u = w_qkv.shape[2], w_up.shape[1]
        self.width = 3 * o
        flat = w_qkv.reshape(3 * n, o)
        wo, wd = w_out.T, w_down.T
        queries = [(flat, slot * n, n, 0, o, slot * o, slot == 2) for slot in range(3)]
        rest = [
            (wo, 0, n, 0, o, 0, False), (w_up, 0, n, 0, 2 * o, o, True),
            (w_up, 0, n, 2 * o, u - 2 * o, 0, False), (wd, 0, n, 0, o, 2 * o, True),
            (wd, 0, n, o, 3 * o, 0, True),
        ]
        self.own, self.q = pack([queries + rest, queries])
        self.gate = self.q
        self.e, self.f, self.g = (self.cut(p) for p in (1, 2, 3))

    def cut(self, piece):
        return lax.slice_in_dim(self.own, piece * self.n, (piece + 1) * self.n, axis=0)

    def note(self, array, items, other=0):
        at = 0
        for piece, rel, row, count in items:
            self.pieces.append(Piece(piece * self.width, self.width, rel, row, count, array, at, other))
            at += count

    def part(self, array, at, count):
        return (array, at, count, 0, self.width, 0, True)

    def full(self, piece, *rels):
        return [(piece, rel, 0, self.n) for rel in rels]

    def upper(self, piece, *rels):
        return [(piece, rel, self.h, self.h) for rel in rels]

    def lower(self, piece, *rels):
        return [(piece, rel, 0, self.h) for rel in rels]

    def exchange(self, arrays, after=()):
        fresh = [a for a, _ in arrays if a is not self.own]
        (packed,) = pack([[self.part(a, 0, a.shape[0]) for a, _ in arrays]], fresh=fresh, after=after)
        (other,) = made_near([swap(packed)])
        self.note(other, [item for _, items in arrays for item in items], 1)
        return packed, other

    def keep(self, got):
        for array, items in got:
            self.note(array, items)
        return got

    def round1(self):
        self.zq = [hop(self.q, k) for k in ZS]
        self.x1, self.y1 = hop(self.own, X), hop(self.own, Y)
        every = range(4)
        got = [(self.own, [i for p in every for i in self.full(p, 0)])]
        got += [(self.x1, [i for p in every for i in self.full(p, X)])]
        got += [(self.y1, [i for p in every for i in self.full(p, Y)])]
        got += [(z, self.full(0, k)) for z, k in zip(self.zq, ZS)]
        self.got1 = self.keep(got)

    def round2(self, after):
        n, h, part = self.n, self.h, self.part
        along = [part(z, 0, n) for z in self.zq]
        xin, yin, e = pack(
            [along + [part(self.y1, h, h)], along + [part(self.x1, 0, h)], [part(self.own, n, n)]],
            fresh=[*self.zq, self.x1, self.y1],
            after=after,
        )
        x, y, self.ze2 = hop(xin, X), hop(yin, Y), hop(e, Z2)
        self.x, self.y = x, y
        self.got2 = self.keep([
            (x, self.full(0, *(X | k for k in ZS)) + self.upper(0, X | Y)),
            (y, self.full(0, *(Y | k for k in ZS)) + self.lower(0, X | Y)),
            (self.ze2, self.full(1, Z2)),
        ])
        return self.exchange(self.got1, [xin])

    def round3(self, after):
        n, h, part = self.n, self.h, self.part
        xin, yin, e, f = pack(
            [
                [part(self.y, i * n + h, h) for i in range(3)] + [part(self.y1, p * n + h, h) for p in (1, 2)],
                [part(self.x, i * n, h) for i in range(3)] + [part(self.x1, p * n, h) for p in (1, 2)],
                [part(self.own, n, n), part(self.ze2, 0, n)],
                [part(self.own, 2 * n, n)],
            ],
            fresh=[self.x, self.y, self.ze2],
            after=after,
        )
        x, y, self.ze1, self.zf2 = hop(xin, X), hop(yin, Y), hop(e, Z1), hop(f, Z2)
        self.x, self.y = x, y
        both = [X | Y | k for k in ZS]
        self.got3 = self.keep([
            (x, self.upper(0, *both) + self.upper(1, X | Y) + self.upper(2, X | Y)),
            (y, self.lower(0, *both) + self.lower(1, X | Y) + self.lower(2, X | Y)),
        ])
        self.late3 = self.keep([(self.ze1, self.full(1, Z1, Z3)), (self.zf2, self.full(2, Z2))])
        return self.exchange(self.got2, [xin])

    def round4(self, after):
        n, h, part = self.n, self.h, self.part
        along = [part(self.ze1, 0, n), part(self.ze2, 0, n), part(self.ze1, n, n)]
        xin, yin, f, g = pack(
            [
                along + [part(self.y1, 3 * n + h, h)],
                along + [part(self.x1, 3 * n, h)],
                [part(self.own, 2 * n, n), part(self.zf2, 0, n)],
                [part(self.own, 3 * n, n)],
            ],
            fresh=[self.ze1, self.zf2],
            after=after,
        )
        x, y, self.zf1, self.zg2 = hop(xin, X), hop(yin, Y), hop(f, Z1), hop(g, Z2)
        self.x, self.y = x, y
        self.got4 = self.keep([
            (x, self.full(1, *(X | k for k in ZS)) + self.upper(3, X | Y)),
            (y, self.full(1, *(Y | k for k in ZS)) + self.lower(3, X | Y)),
            (self.zf1, self.full(2, Z1, Z3)),
            (self.zg2, self.full(3, Z2)),
        ])
        return self.exchange(self.got3, [xin])

    def round5(self, after):
        n, h, part = self.n, self.h, self.part
        along = [part(self.zf1, 0, n), part(self.zf2, 0, n), part(self.zf1, n, n)]
        xin, yin, g, d = pack(
            [
                [part(self.y, i * n + h, h) for i in range(3)] + along,
                [part(self.x, i * n, h) for i in range(3)] + along,
                [part(self.own, 3 * n, n), part(self.zg2, 0, n)],
                [part(self.y, 3 * n, h), part(self.x, 3 * n, h)],
            ],
            fresh=[self.x, self.y, self.zf1, self.zg2],
            after=after,
        )
        self.d = d
        x, y, self.zg1, self.zd2 = hop(xin, X), hop(yin, Y), hop(g, Z1), hop(d, Z2)
        self.x, self.y = x, y
        both = [X | Y | k for k in ZS]
        self.got5 = self.keep([
            (x, self.upper(1, *both) + self.full(2, *(X | k for k in ZS))),
            (y, self.lower(1, *both) + self.full(2, *(Y | k for k in ZS))),
            (self.zg1, self.full(3, Z1, Z3)),
            (self.zd2, self.full(3, X | Y | Z2)),
        ])
        return self.exchange(self.late3 + self.got4, [xin])

    def round6(self, after):
        n, h, part = self.n, self.h, self.part
        along = [part(self.zg1, 0, n), part(self.zg2, 0, n), part(self.zg1, n, n)]
        xin, yin, d = pack(
            [
                [part(self.y, 3 * h + i * n + h, h) for i in range(3)] + along,
                [part(self.x, 3 * h + i * n, h) for i in range(3)] + along,
                [part(self.d, 0, n), part(self.zd2, 0, n)],
            ],
            fresh=[self.x, self.y, self.zg1, self.zd2],
            after=after,
        )
        x, y, zd1 = hop(xin, X), hop(yin, Y), hop(d, Z1)
        both = [X | Y | k for k in ZS]
        self.got6 = self.keep([
            (x, self.upper(2, *both) + self.full(3, *(X | k for k in ZS))),
            (y, self.lower(2, *both) + self.full(3, *(Y | k for k in ZS))),
            (zd1, self.full(3, X | Y | Z1, X | Y | Z3)),
        ])
        return self.exchange(self.got5, [xin])

    def last(self, after):
        return self.exchange(self.got6, after)


class GatherPlain:
    def __init__(self, w_qkv, w_out, w_up, w_down):
        local = jnp.concatenate([w_qkv[0], w_qkv[1], w_qkv[2], w_out.T, w_up, w_down.T], axis=1)
        rows, width = local.shape
        whole = lax.all_gather(local, ("dp", "tensor")).reshape(lax.axis_size("dp"), 2, rows, width)
        self.pieces = [Piece(0, width, None, 0, 0, whole, 0, other) for other in range(2)]
        self.gate = None

    def round1(self):
        return None

    def round2(self, after):
        return None, None

    round3 = round4 = round5 = round6 = last = round2


class Spot:
    def __init__(self, array, row, rows, col, cols):
        self.array, self.row, self.rows, self.col, self.cols = array, row, rows, col, cols

    def of(self, ref, me, t):
        at = lambda v, unit: pl.multiple_of(v(me, t), unit) if callable(v) else v
        return ref.at[pl.ds(at(self.row, 16), self.rows), pl.ds(at(self.col, 128), self.cols)]


def arrange(where, shapes, moves, fresh=(), after=()):
    after_specs, after = waits(after)
    arrays = []
    for source, _, _ in moves:
        if not any(a is source.array for a in arrays):
            arrays.append(source.array)
    near = [any(a is f for f in fresh) for a in arrays]
    number = lambda array: next(i for i, a in enumerate(arrays) if a is array)
    plan = [(number(source.array), source, out, target) for source, out, target in moves]

    def kernel(where_ref, *refs):
        ins, results, sems = refs[: len(arrays)], refs[len(arrays) + len(after) : -1], refs[-1]
        me, t = where_ref[0], where_ref[1]
        copies = []
        for index, (slot, source, out, target) in enumerate(plan):
            copy = pltpu.make_async_copy(
                source.of(ins[slot], me, t), target.of(results[out], me, t), sems.at[index]
            )
            copy.start()
            copies.append(copy)
        for copy in copies:
            copy.wait()

    spaces = [pltpu.VMEM if n else pltpu.HBM for n in near]
    return made_near(pl.pallas_call(
        kernel,
        in_specs=[pl.BlockSpec(memory_space=pltpu.SMEM)]
        + [pl.BlockSpec(memory_space=m) for m in spaces]
        + after_specs,
        out_specs=[pl.BlockSpec(memory_space=pltpu.VMEM)] * len(shapes),
        out_shape=[pltpu.VMEM(shape, BF) for shape in shapes],
        scratch_shapes=[pltpu.SemaphoreType.DMA((len(plan),))],
        compiler_params=pltpu.CompilerParams(vmem_limit_bytes=8 * 2**20),
        cost_estimate=pl.CostEstimate(
            flops=0, bytes_accessed=sum(h * w * 4 for h, w in shapes), transcendentals=0
        ),
    )(where, *[pltpu.with_memory_space_constraint(a, m) for a, m in zip(arrays, spaces)], *after))


class GradientSum:
    def __init__(self, where, array, widths, mine, rank, adapters, picks):
        self.where, self.array, self.picks = where, array, picks
        self.mine, self.rank, self.adapters = mine, rank, adapters
        self.rows = mine * rank
        self.widths = widths
        self.starts = [sum(widths[:i]) for i in range(len(widths))]
        self.chunk = sum(widths) // 8

    def cores(self, after=()):
        half = 4 * self.chunk
        source = Spot(self.array, 0, self.rows, lambda me, t: (1 - t) * half, half)
        moves = [(source, 0, Spot(None, 0, self.rows, 0, half))]
        (out,) = arrange(self.where, [(self.rows, half)], moves, after=after)
        self.other = swap(out)
        return out

    def plane(self, after=()):
        rows, chunk = self.rows, self.chunk
        moves = []
        for k in range(4):
            mine = Spot(self.array, 0, rows, lambda me, t, k=k: (t * 4 + ((me & 3) ^ k)) * chunk, chunk)
            theirs = Spot(self.other, 0, rows, lambda me, t, k=k: ((me & 3) ^ k) * chunk, chunk)
            moves += [
                (mine, k, Spot(None, 0, rows, 0, chunk)),
                (theirs, k, Spot(None, rows, rows, 0, chunk)),
                (Spot(self.picks, 0, self.rank, 0, chunk), k, Spot(None, 2 * rows, self.rank, 0, chunk)),
            ]
        shape = (2 * rows + self.rank, chunk)
        outs = arrange(self.where, [shape] * 4, moves, fresh=[self.other], after=after)
        self.parts = [outs[0], hop(outs[1], X), hop(outs[2], Y), hop(outs[3], X | Y)]
        return outs[0]

    def fold(self, after=()):
        rank, chunk, data = self.rank, self.chunk, 2 * self.rows
        tall = self.adapters * rank
        quarter = tall // 4

        def kernel(where_ref, *refs):
            ins, outs, total = refs[:4], refs[-5:-1], refs[-1]
            z = where_ref[0] // 4
            row = lax.broadcasted_iota(jnp.int32, (tall, data), 0)
            col = lax.broadcasted_iota(jnp.int32, (tall, data), 1)
            adapter = (row // rank).astype(F32)
            same_row = row % rank == col % rank
            for k in range(4):
                picks = ins[k][data : data + 1, 0:data].astype(F32)
                chosen = jnp.logical_and(adapter == picks, same_row).astype(F32).astype(BF)
                part = nn(chosen, ins[k][0:data, :])
                total[...] = part if k == 0 else total[...] + part
            for k in range(4):
                rows = pl.ds(pl.multiple_of((z ^ k) * quarter, quarter), quarter)
                outs[k][...] = total[rows, :].astype(BF)

        outs = self.local(kernel, self.parts, after, [(quarter, chunk)] * 4, [(tall, chunk)])
        self.parts = [outs[0]] + [hop(outs[k], 4 * k) for k in (1, 2, 3)]
        return outs[0]

    def local(self, kernel, arrays, after, shapes, scratch):
        after_specs, after = waits(after)
        vmem = pl.BlockSpec(memory_space=pltpu.VMEM)
        return made_near(pl.pallas_call(
            kernel,
            in_specs=[pl.BlockSpec(memory_space=pltpu.SMEM)] + [vmem] * len(arrays) + after_specs,
            out_specs=[vmem] * len(shapes),
            out_shape=[pltpu.VMEM(shape, BF) for shape in shapes],
            scratch_shapes=[pltpu.VMEM(shape, F32) for shape in scratch],
            compiler_params=pltpu.CompilerParams(vmem_limit_bytes=12 * 2**20),
            cost_estimate=pl.CostEstimate(
                flops=0, bytes_accessed=sum(h * w * 8 for h, w in shapes), transcendentals=0
            ),
        )(
            self.where,
            *[pltpu.with_memory_space_constraint(a, pltpu.VMEM) for a in arrays],
            *after,
        ))

    def depth(self, after=()):
        def kernel(where_ref, *refs):
            total = refs[0][...].astype(F32)
            for ref in refs[1:4]:
                total += ref[...].astype(F32)
            refs[-1][...] = total.astype(BF)

        (out,) = self.local(kernel, self.parts, after, [self.parts[0].shape], [])
        self.parts = [out] + [hop(out, 4 * k) for k in (1, 2, 3)]
        return out

    def back(self, after=()):
        tall = self.adapters * self.rank
        quarter, side = tall // 4, self.chunk // 2
        moves = [
            (
                Spot(self.parts[k], 0, quarter, part * side, side),
                part,
                Spot(None, lambda me, t, k=k: ((me >> 2) ^ k) * quarter, quarter, 0, side),
            )
            for k in range(4)
            for part in range(2)
        ]
        self.a, self.b = arrange(self.where, [(tall, side)] * 2, moves, fresh=self.parts, after=after)
        self.xa, self.yb = hop(self.a, X), hop(self.b, Y)
        return self.a

    def spread(self, after=()):
        tall, side = self.adapters * self.rank, self.chunk // 2
        moves = [
            (Spot(source, 0, tall, 0, side), out, Spot(None, row * tall, tall, 0, side))
            for out, pair in enumerate(((self.a, self.xa), (self.b, self.yb)))
            for row, source in enumerate(pair)
        ]
        fresh = [self.a, self.b, self.xa, self.yb]
        up, down = arrange(self.where, [(2 * tall, side)] * 2, moves, fresh=fresh, after=after)
        self.ya, self.xb = hop(up, Y), hop(down, X)
        return up

    def give(self, after=()):
        tall, side = self.adapters * self.rank, self.chunk // 2
        sources = [
            ((self.a, 0), (self.b, 0)),
            ((self.xa, 0), (self.xb, 0)),
            ((self.ya, 0), (self.yb, 0)),
            ((self.ya, tall), (self.xb, tall)),
        ]
        moves = [
            (Spot(source, row, tall, 0, side), 0, Spot(None, k * tall, tall, part * side, side))
            for k, both in enumerate(sources)
            for part, (source, row) in enumerate(both)
        ]
        fresh = [self.a, self.b, self.xa, self.yb, self.ya, self.xb]
        (out,) = arrange(self.where, [(4 * tall, self.chunk)], moves, fresh=fresh, after=after)
        self.theirs = swap(out)
        self.ours = out
        return out


def finish(where, sums, results, after=()):
    tall = sums[0].adapters * sums[0].rank
    after_specs, after = waits(after)
    inputs = [a for s in sums for a in (s.ours, s.theirs)]

    def kernel(where_ref, *refs):
        outs = refs[len(inputs) + len(after) :]
        me, t = where_ref[0], where_ref[1]
        for out, parts in zip(outs, results):
            for place, (number, which) in enumerate(parts):
                total = sums[number]
                start, width = total.starts[which] // 8, total.widths[which] // 8
                for core in range(2):
                    for k in range(4):
                        column = ((t ^ core) * 4 + ((me & 3) ^ k)) * width
                        out[place * tall : (place + 1) * tall, pl.ds(pl.multiple_of(column, 128), width)] = refs[
                            2 * number + core
                        ][k * tall : (k + 1) * tall, start : start + width].astype(F32)

    vmem = pl.BlockSpec(memory_space=pltpu.VMEM)
    shapes = [(len(parts) * tall, sums[parts[0][0]].widths[parts[0][1]]) for parts in results]
    return pl.pallas_call(
        kernel,
        in_specs=[pl.BlockSpec(memory_space=pltpu.SMEM)]
        + [vmem] * len(inputs)
        + after_specs,
        out_specs=[vmem] * len(results),
        out_shape=[pltpu.HBM(shape, F32) for shape in shapes],
        compiler_params=pltpu.CompilerParams(vmem_limit_bytes=32 * 2**20),
        cost_estimate=pl.CostEstimate(
            flops=0, bytes_accessed=sum(h * w * 6 for h, w in shapes), transcendentals=0
        ),
    )(where, *inputs, *after)


def hold(array, after):
    after_specs, after = waits(after)
    return pl.pallas_call(
        lambda *refs: None,
        in_specs=after_specs + [pl.BlockSpec(memory_space=pltpu.HBM)],
        out_specs=pl.BlockSpec(memory_space=pltpu.HBM),
        out_shape=pltpu.HBM(array.shape, array.dtype),
        input_output_aliases={len(after): 0},
        cost_estimate=pl.CostEstimate(flops=0, bytes_accessed=0, transcendentals=0),
    )(*after, in_hbm(array))


def place(where, filled, arrived, after=()):
    after_specs, after = waits(after)
    mine, rows, width = arrived.shape

    def kernel(where_ref, arrived_ref, *refs):
        refs[-1][...] = arrived_ref[...]

    return pl.pallas_call(
        kernel,
        grid_spec=pltpu.PrefetchScalarGridSpec(
            num_scalar_prefetch=1,
            grid=(mine,),
            in_specs=[pl.BlockSpec((1, rows, width), lambda s, w: (s, 0, 0))]
            + after_specs
            + [pl.BlockSpec(memory_space=pltpu.HBM)],
            out_specs=pl.BlockSpec((1, rows, width), lambda s, w: ((1 - w[1]) * mine + s, 0, 0)),
        ),
        out_shape=pltpu.HBM(filled.shape, filled.dtype),
        input_output_aliases={2 + len(after): 0},
        **params(1, 2 * arrived.size * arrived.dtype.itemsize, 16 * 2**20),
    )(where, in_hbm(arrived), *after, in_hbm(filled))


def shards(
    hidden_in, segment_ids, adapter_pick, w_qkv, w_out, w_up, w_down, ln_gain, ln_bias,
    adapt_a, adapt_b, up_a, up_b, down_a, down_b, grad_out,
):
    dp = lax.axis_size("dp")
    t = lax.axis_index("tensor")
    block, ff_half = w_up.shape
    width = hidden_in.shape[2]
    half = width // 2
    ff = 2 * ff_half
    positions = hidden_in.shape[1]
    length = 2 * positions
    mine = hidden_in.shape[0] // 2
    rank = adapt_b.shape[2]
    adapters = adapt_b.shape[1]

    NEAR.clear()
    pick = lax.dynamic_slice_in_dim(adapter_pick, mine * t, mine, 0)
    where = jnp.stack([lax.axis_index("dp"), t]).astype(pick.dtype)
    meta = jnp.concatenate([pick, where])
    ordered = jnp.where(t == 0, adapter_pick, jnp.roll(adapter_pick, -mine))
    picks = jnp.repeat(ordered, rank).astype(BF)
    picks = jnp.broadcast_to(jnp.pad(picks, (0, 3 * half - picks.shape[0]))[None], (rank, 3 * half))
    segs = lax.dynamic_slice_in_dim(segment_ids, mine * t, mine, 0)
    seg_col = segs.reshape(mine, length, 1)
    seg_row = segs.reshape(mine, 1, length)

    sent_rows = mine * positions

    def send_half(value, after):
        flat = value.reshape(2 * sent_rows, width)
        spot = Spot(flat, lambda me, t: (1 - t) * sent_rows, sent_rows, 0, width)
        (out,) = arrange(where, [(sent_rows, width)], [(spot, 0, Spot(None, 0, sent_rows, 0, width))], after=after)
        return flat, out, swap(out)

    def join(flat, there, after):
        moves = []
        for s in range(mine):
            moves.append((
                Spot(flat, lambda me, t, s=s: (t * mine + s) * positions, positions, 0, width), 0,
                Spot(None, lambda me, t, s=s: s * length + t * positions, positions, 0, width),
            ))
            moves.append((
                Spot(there, s * positions, positions, 0, width), 0,
                Spot(None, lambda me, t, s=s: s * length + (1 - t) * positions, positions, 0, width),
            ))
        (out,) = arrange(where, [(mine * length, width)], moves, fresh=[there], after=after)
        return out.reshape(mine, length, width), out

    gather = (Gather if dp == 16 else GatherPlain)(w_qkv, w_out, w_up, w_down)
    gather.round1()
    def columns(first, count):
        return (gather.pieces, first, count, dp, block)

    qkv_w = columns(0, 3 * half)
    out_w = columns(3 * half, half)
    part = 2 * half
    up_parts = [columns(4 * half + p, part) for p in range(0, ff_half, part)]
    up_w = columns(4 * half, ff_half)
    down_w = columns(4 * half + ff_half, ff_half)

    a_t = jnp.swapaxes(adapt_a, 2, 3)
    ua_t = jnp.swapaxes(up_a, 1, 2)
    da_t = jnp.swapaxes(down_a, 1, 2)

    flat_x, gate, there_x = send_half(hidden_in, [gather.gate])
    flat_c, gate, there_c = send_half(grad_out, [gate])
    gate, met = gather.round2([meta, seg_col, seg_row, picks, gate])
    x, gate = join(flat_x, there_x, [gate])
    cotangent, gate = join(flat_c, there_c, [gate])
    _, met = gather.round3([met, gate])
    gate, _ = gather.round4([met])
    tokens = mine * length
    tiles = 2
    tile = length // tiles
    seq3 = lambda s, i, m: (s, 0, 0)
    row3 = lambda s, i, m: (s, i, 0)
    fixed2 = lambda s, i, m: (0, 0)
    picked3 = lambda s, i, m: (m[s], 0, 0)
    slots4 = lambda s, i, m: (0, m[s], 0, 0)
    last4 = lambda s, i, m: (3, m[s], 0, 0)
    full = lambda a: (a, (1, *a.shape[1:]), seq3)
    row = lambda a: (a, (1, tile, a.shape[2]), row3)
    across = lambda a: (a, (1, a.shape[1], tile), lambda s, i, m: (s, 0, i))
    whole = lambda a: (a, a.shape, fixed2)
    factor = lambda a: (a, (1, *a.shape[1:]), picked3)
    slots = lambda a: (a, (a.shape[0], 1, *a.shape[2:]), slots4)
    last = lambda a: (a, (1, 1, *a.shape[2:]), last4)
    rows_made = lambda dtype, cols: ((mine, length, cols), dtype, (1, tile, cols), row3)
    across_made = lambda rows: ((mine, rows, length), BF, (1, rows, tile), lambda s, i, m: (s, 0, i))
    def kept_made(dtype):
        block = (1, positions, width)
        return [
            ((2 * mine, positions, width), dtype, block, lambda s, i, m: (m[mine + 1] * mine + s, 0, 0)),
            ((mine, positions, width), dtype, block, seq3),
        ]

    sum_made = lambda rows, cols: ((mine, rows, cols), BF, (1, rows, cols), seq3)

    qkv, rank_qkv, whole_qkv = call(
        qkv_kernel, meta,
        [row(x), slots(a_t), slots(adapt_b)],
        [((mine, 3, length, width), BF, (1, 3, tile, width), lambda s, i, m: (s, 0, i, 0)),
         across_made(3 * rank)],
        6 * tokens * width * width,
        weights=[qkv_w],
        after=[gate],
        limit=24 * 2**20,
        tiles=tiles,
        saves=[(0, 3 * half, 0, None)],
    )
    gate, met = gather.round5([qkv])

    groups = width // GROUP

    def heads_of(slot, first, group=0):
        return pl.BlockSpec((1, 1, length, GROUP), lambda s, h: (s + first, slot, 0, h + group))

    def seg_specs(first):
        return [
            pl.BlockSpec((1, length, 1), lambda s, h: (s + first, 0, 0)),
            pl.BlockSpec((1, 1, length), lambda s, h: (s + first, 0, 0)),
        ]

    def lse_at(first, group=0):
        return pl.BlockSpec((1, 1, 8, length), lambda s, h: (s + first, h + group, 0, 0))

    def heads_at(first, group=0):
        return pl.BlockSpec((1, length, GROUP), lambda s, h: (s + first, 0, h + group))

    after_specs, after = waits([gate])
    attention, lse = pl.pallas_call(
        lambda q, k, v, sc, sr, *refs: attend_kernel(q, k, v, sc, sr, *refs[len(after) :]),
        grid=(mine, groups),
        in_specs=[heads_of(j, 0) for j in range(3)] + seg_specs(0) + after_specs,
        out_specs=[heads_at(0), lse_at(0)],
        out_shape=[
            pltpu.HBM((mine, length, width), BF),
            pltpu.HBM((mine, groups, 8, length), F32),
        ],
        **params(16 * tokens * length * width, tokens * width * 8, 16 * 2**20),
    )(*[in_hbm(a) for a in [qkv, qkv, qkv, seg_col, seg_row]], *after)
    gate, _ = gather.round6([lse, met])

    normed, inverse, middle_low, rank_out, whole_out = call(
        out_kernel, meta,
        [row(attention), row(x), last(a_t), last(adapt_b), whole(ln_gain), whole(ln_bias)],
        [rows_made(F32, width), rows_made(F32, 128), rows_made(BF, width), across_made(rank)],
        2 * tokens * width * width,
        scratch=[pltpu.VMEM((tile, width), F32)],
        weights=[out_w],
        limit=18 * 2**20,
        after=[gate],
        tiles=tiles,
        stays=[0],
    )

    gate = rank_out
    blocks = ff_half // part
    made_up, whole_up = [], []
    for index, weight in enumerate(up_parts):
        up_cols = [
            (up_b, (1, rank, part), lambda s, i, m, at=h * blocks + index: (m[s], 0, at)) for h in range(2)
        ]
        units_made = (
            (mine, 2, length, ff_half), BF, (1, 2, tile, part), lambda s, i, m, index=index: (s, 0, i, index)
        )
        last_part = index == len(up_parts) - 1
        made = call(
            up_kernel, meta,
            [row(middle_low), factor(ua_t), *up_cols],
            [units_made, units_made, across_made(rank)],
            4 * tokens * width * part * 2,
            weights=[weight, down_w] if last_part else [weight],
            limit=18 * 2**20,
            after=[gate],
            tiles=tiles,
            filled=made_up,
            stays=list(range(1 + last_part)),
        )
        *made_up, rank_up = made[:3]
        gate = rank_up
        whole_up.append(made[3])
        if last_part:
            whole_down = made[4]
        elif index == 0:
            gate, _ = gather.last([rank_up])
    units = lambda a: (a, (1, 2, tile, ff_half), lambda s, i, m: (s, 0, i, 0))
    act, slope = made_up

    layer_out, layer_sent, grad_first, grad_att, sooner = call(
        middle_kernel, meta,
        [units(act), units(slope), row(normed), row(inverse), row(cotangent), row(middle_low), row(attention),
         across(rank_up), across(rank_out), factor(da_t), factor(down_b), factor(ua_t), factor(up_b),
         last(a_t), last(adapt_b), whole(ln_gain), whole(ln_bias)],
        [*kept_made(BF), rows_made(F32, width), rows_made(BF, width),
         sum_made(rank, 2 * ff + 4 * width)],
        tokens * width * (6 * ff + 2 * width),
        scratch=[pltpu.VMEM((tile, width), F32), pltpu.VMEM((tile, width), F32), pltpu.VMEM((tile, width), BF),
                 pltpu.VMEM((tile, ff), BF), pltpu.VMEM((tile, width), BF),
                 pltpu.VMEM((rank, ff), F32), pltpu.VMEM((rank, width), F32),
                 pltpu.VMEM((rank, width), F32), pltpu.VMEM((rank, ff), F32),
                 pltpu.VMEM((rank, width), F32), pltpu.VMEM((rank, width), F32)],
        tiles=tiles,
        held=[whole_down, *whole_up, whole_out],
        limit=34 * 2**20,
    )

    layer_there = swap(layer_sent)
    flat = lambda g: g.reshape(mine * rank, g.shape[-1])
    sooner_widths = [ff, width, width, ff, width, width]
    later_widths = [width] * 6
    fast = dp == 16
    gate = None
    if fast:
        first_sum = GradientSum(where, flat(sooner), sooner_widths, mine, rank, adapters, picks)
        gate = first_sum.cores()

    halves = 2
    span = groups // halves

    def attend_back(first, group, made, after):
        after_specs, after = waits(after)
        extra = len(made) + len(after)

        def body(q, k, v, sc, sr, l, o, do, *refs):
            attend_back_kernel(q, k, v, sc, sr, l, o, do, *refs[extra:])

        args = [qkv, qkv, qkv, seg_col, seg_row, lse, attention, grad_att, *made]
        return pl.pallas_call(
            body,
            grid=(1, span),
            in_specs=[heads_of(j, first, group) for j in range(3)]
            + seg_specs(first)
            + [lse_at(first, group), heads_at(first, group), heads_at(first, group)]
            + [pl.BlockSpec(memory_space=pltpu.HBM) for _ in made]
            + after_specs,
            out_specs=[heads_at(first, group)] * 3,
            out_shape=[pltpu.HBM((mine, length, width), BF)] * 3,
            input_output_aliases={8 + i: i for i in range(len(made))},
            **params(40 * length * length * width // halves, length * width * 16, 32 * 2**20),
        )(*[in_hbm(a) for a in args], *after)

    grads_qkv = []
    between = iter([first_sum.plane, first_sum.fold, first_sum.depth, first_sum.back] if fast else [])
    for index in range(mine):
        for group in range(0, groups, span):
            grads_qkv = attend_back(index, group, grads_qkv, [gate])
            gate = None
            phase = next(between, None)
            if phase is not None and (index, group) != (mine - 1, groups - span):
                gate = phase([grads_qkv[0]])
    gate = first_sum.back([grads_qkv[0]]) if fast else None

    grad_rank, later = call(
        rank_back_kernel, meta,
        [full(g) for g in grads_qkv] + [full(x), full(rank_qkv), slots(adapt_b)],
        [sum_made(3 * rank, length), sum_made(rank, 6 * width)],
        18 * tokens * width * rank,
        after=[gate],
        limit=32 * 2**20,
    )
    gate = grad_rank
    if fast:
        second_sum = GradientSum(where, flat(later), later_widths, mine, rank, adapters, picks)
        gate = second_sum.cores([gate])
        gate = first_sum.spread([gate])
        gate = second_sum.plane([gate])

    grad_in, grad_sent = call(
        qkv_back_kernel, meta,
        [row(g) for g in grads_qkv] + [across(grad_rank), row(grad_first), slots(a_t)],
        kept_made(F32),
        6 * tokens * width * width,
        held=[whole_qkv],
        after=[gate],
        limit=40 * 2**20,
        tiles=tiles,
    )
    turned = lambda v: jnp.swapaxes(v, -1, -2)
    if fast:
        gate = second_sum.fold([grad_in])
        gate = first_sum.give([gate])
        layer_out = place(where, layer_out, layer_there, [gate])
        gate = second_sum.depth([layer_out])
        there = swap(hold(grad_sent, [gate]))
        done1 = finish(where, [first_sum], [[(0, 0)], [(0, 1)], [(0, 2)], [(0, 3)]], [gate])
        gate = second_sum.back([done1[0]])
        grad_in = place(where, grad_in, there, [gate])
        gate = second_sum.spread([grad_in])
        second_sum.give([gate])
        all_a, all_b = finish(
            where, [second_sum, first_sum],
            [[(0, 0), (0, 1), (0, 2), (1, 4)], [(0, 3), (0, 4), (0, 5), (1, 5)]],
        )
        shaped = lambda v: v.reshape(-1, adapters, rank, v.shape[1])
        da, db, ua, ub = (shaped(v)[0] for v in done1)
        return (layer_out, grad_in, turned(shaped(all_a)), shaped(all_b), turned(ua), ub, turned(da), db)

    layer_out = place(where, layer_out, layer_there)
    grad_in = place(where, grad_in, swap(grad_sent))
    onehot = (pick[:, None] == jnp.arange(adapters)[None, :]).astype(F32)

    def fold(per_sequence):
        total = onehot[0][:, None, None] * per_sequence[0][None].astype(F32)
        for index in range(1, mine):
            total += onehot[index][:, None, None] * per_sequence[index][None].astype(F32)
        return total

    def apart(array, widths):
        chunks, at, parts = array.reshape(mine, rank, 8, -1), 0, []
        for columns_of in widths:
            part = chunks[..., at : at + columns_of // 8]
            parts.append(part.reshape(mine, rank, columns_of))
            at += columns_of // 8
        return parts

    g_down_a, g_down_b, g_up_a, g_up_b, g_out_a, g_out_b = apart(sooner, sooner_widths)
    qkv_sums = apart(later, later_widths)
    sums = lax.psum(
        tuple(
            fold(g)
            for g in [*qkv_sums[:3], g_out_a, *qkv_sums[3:], g_out_b, g_up_a, g_up_b, g_down_a, g_down_b]
        ),
        ("dp", "tensor"),
    )
    return (
        layer_out,
        grad_in,
        turned(jnp.stack(sums[:4])),
        jnp.stack(sums[4:8]),
        turned(sums[8]),
        sums[9],
        turned(sums[10]),
        sums[11],
    )


def solution(mesh):
    placed = (
        P("dp", "tensor", None),
        P("dp", None),
        P("dp"),
        P(None, "dp", "tensor"),
        P("tensor", "dp"),
        P("dp", "tensor"),
        P("tensor", "dp"),
        P(),
        P(),
        P(),
        P(),
        P(),
        P(),
        P(),
        P(),
        P("dp", "tensor", None),
    )
    return jax.shard_map(
        shards,
        mesh=mesh,
        in_specs=placed,
        out_specs=(P("dp", "tensor", None), P("dp", "tensor", None), P(), P(), P(), P(), P(), P()),
        check_vma=False,
    )
```

```python
import functools

import jax
import jax.numpy as jnp
from jax import lax
from jax.experimental import pallas as pl
from jax.experimental.pallas import tpu as pltpu
from jax.sharding import PartitionSpec as P

HEAD_DIM = 64
BF = jnp.bfloat16
F32 = jnp.float32
LOG2E = 1.4426950408889634
VMEM = 60 * 2**20


def nn(a, b):
    return lax.dot_general(a, b, (((1,), (0,)), ((), ())), preferred_element_type=F32)


def nt(a, b):
    return lax.dot_general(a, b, (((1,), (1,)), ((), ())), preferred_element_type=F32)


def tn(a, b):
    return lax.dot_general(a, b, (((0,), (0,)), ((), ())), preferred_element_type=F32)


def params(flops, nbytes, limit=VMEM):
    return dict(
        compiler_params=pltpu.CompilerParams(vmem_limit_bytes=limit),
        cost_estimate=pl.CostEstimate(flops=flops, bytes_accessed=nbytes, transcendentals=0),
    )


class Piece:
    def __init__(self, col, width, rel, row, count, array, at, other):
        self.col, self.width, self.rel, self.row = col, width, rel, row
        self.count, self.array, self.at, self.other = count, array, at, other


def first_tile():
    return jnp.logical_and(pl.program_id(0) == 0, pl.program_id(1) == 0)


class Loader:
    def __init__(self, plan, refs, scratch, sems, me, t, dp):
        self.plan, self.refs, self.scratch, self.sems = plan, refs, scratch, sems
        self.me, self.t, self.dp = me, t, dp
        self.saved = None
        self.width = scratch.shape[1] // 2
        self.block = scratch.shape[0] // dp

    def start(self):
        def copy(source, block, row, count, into, width, other):
            rows = pl.ds(pl.multiple_of(block * self.block + row, 16), count)
            cols = pl.ds(pl.multiple_of((self.t ^ other) * self.width + into, 128), width)
            pltpu.make_async_copy(source, self.scratch.at[rows, cols], self.sems.at[other]).start()

        for slot, at, count, col, width, other, rel, row, into in self.plan:
            cols = pl.ds(col, width)
            if rel is None:
                for block in range(self.dp):
                    source = self.refs[slot].at[block, self.t ^ other, :, cols]
                    copy(source, block, 0, self.block, into, width, other)
            else:
                copy(self.refs[slot].at[pl.ds(at, count), cols], self.me ^ rel, row, count, into, width, other)

    def wait(self, other):
        cols = pl.ds(pl.multiple_of((self.t ^ other) * self.width, 128), self.width)
        whole = self.scratch.at[:, cols]
        pltpu.make_async_copy(whole, whole, self.sems.at[other]).wait()

    def first_step(self):
        pl.when(first_tile())(self.start)

    def first_wait(self, other):
        pl.when(first_tile())(lambda: self.wait(other))

    def first_wait_all(self):
        @pl.when(first_tile())
        def _():
            self.wait(0)
            self.wait(1)
            if self.saved is not None:
                for copy in self.save_copies():
                    copy.start()

    def save_copies(self):
        ref, first, sems = self.saved
        half = ref.shape[1] // 2
        return [
            pltpu.make_async_copy(
                self.scratch.at[:, pl.ds(h * self.width, self.width)],
                ref.at[:, pl.ds(h * half + first, self.width)],
                sems.at[h],
            )
            for h in range(2)
        ]

    def cols(self, half, lo, width):
        at = half * self.width + lo
        return self.scratch[:, pl.ds(at if isinstance(at, int) else pl.multiple_of(at, 128), width)]


class Held:
    def __init__(self, ref):
        self.scratch, self.width = ref, ref.shape[1] // 2

    cols = Loader.cols


def weight_plan(pieces, first, width):
    arrays, plan = [], []
    for p in pieces:
        lo, hi = max(p.col, first), min(p.col + p.width, first + width)
        if lo >= hi:
            continue
        slot = next((i for i, a in enumerate(arrays) if a is p.array), None)
        if slot is None:
            slot = len(arrays)
            arrays.append(p.array)
        plan.append((slot, p.at, p.count, lo - p.col, hi - lo, p.other, p.rel, p.row, lo - first))
    return arrays, plan


def qkv_kernel(meta, ins, outs, weights, scratch):
    x_ref, a_ref, b_ref = ins
    qkv_ref, rank_ref = outs
    (w,) = weights
    w.first_step()
    w.first_wait_all()
    x = x_ref[0]
    slots, rank_size = rank_ref.shape[1] // a_ref.shape[2], a_ref.shape[2]
    factors = a_ref[0:slots, 0].reshape(slots * rank_size, x.shape[1])
    rank = nt(x, factors)
    rank_ref[0] = rank.T.astype(BF)
    rank = rank.astype(BF)
    width = w.width // slots
    for half in range(2):
        cols = slice(half * width, (half + 1) * width)
        for slot in range(slots):
            mine = rank[:, slot * rank_size : (slot + 1) * rank_size]
            full = nn(x, w.cols(half, slot * width, width)) + nn(mine, b_ref[slot, 0, :, cols])
            qkv_ref[0, slot, :, cols] = full.astype(BF)


SCALE = HEAD_DIM**-0.5
SCALE2 = SCALE * LOG2E
GROUP = 4 * HEAD_DIM


def one_head(lane, head, value):
    return jnp.where(lane // HEAD_DIM == head, value, jnp.zeros((), value.dtype))


def attend_kernel(q_ref, k_ref, v_ref, segc_ref, segr_ref, out_ref, lse_ref):
    q, k, v = q_ref[0, 0], k_ref[0, 0], v_ref[0, 0]
    length, lanes = q.shape
    heads = lanes // HEAD_DIM
    lane = lax.broadcasted_iota(jnp.int32, (1, lanes), 1)
    same = segc_ref[0] == segr_ref[0]
    v_t = v.T

    def score(head):
        return nt(one_head(lane, head, k), q)

    mixed = []
    scores = score(0)
    for head in range(heads):
        following = score(head + 1) if head + 1 < heads else None
        masked = jnp.where(same, scores, F32(-1000000000.0 / SCALE))
        peak = jnp.max(masked, axis=0, keepdims=True) * SCALE2
        weights = jnp.exp2(masked * SCALE2 - peak)
        mass = jnp.sum(weights, axis=0, keepdims=True)
        rows = slice(head * HEAD_DIM, (head + 1) * HEAD_DIM)
        mixed.append(nn(v_t[rows, :], weights.astype(BF)) * (1.0 / mass))
        lse_ref[0, 0, head : head + 1, :] = peak + jnp.log2(mass)
        scores = following
    out_ref[0] = jnp.concatenate(mixed, axis=0).astype(BF).T
    lse_ref[0, 0, heads:, :] = jnp.zeros((lse_ref.shape[2] - heads, length), F32)


def attend_back_kernel(
    q_ref, k_ref, v_ref, segc_ref, segr_ref, lse_ref, o_ref, do_ref, gq_ref, gk_ref, gv_ref
):
    q, k, v, do = q_ref[0, 0], k_ref[0, 0], v_ref[0, 0], do_ref[0]
    lanes = q.shape[1]
    lane = lax.broadcasted_iota(jnp.int32, (1, lanes), 1)
    product = do.astype(F32) * o_ref[0].astype(F32)
    high = product.astype(BF)
    low = (product - high.astype(F32)).astype(BF)
    picker = (
        lax.broadcasted_iota(jnp.int32, (8, lanes), 0)
        == lax.broadcasted_iota(jnp.int32, (8, lanes), 1) // HEAD_DIM
    ).astype(BF)
    inner = nt(picker, high) + nt(picker, low)
    same = segc_ref[0] == segr_ref[0]
    grad_q = grad_k = grad_v = None
    for head in range(lanes // HEAD_DIM):
        k_mine = one_head(lane, head, k)
        masked = jnp.where(same, nt(k_mine, q), F32(-1000000000.0 / SCALE))
        probs = jnp.exp2(masked * SCALE2 - lse_ref[0, 0, head : head + 1, :])
        grad_probs = nt(one_head(lane, head, v), do)
        grad_scores = (probs * (grad_probs - inner[head : head + 1, :])).astype(BF)
        part_v = nn(probs.astype(BF), one_head(lane, head, do))
        part_k = nn(grad_scores, one_head(lane, head, q))
        part_q = tn(grad_scores, k_mine)
        grad_v = part_v if head == 0 else grad_v + part_v
        grad_k = part_k if head == 0 else grad_k + part_k
        grad_q = part_q if head == 0 else grad_q + part_q
    gq_ref[0] = (grad_q * SCALE).astype(BF)
    gk_ref[0] = (grad_k * SCALE).astype(BF)
    gv_ref[0] = grad_v.astype(BF)


def norm_parts(values):
    mean = jnp.mean(values, axis=-1, keepdims=True)
    centred = values - mean
    inverse = lax.rsqrt(jnp.mean(centred * centred, axis=-1, keepdims=True) + 1e-06)
    return centred * inverse, inverse


def norm_back(scaled, normed, inverse):
    mean_grad = jnp.mean(scaled, axis=-1, keepdims=True)
    mean_proj = jnp.mean(scaled * normed, axis=-1, keepdims=True)
    return (scaled - mean_grad - normed * mean_proj) * inverse


ROWS = 64


def by_rows(count, step):
    for row in range(0, count, ROWS):
        step(slice(row, row + ROWS))


def out_kernel(meta, ins, outs, weights, scratch):
    att_ref, x_ref, a_ref, b_ref, gain_ref, bias_ref = ins
    normed_ref, inverse_ref, low_ref, rank_ref = outs
    (w,) = weights
    (v_scr,) = scratch
    w.first_step()
    w.first_wait_all()
    att = att_ref[0]
    rank = nt(att, a_ref[0, 0])
    rank_ref[0] = rank.T.astype(BF)
    rank = rank.astype(BF)
    width = w.width
    v_scr[...] = (
        nt(att[:, :width], w.cols(0, 0, width))
        + nt(att[:, width:], w.cols(1, 0, width))
        + nn(rank, b_ref[0, 0])
    )

    def step(rows):
        normed, inverse = norm_parts(v_scr[rows, :] + x_ref[0, rows, :].astype(F32))
        normed_ref[0, rows, :] = normed
        inverse_ref[0, rows, :] = jnp.broadcast_to(inverse, (ROWS, 128))
        low_ref[0, rows, :] = (normed * gain_ref[0:1, :] + bias_ref[0:1, :]).astype(BF)

    by_rows(v_scr.shape[0], step)


def gelu_parts(x):
    phi = 0.5 + 0.5 * lax.erf(x * 0.7071067811865476)
    density = jnp.exp2((-0.5 * LOG2E) * x * x)
    return x * phi, phi + x * (density * 0.3989422804014327)


CHUNK = 512


def up_kernel(meta, ins, outs, weights, scratch):
    w, *more = weights
    m_ref, a_ref = ins[:2]
    b_refs = ins[2:]
    act_ref, slope_ref, rank_ref = outs
    for loader in weights:
        loader.first_step()
    w.first_wait_all()
    m = m_ref[0]
    rank = nt(m, a_ref[0])
    rank_ref[0] = rank.T.astype(BF)
    rank = rank.astype(BF)
    width = w.width
    for half, b_ref in enumerate(b_refs):
        for lo in range(0, width, CHUNK):
            cols = slice(lo, lo + CHUNK)
            units = nn(m, w.cols(half, lo, CHUNK)) + nn(rank, b_ref[0, :, cols])
            act, slope = gelu_parts(units)
            act_ref[0, half, :, cols] = act.astype(BF)
            slope_ref[0, half, :, cols] = slope.astype(BF)

    last = jnp.logical_and(
        pl.program_id(0) == pl.num_programs(0) - 1, pl.program_id(1) == pl.num_programs(1) - 1
    )

    @pl.when(last)
    def _():
        for loader in more:
            loader.wait(0)
            loader.wait(1)


def add_up(total, part, fresh):
    total[...] = jnp.where(fresh, part, total[...] + part)


def by_chunks(ref, parts):
    at = 0
    for chunk in range(8):
        for part in parts:
            width = part.shape[1] // 8
            ref[0, :, at : at + width] = part[:, chunk * width : (chunk + 1) * width].astype(BF)
            at += width


def keep_or_send(t, value, kept_ref, sent_ref):
    @pl.when(pl.program_id(1) == t)
    def _():
        kept_ref[0] = value

    @pl.when(pl.program_id(1) != t)
    def _():
        sent_ref[0] = value


def middle_kernel(meta, ins, outs, weights, scratch):
    (act_ref, slope_ref, n1_ref, r1_ref, go_ref, m_ref, att_ref, ranku_ref, ranko_ref,
     da_ref, db_ref, ua_ref, ub_ref, oa_ref, ob_ref, gain_ref, bias_ref) = ins
    kept_ref, sent_ref, first_ref, gatt_ref = outs[:4]
    down, early_up, late_up, out = weights
    v_scr, second_scr, gf_scr, gh_scr, out_scr = scratch[:5]
    sums = scratch[5:]
    sum_da, sum_db, sum_ua, sum_ub, sum_oa, sum_ob = sums
    tile = pl.program_id(1)
    fresh = tile == 0
    width = down.width
    part = early_up.width
    halves = [slice(0, width), slice(width, 2 * width)]

    rank = sum(nt(act_ref[0, h], da_ref[0, :, halves[h]]) for h in range(2)).astype(BF)
    model = v_scr.shape[1]
    for at in range(0, model, CHUNK):
        cols = slice(at, at + CHUNK)
        v_scr[:, cols] = (
            nt(act_ref[0, 0], down.scratch[cols, halves[0]])
            + nt(act_ref[0, 1], down.scratch[cols, halves[1]])
            + nn(rank, db_ref[0, :, cols])
        )

    def second_norm(rows):
        middle = n1_ref[0, rows, :] * gain_ref[0:1, :] + bias_ref[0:1, :]
        normed, inverse = norm_parts(v_scr[rows, :] + middle)
        out_scr[rows, :] = (normed * gain_ref[1:2, :] + bias_ref[1:2, :]).astype(BF)
        second = norm_back(go_ref[0, rows, :].astype(F32) * gain_ref[1:2, :], normed, inverse)
        second_scr[rows, :] = second
        gf_scr[rows, :] = second.astype(BF)

    by_rows(v_scr.shape[0], second_norm)
    grad_feed = gf_scr[...]
    add_up(sum_db, tn(rank, grad_feed), fresh)
    grad_rank = nt(grad_feed, db_ref[0]).astype(BF)
    chunk = 2 * CHUNK
    for half in range(2):
        for lo in range(0, width, chunk):
            cols = slice(half * width + lo, half * width + lo + chunk)
            grad_act = nn(grad_feed, down.cols(half, lo, chunk)) + nn(grad_rank, da_ref[0, :, cols])
            local = slice(lo, lo + chunk)
            gh_scr[:, cols] = (grad_act * slope_ref[0, half, :, local].astype(F32)).astype(BF)
    grad_rank_down = grad_rank

    grad_rank = nt(gh_scr[...], ub_ref[0]).astype(BF)
    for at in range(0, model, CHUNK):
        cols = slice(at, at + CHUNK)
        total = nn(grad_rank, ua_ref[0, :, cols])
        for half in range(2):
            lo = half * width
            local = slice(half * part, (half + 1) * part)
            total = total + nt(gh_scr[:, lo : lo + part], early_up.scratch[cols, local])
            total = total + nt(gh_scr[:, lo + part : lo + width], late_up.scratch[cols, local])
        v_scr[:, cols] = total
    add_up(sum_ua, tn(grad_rank, m_ref[0]), fresh)
    add_up(sum_ub, nn(ranku_ref[0], gh_scr[...]), fresh)
    for half in range(2):
        add_up(sum_da.at[:, halves[half]], tn(grad_rank_down, act_ref[0, half]), fresh)

    def first_norm(rows):
        scaled = (second_scr[rows, :] + v_scr[rows, :]) * gain_ref[0:1, :]
        first = norm_back(scaled, n1_ref[0, rows, :], r1_ref[0, rows, 0:1])
        first_ref[0, rows, :] = first
        gf_scr[rows, :] = first.astype(BF)

    by_rows(v_scr.shape[0], first_norm)
    grad_branch = gf_scr[...]
    grad_rank = nt(grad_branch, ob_ref[0, 0]).astype(BF)
    add_up(sum_oa, tn(grad_rank, att_ref[0]), fresh)
    add_up(sum_ob, nn(ranko_ref[0], grad_branch), fresh)
    owidth = out.width
    for half in range(2):
        cols = slice(half * owidth, (half + 1) * owidth)
        full = nn(grad_branch, out.cols(half, 0, owidth)) + nn(grad_rank, oa_ref[0, 0, :, cols])
        gatt_ref[0, :, cols] = full.astype(BF)

    keep_or_send(meta[meta.shape[0] - 1], out_scr[...], kept_ref, sent_ref)

    @pl.when(tile == pl.num_programs(1) - 1)
    def _():
        by_chunks(outs[4], sums)


def rank_back_kernel(meta, ins, outs, weights, scratch):
    gq_ref, gk_ref, gv_ref, x_ref, rank_ref, b_ref = ins
    gr_ref, sum_ref = outs
    size = b_ref.shape[2]
    ranks, parts_b = [], []
    for slot, ref in enumerate((gq_ref, gk_ref, gv_ref)):
        grad = ref[0]
        ranks.append(nt(b_ref[slot, 0], grad))
        parts_b.append(nn(rank_ref[0, slot * size : (slot + 1) * size, :], grad))
    stacked = jnp.concatenate(ranks, axis=0).astype(BF)
    gr_ref[0] = stacked
    products = nn(stacked, x_ref[0])
    parts_a = [products[slot * size : (slot + 1) * size] for slot in range(3)]
    by_chunks(sum_ref, parts_a + parts_b)


def qkv_back_kernel(meta, ins, outs, weights, scratch):
    gq_ref, gk_ref, gv_ref, gr_ref, first_ref, a_ref = ins
    kept_ref, sent_ref = outs
    (w,) = weights
    slots = 3
    width = w.width // slots
    size = a_ref.shape[2]
    total = first_ref[0] + tn(
        gr_ref[0], a_ref[0:slots, 0].reshape(slots * size, kept_ref.shape[2])
    )
    for half in range(2):
        cols = slice(half * width, (half + 1) * width)
        for slot, ref in enumerate((gq_ref, gk_ref, gv_ref)):
            total += nt(ref[0, :, cols], w.cols(half, slot * width, width))
    keep_or_send(meta[meta.shape[0] - 1], total, kept_ref, sent_ref)


NEAR = []


def made_near(arrays):
    NEAR.extend(arrays)
    return arrays


def waits(arrays):
    arrays = [a for a in arrays if a is not None]
    near = [any(a is n for n in NEAR) for a in arrays]
    specs = [pl.BlockSpec(memory_space=pl.ANY if n else pltpu.HBM) for n in near]
    return specs, [a if n else in_hbm(a) for a, n in zip(arrays, near)]


def far(arrays):
    return [pl.BlockSpec(memory_space=pltpu.HBM) for _ in arrays], [in_hbm(a) for a in arrays]


def call(kernel, meta, ins, outs, flops, scratch=(), weights=(), limit=VMEM, after=(), tiles=1, filled=(),
         saves=(), held=(), near=True, stays=()):
    plans = [weight_plan(pieces, first, width) for pieces, first, width, _, _ in weights]
    n_in, n_out, n_w = len(ins), len(outs), len(weights)
    counts = [len(arrays) for arrays, _ in plans]
    steps = meta.shape[0] - 2
    after_specs, after = waits(after)
    n_after = len(after)

    def body(meta_ref, *refs):
        refs = list(refs)
        take = lambda n: [refs.pop(0) for _ in range(n)]
        in_refs = take(n_in)
        w_refs = [take(n) for n in counts]
        take(n_after + len(filled))
        held_refs = take(len(held))
        take(len(started))
        out_refs = take(n_out)
        save_refs = take(len(saves))
        stay_refs = dict(zip(stays, take(len(stays))))
        w_scr = [stay_refs[i] if i in stay_refs else take(1)[0] for i in range(n_w)]
        w_sem = take(n_w)
        save_sems = take(len(saves))
        me, t = meta_ref[steps], meta_ref[steps + 1]
        loaders = [
            Loader(plan, r, s, m, me, t, w[3])
            for (_, plan), r, s, m, w in zip(plans, w_refs, w_scr, w_sem, weights)
        ]
        for (number, _, first, _), ref, sem in zip(saves, save_refs, save_sems):
            loaders[number].saved = (ref, first, sem)
        kernel(meta_ref, in_refs, out_refs, loaders + [Held(ref) for ref in held_refs], refs)
        for number, *_ in saves:

            @pl.when(jnp.logical_and(pl.program_id(0) == steps - 1, pl.program_id(1) == tiles - 1))
            def _(loader=loaders[number]):
                for copy in loader.save_copies():
                    copy.wait()

    started = [array for *_, array in saves if array is not None]
    w_arrays = [a for arrays, _ in plans for a in arrays]
    first_alias = 1 + n_in + len(w_arrays) + n_after
    w_specs, w_arrays = waits(w_arrays) if near else far(w_arrays)
    nbytes = sum(a.size * a.dtype.itemsize for a, _, _ in ins)
    nbytes += sum(2 * dp * rows * width * 2 for _, _, width, dp, rows in weights)
    for shape, dtype, _, _ in outs:
        size = jnp.dtype(dtype).itemsize
        for extent in shape:
            size *= extent
        nbytes += size
    return pl.pallas_call(
        body,
        grid_spec=pltpu.PrefetchScalarGridSpec(
            num_scalar_prefetch=1,
            grid=(steps, tiles),
            in_specs=[pl.BlockSpec(block, index) for _, block, index in ins]
            + w_specs
            + after_specs
            + [pl.BlockSpec(memory_space=pltpu.HBM) for _ in filled]
            + [pl.BlockSpec(memory_space=pltpu.VMEM) for _ in held]
            + [pl.BlockSpec(memory_space=pltpu.HBM) for _ in started],
            out_specs=[pl.BlockSpec(block, index) for _, _, block, index in outs]
            + [pl.BlockSpec(memory_space=pltpu.HBM) for _ in saves]
            + [pl.BlockSpec(memory_space=pltpu.VMEM) for _ in stays],
            scratch_shapes=[
                pltpu.VMEM((dp * rows, 2 * width), BF)
                for i, (_, _, width, dp, rows) in enumerate(weights)
                if i not in stays
            ]
            + [pltpu.SemaphoreType.DMA((2,)) for _ in [*weights, *saves]]
            + list(scratch),
        ),
        out_shape=[pltpu.HBM(shape, dtype) for shape, dtype, _, _ in outs]
        + [pltpu.HBM((weights[n][3] * weights[n][4], 2 * half), BF) for n, half, _, _ in saves]
        + [pltpu.VMEM((weights[n][3] * weights[n][4], 2 * weights[n][2]), BF) for n in stays],
        input_output_aliases={first_alias + i: i for i in range(len(filled))}
        | {first_alias + len(filled) + len(held) + i: n_out + i for i in range(len(started))},
        **params(flops, nbytes, limit),
    )(
        meta, *[in_hbm(a) for a, _, _ in ins], *w_arrays, *after, *[in_hbm(a) for a in filled],
        *[pltpu.with_memory_space_constraint(a, pltpu.VMEM) for a in held], *[in_hbm(a) for a in started],
    )


def pack(outs, fresh=(), after=()):
    after_specs, after = waits(after)
    arrays, plan, heights, widths = [], [], [], []

    def slot(array):
        for index, known in enumerate(arrays):
            if known is array:
                return index
        arrays.append(array)
        return len(arrays) - 1

    for index, parts in enumerate(outs):
        row = 0
        for part in parts:
            array, at, count, col, cols, into, advance = part
            plan.append((slot(array), at, count, col, cols, index, row, into))
            if advance:
                row += count
        heights.append(row)
        widths.append(max(part[4] + part[5] for part in parts))
    used, n_in = len(arrays), len(arrays) + len(after)
    near = [any(a is f for f in fresh) for a in arrays]

    def kernel(*refs):
        ins, results, sems = refs[:n_in], refs[n_in:-1], refs[-1]
        copies = []
        for number, (a, at, count, col, cols, o, row, into) in enumerate(plan):
            source = ins[a].at[pl.ds(at, count), pl.ds(col, cols)]
            target = results[o].at[pl.ds(row, count), pl.ds(into, cols)]
            if not near[a]:
                copy = pltpu.make_async_copy(source, target, sems.at[number])
                copy.start()
                copies.append(copy)
        for a, at, count, col, cols, o, row, into in plan:
            if near[a]:
                results[o][pl.ds(row, count), pl.ds(into, cols)] = ins[a][pl.ds(at, count), pl.ds(col, cols)]
        for copy in copies:
            copy.wait()

    spaces = [pltpu.VMEM if n else pltpu.HBM for n in near]
    return made_near(pl.pallas_call(
        kernel,
        in_specs=[pl.BlockSpec(memory_space=space) for space in spaces] + after_specs,
        out_specs=[pl.BlockSpec(memory_space=pltpu.VMEM)] * len(outs),
        out_shape=[pltpu.VMEM(shape, BF) for shape in zip(heights, widths)],
        scratch_shapes=[pltpu.SemaphoreType.DMA((len(plan),))],
        compiler_params=pltpu.CompilerParams(vmem_limit_bytes=8 * 2**20),
        cost_estimate=pl.CostEstimate(
            flops=0, bytes_accessed=sum(h * w * 4 for h, w in zip(heights, widths)), transcendentals=0
        ),
    )(*[pltpu.with_memory_space_constraint(a, space) for a, space in zip(arrays, spaces)], *after))


def in_hbm(array):
    return pltpu.with_memory_space_constraint(array, pltpu.HBM)


X, Y, Z1, Z2, Z3 = 1, 2, 4, 8, 12
ZS = (Z1, Z2, Z3)


def hop(array, bits):
    return lax.ppermute(array, "dp", [(i, i ^ bits) for i in range(lax.axis_size("dp"))])


def swap(array):
    return lax.ppermute(array, "tensor", [(0, 1), (1, 0)])


class Gather:
    def __init__(self, w_qkv, w_out, w_up, w_down):
        self.n = n = w_up.shape[0]
        self.h = n // 2
        self.pieces = []
        o, u = w_qkv.shape[2], w_up.shape[1]
        self.width = 3 * o
        flat = w_qkv.reshape(3 * n, o)
        wo, wd = w_out.T, w_down.T
        queries = [(flat, slot * n, n, 0, o, slot * o, slot == 2) for slot in range(3)]
        rest = [
            (wo, 0, n, 0, o, 0, False), (w_up, 0, n, 0, 2 * o, o, True),
            (w_up, 0, n, 2 * o, u - 2 * o, 0, False), (wd, 0, n, 0, o, 2 * o, True),
            (wd, 0, n, o, 3 * o, 0, True),
        ]
        self.own, self.q = pack([queries + rest, queries])
        self.gate = self.q
        self.e, self.f, self.g = (self.cut(p) for p in (1, 2, 3))

    def cut(self, piece):
        return lax.slice_in_dim(self.own, piece * self.n, (piece + 1) * self.n, axis=0)

    def note(self, array, items, other=0):
        at = 0
        for piece, rel, row, count in items:
            self.pieces.append(Piece(piece * self.width, self.width, rel, row, count, array, at, other))
            at += count

    def part(self, array, at, count):
        return (array, at, count, 0, self.width, 0, True)

    def full(self, piece, *rels):
        return [(piece, rel, 0, self.n) for rel in rels]

    def upper(self, piece, *rels):
        return [(piece, rel, self.h, self.h) for rel in rels]

    def lower(self, piece, *rels):
        return [(piece, rel, 0, self.h) for rel in rels]

    def exchange(self, arrays, after=()):
        fresh = [a for a, _ in arrays if a is not self.own]
        (packed,) = pack([[self.part(a, 0, a.shape[0]) for a, _ in arrays]], fresh=fresh, after=after)
        (other,) = made_near([swap(packed)])
        self.note(other, [item for _, items in arrays for item in items], 1)
        return packed, other

    def keep(self, got):
        for array, items in got:
            self.note(array, items)
        return got

    def round1(self):
        self.zq = [hop(self.q, k) for k in ZS]
        self.x1, self.y1 = hop(self.own, X), hop(self.own, Y)
        every = range(4)
        got = [(self.own, [i for p in every for i in self.full(p, 0)])]
        got += [(self.x1, [i for p in every for i in self.full(p, X)])]
        got += [(self.y1, [i for p in every for i in self.full(p, Y)])]
        got += [(z, self.full(0, k)) for z, k in zip(self.zq, ZS)]
        self.got1 = self.keep(got)

    def round2(self, after):
        n, h, part = self.n, self.h, self.part
        along = [part(z, 0, n) for z in self.zq]
        xin, yin, e = pack(
            [along + [part(self.y1, h, h)], along + [part(self.x1, 0, h)], [part(self.own, n, n)]],
            fresh=[*self.zq, self.x1, self.y1],
            after=after,
        )
        x, y, self.ze2 = hop(xin, X), hop(yin, Y), hop(e, Z2)
        self.x, self.y = x, y
        self.got2 = self.keep([
            (x, self.full(0, *(X | k for k in ZS)) + self.upper(0, X | Y)),
            (y, self.full(0, *(Y | k for k in ZS)) + self.lower(0, X | Y)),
            (self.ze2, self.full(1, Z2)),
        ])
        return self.exchange(self.got1, [xin])

    def round3(self, after):
        n, h, part = self.n, self.h, self.part
        xin, yin, e, f = pack(
            [
                [part(self.y, i * n + h, h) for i in range(3)] + [part(self.y1, p * n + h, h) for p in (1, 2)],
                [part(self.x, i * n, h) for i in range(3)] + [part(self.x1, p * n, h) for p in (1, 2)],
                [part(self.own, n, n), part(self.ze2, 0, n)],
                [part(self.own, 2 * n, n)],
            ],
            fresh=[self.x, self.y, self.ze2],
            after=after,
        )
        x, y, self.ze1, self.zf2 = hop(xin, X), hop(yin, Y), hop(e, Z1), hop(f, Z2)
        self.x, self.y = x, y
        both = [X | Y | k for k in ZS]
        self.got3 = self.keep([
            (x, self.upper(0, *both) + self.upper(1, X | Y) + self.upper(2, X | Y)),
            (y, self.lower(0, *both) + self.lower(1, X | Y) + self.lower(2, X | Y)),
        ])
        self.late3 = self.keep([(self.ze1, self.full(1, Z1, Z3)), (self.zf2, self.full(2, Z2))])
        return self.exchange(self.got2, [xin])

    def round4(self, after):
        n, h, part = self.n, self.h, self.part
        along = [part(self.ze1, 0, n), part(self.ze2, 0, n), part(self.ze1, n, n)]
        xin, yin, f, g = pack(
            [
                along + [part(self.y1, 3 * n + h, h)],
                along + [part(self.x1, 3 * n, h)],
                [part(self.own, 2 * n, n), part(self.zf2, 0, n)],
                [part(self.own, 3 * n, n)],
            ],
            fresh=[self.ze1, self.zf2],
            after=after,
        )
        x, y, self.zf1, self.zg2 = hop(xin, X), hop(yin, Y), hop(f, Z1), hop(g, Z2)
        self.x, self.y = x, y
        self.got4 = self.keep([
            (x, self.full(1, *(X | k for k in ZS)) + self.upper(3, X | Y)),
            (y, self.full(1, *(Y | k for k in ZS)) + self.lower(3, X | Y)),
            (self.zf1, self.full(2, Z1, Z3)),
            (self.zg2, self.full(3, Z2)),
        ])
        return self.exchange(self.got3, [xin])

    def round5(self, after):
        n, h, part = self.n, self.h, self.part
        along = [part(self.zf1, 0, n), part(self.zf2, 0, n), part(self.zf1, n, n)]
        xin, yin, g, d = pack(
            [
                [part(self.y, i * n + h, h) for i in range(3)] + along,
                [part(self.x, i * n, h) for i in range(3)] + along,
                [part(self.own, 3 * n, n), part(self.zg2, 0, n)],
                [part(self.y, 3 * n, h), part(self.x, 3 * n, h)],
            ],
            fresh=[self.x, self.y, self.zf1, self.zg2],
            after=after,
        )
        self.d = d
        x, y, self.zg1, self.zd2 = hop(xin, X), hop(yin, Y), hop(g, Z1), hop(d, Z2)
        self.x, self.y = x, y
        both = [X | Y | k for k in ZS]
        self.got5 = self.keep([
            (x, self.upper(1, *both) + self.full(2, *(X | k for k in ZS))),
            (y, self.lower(1, *both) + self.full(2, *(Y | k for k in ZS))),
            (self.zg1, self.full(3, Z1, Z3)),
            (self.zd2, self.full(3, X | Y | Z2)),
        ])
        return self.exchange(self.late3 + self.got4, [xin])

    def round6(self, after):
        n, h, part = self.n, self.h, self.part
        along = [part(self.zg1, 0, n), part(self.zg2, 0, n), part(self.zg1, n, n)]
        xin, yin, d = pack(
            [
                [part(self.y, 3 * h + i * n + h, h) for i in range(3)] + along,
                [part(self.x, 3 * h + i * n, h) for i in range(3)] + along,
                [part(self.d, 0, n), part(self.zd2, 0, n)],
            ],
            fresh=[self.x, self.y, self.zg1, self.zd2],
            after=after,
        )
        x, y, zd1 = hop(xin, X), hop(yin, Y), hop(d, Z1)
        both = [X | Y | k for k in ZS]
        self.got6 = self.keep([
            (x, self.upper(2, *both) + self.full(3, *(X | k for k in ZS))),
            (y, self.lower(2, *both) + self.full(3, *(Y | k for k in ZS))),
            (zd1, self.full(3, X | Y | Z1, X | Y | Z3)),
        ])
        return self.exchange(self.got5, [xin])

    def last(self, after):
        return self.exchange(self.got6, after)


class GatherPlain:
    def __init__(self, w_qkv, w_out, w_up, w_down):
        local = jnp.concatenate([w_qkv[0], w_qkv[1], w_qkv[2], w_out.T, w_up, w_down.T], axis=1)
        rows, width = local.shape
        whole = lax.all_gather(local, ("dp", "tensor")).reshape(lax.axis_size("dp"), 2, rows, width)
        self.pieces = [Piece(0, width, None, 0, 0, whole, 0, other) for other in range(2)]
        self.gate = None

    def round1(self):
        return None

    def round2(self, after):
        return None, None

    round3 = round4 = round5 = round6 = last = round2


class Spot:
    def __init__(self, array, row, rows, col, cols):
        self.array, self.row, self.rows, self.col, self.cols = array, row, rows, col, cols

    def of(self, ref, me, t):
        at = lambda v, unit: pl.multiple_of(v(me, t), unit) if callable(v) else v
        return ref.at[pl.ds(at(self.row, 16), self.rows), pl.ds(at(self.col, 128), self.cols)]


def arrange(where, shapes, moves, fresh=(), after=()):
    after_specs, after = waits(after)
    arrays = []
    for source, _, _ in moves:
        if not any(a is source.array for a in arrays):
            arrays.append(source.array)
    near = [any(a is f for f in fresh) for a in arrays]
    number = lambda array: next(i for i, a in enumerate(arrays) if a is array)
    plan = [(number(source.array), source, out, target) for source, out, target in moves]

    def kernel(where_ref, *refs):
        ins, results, sems = refs[: len(arrays)], refs[len(arrays) + len(after) : -1], refs[-1]
        me, t = where_ref[0], where_ref[1]
        copies = []
        for index, (slot, source, out, target) in enumerate(plan):
            copy = pltpu.make_async_copy(
                source.of(ins[slot], me, t), target.of(results[out], me, t), sems.at[index]
            )
            copy.start()
            copies.append(copy)
        for copy in copies:
            copy.wait()

    spaces = [pltpu.VMEM if n else pltpu.HBM for n in near]
    return made_near(pl.pallas_call(
        kernel,
        in_specs=[pl.BlockSpec(memory_space=pltpu.SMEM)]
        + [pl.BlockSpec(memory_space=m) for m in spaces]
        + after_specs,
        out_specs=[pl.BlockSpec(memory_space=pltpu.VMEM)] * len(shapes),
        out_shape=[pltpu.VMEM(shape, BF) for shape in shapes],
        scratch_shapes=[pltpu.SemaphoreType.DMA((len(plan),))],
        compiler_params=pltpu.CompilerParams(vmem_limit_bytes=8 * 2**20),
        cost_estimate=pl.CostEstimate(
            flops=0, bytes_accessed=sum(h * w * 4 for h, w in shapes), transcendentals=0
        ),
    )(where, *[pltpu.with_memory_space_constraint(a, m) for a, m in zip(arrays, spaces)], *after))


class GradientSum:
    def __init__(self, where, array, widths, mine, rank, adapters, picks):
        self.where, self.array, self.picks = where, array, picks
        self.mine, self.rank, self.adapters = mine, rank, adapters
        self.rows = mine * rank
        self.widths = widths
        self.starts = [sum(widths[:i]) for i in range(len(widths))]
        self.chunk = sum(widths) // 8

    def cores(self, after=()):
        half = 4 * self.chunk
        source = Spot(self.array, 0, self.rows, lambda me, t: (1 - t) * half, half)
        moves = [(source, 0, Spot(None, 0, self.rows, 0, half))]
        (out,) = arrange(self.where, [(self.rows, half)], moves, after=after)
        self.other = swap(out)
        return out

    def plane(self, after=()):
        rows, chunk = self.rows, self.chunk
        moves = []
        for k in range(4):
            mine = Spot(self.array, 0, rows, lambda me, t, k=k: (t * 4 + ((me & 3) ^ k)) * chunk, chunk)
            theirs = Spot(self.other, 0, rows, lambda me, t, k=k: ((me & 3) ^ k) * chunk, chunk)
            moves += [
                (mine, k, Spot(None, 0, rows, 0, chunk)),
                (theirs, k, Spot(None, rows, rows, 0, chunk)),
                (Spot(self.picks, 0, self.rank, 0, chunk), k, Spot(None, 2 * rows, self.rank, 0, chunk)),
            ]
        shape = (2 * rows + self.rank, chunk)
        outs = arrange(self.where, [shape] * 4, moves, fresh=[self.other], after=after)
        self.parts = [outs[0], hop(outs[1], X), hop(outs[2], Y), hop(outs[3], X | Y)]
        return outs[0]

    def fold(self, after=()):
        rank, chunk, data = self.rank, self.chunk, 2 * self.rows
        tall = self.adapters * rank
        quarter = tall // 4

        def kernel(where_ref, *refs):
            ins, outs, total = refs[:4], refs[-5:-1], refs[-1]
            z = where_ref[0] // 4
            row = lax.broadcasted_iota(jnp.int32, (tall, data), 0)
            col = lax.broadcasted_iota(jnp.int32, (tall, data), 1)
            adapter = (row // rank).astype(F32)
            same_row = row % rank == col % rank
            for k in range(4):
                picks = ins[k][data : data + 1, 0:data].astype(F32)
                chosen = jnp.logical_and(adapter == picks, same_row).astype(F32).astype(BF)
                part = nn(chosen, ins[k][0:data, :])
                total[...] = part if k == 0 else total[...] + part
            for k in range(4):
                rows = pl.ds(pl.multiple_of((z ^ k) * quarter, quarter), quarter)
                outs[k][...] = total[rows, :].astype(BF)

        outs = self.local(kernel, self.parts, after, [(quarter, chunk)] * 4, [(tall, chunk)])
        self.parts = [outs[0]] + [hop(outs[k], 4 * k) for k in (1, 2, 3)]
        return outs[0]

    def local(self, kernel, arrays, after, shapes, scratch):
        after_specs, after = waits(after)
        vmem = pl.BlockSpec(memory_space=pltpu.VMEM)
        return made_near(pl.pallas_call(
            kernel,
            in_specs=[pl.BlockSpec(memory_space=pltpu.SMEM)] + [vmem] * len(arrays) + after_specs,
            out_specs=[vmem] * len(shapes),
            out_shape=[pltpu.VMEM(shape, BF) for shape in shapes],
            scratch_shapes=[pltpu.VMEM(shape, F32) for shape in scratch],
            compiler_params=pltpu.CompilerParams(vmem_limit_bytes=12 * 2**20),
            cost_estimate=pl.CostEstimate(
                flops=0, bytes_accessed=sum(h * w * 8 for h, w in shapes), transcendentals=0
            ),
        )(
            self.where,
            *[pltpu.with_memory_space_constraint(a, pltpu.VMEM) for a in arrays],
            *after,
        ))

    def depth(self, after=()):
        def kernel(where_ref, *refs):
            total = refs[0][...].astype(F32)
            for ref in refs[1:4]:
                total += ref[...].astype(F32)
            refs[-1][...] = total.astype(BF)

        (out,) = self.local(kernel, self.parts, after, [self.parts[0].shape], [])
        self.parts = [out] + [hop(out, 4 * k) for k in (1, 2, 3)]
        return out

    def back(self, after=()):
        tall = self.adapters * self.rank
        quarter, side = tall // 4, self.chunk // 2
        moves = [
            (
                Spot(self.parts[k], 0, quarter, part * side, side),
                part,
                Spot(None, lambda me, t, k=k: ((me >> 2) ^ k) * quarter, quarter, 0, side),
            )
            for k in range(4)
            for part in range(2)
        ]
        self.a, self.b = arrange(self.where, [(tall, side)] * 2, moves, fresh=self.parts, after=after)
        self.xa, self.yb = hop(self.a, X), hop(self.b, Y)
        return self.a

    def spread(self, after=()):
        tall, side = self.adapters * self.rank, self.chunk // 2
        moves = [
            (Spot(source, 0, tall, 0, side), out, Spot(None, row * tall, tall, 0, side))
            for out, pair in enumerate(((self.a, self.xa), (self.b, self.yb)))
            for row, source in enumerate(pair)
        ]
        fresh = [self.a, self.b, self.xa, self.yb]
        up, down = arrange(self.where, [(2 * tall, side)] * 2, moves, fresh=fresh, after=after)
        self.ya, self.xb = hop(up, Y), hop(down, X)
        return up

    def give(self, after=()):
        tall, side = self.adapters * self.rank, self.chunk // 2
        sources = [
            ((self.a, 0), (self.b, 0)),
            ((self.xa, 0), (self.xb, 0)),
            ((self.ya, 0), (self.yb, 0)),
            ((self.ya, tall), (self.xb, tall)),
        ]
        moves = [
            (Spot(source, row, tall, 0, side), 0, Spot(None, k * tall, tall, part * side, side))
            for k, both in enumerate(sources)
            for part, (source, row) in enumerate(both)
        ]
        fresh = [self.a, self.b, self.xa, self.yb, self.ya, self.xb]
        (out,) = arrange(self.where, [(4 * tall, self.chunk)], moves, fresh=fresh, after=after)
        self.theirs = swap(out)
        self.ours = out
        return out


def finish(where, sums, results, after=()):
    tall = sums[0].adapters * sums[0].rank
    after_specs, after = waits(after)
    inputs = [a for s in sums for a in (s.ours, s.theirs)]

    def kernel(where_ref, *refs):
        outs = refs[len(inputs) + len(after) :]
        me, t = where_ref[0], where_ref[1]
        for out, parts in zip(outs, results):
            for place, (number, which) in enumerate(parts):
                total = sums[number]
                start, width = total.starts[which] // 8, total.widths[which] // 8
                for core in range(2):
                    for k in range(4):
                        column = ((t ^ core) * 4 + ((me & 3) ^ k)) * width
                        out[place * tall : (place + 1) * tall, pl.ds(pl.multiple_of(column, 128), width)] = refs[
                            2 * number + core
                        ][k * tall : (k + 1) * tall, start : start + width].astype(F32)

    vmem = pl.BlockSpec(memory_space=pltpu.VMEM)
    shapes = [(len(parts) * tall, sums[parts[0][0]].widths[parts[0][1]]) for parts in results]
    return pl.pallas_call(
        kernel,
        in_specs=[pl.BlockSpec(memory_space=pltpu.SMEM)]
        + [vmem] * len(inputs)
        + after_specs,
        out_specs=[vmem] * len(results),
        out_shape=[pltpu.HBM(shape, F32) for shape in shapes],
        compiler_params=pltpu.CompilerParams(vmem_limit_bytes=32 * 2**20),
        cost_estimate=pl.CostEstimate(
            flops=0, bytes_accessed=sum(h * w * 6 for h, w in shapes), transcendentals=0
        ),
    )(where, *inputs, *after)


def hold(array, after):
    after_specs, after = waits(after)
    return pl.pallas_call(
        lambda *refs: None,
        in_specs=after_specs + [pl.BlockSpec(memory_space=pltpu.HBM)],
        out_specs=pl.BlockSpec(memory_space=pltpu.HBM),
        out_shape=pltpu.HBM(array.shape, array.dtype),
        input_output_aliases={len(after): 0},
        cost_estimate=pl.CostEstimate(flops=0, bytes_accessed=0, transcendentals=0),
    )(*after, in_hbm(array))


def place(where, filled, arrived, after=()):
    after_specs, after = waits(after)
    mine, rows, width = arrived.shape

    def kernel(where_ref, arrived_ref, *refs):
        refs[-1][...] = arrived_ref[...]

    return pl.pallas_call(
        kernel,
        grid_spec=pltpu.PrefetchScalarGridSpec(
            num_scalar_prefetch=1,
            grid=(mine,),
            in_specs=[pl.BlockSpec((1, rows, width), lambda s, w: (s, 0, 0))]
            + after_specs
            + [pl.BlockSpec(memory_space=pltpu.HBM)],
            out_specs=pl.BlockSpec((1, rows, width), lambda s, w: ((1 - w[1]) * mine + s, 0, 0)),
        ),
        out_shape=pltpu.HBM(filled.shape, filled.dtype),
        input_output_aliases={2 + len(after): 0},
        **params(1, 2 * arrived.size * arrived.dtype.itemsize, 16 * 2**20),
    )(where, arrived, *after, in_hbm(filled))


def shards(
    hidden_in, segment_ids, adapter_pick, w_qkv, w_out, w_up, w_down, ln_gain, ln_bias,
    adapt_a, adapt_b, up_a, up_b, down_a, down_b, grad_out,
):
    dp = lax.axis_size("dp")
    t = lax.axis_index("tensor")
    block, ff_half = w_up.shape
    width = hidden_in.shape[2]
    half = width // 2
    ff = 2 * ff_half
    positions = hidden_in.shape[1]
    length = 2 * positions
    mine = hidden_in.shape[0] // 2
    rank = adapt_b.shape[2]
    adapters = adapt_b.shape[1]

    NEAR.clear()
    pick = lax.dynamic_slice_in_dim(adapter_pick, mine * t, mine, 0)
    where = jnp.stack([lax.axis_index("dp"), t]).astype(pick.dtype)
    meta = jnp.concatenate([pick, where])
    ordered = jnp.where(t == 0, adapter_pick, jnp.roll(adapter_pick, -mine))
    picks = jnp.repeat(ordered, rank).astype(BF)
    picks = jnp.broadcast_to(jnp.pad(picks, (0, 3 * half - picks.shape[0]))[None], (rank, 3 * half))
    segs = lax.dynamic_slice_in_dim(segment_ids, mine * t, mine, 0)
    seg_col = segs.reshape(mine, length, 1)
    seg_row = segs.reshape(mine, 1, length)

    sent_rows = mine * positions

    def send_half(value, after):
        flat = value.reshape(2 * sent_rows, width)
        spot = Spot(flat, lambda me, t: (1 - t) * sent_rows, sent_rows, 0, width)
        (out,) = arrange(where, [(sent_rows, width)], [(spot, 0, Spot(None, 0, sent_rows, 0, width))], after=after)
        return flat, out, swap(out)

    def join(flat, there, after):
        moves = []
        for s in range(mine):
            moves.append((
                Spot(flat, lambda me, t, s=s: (t * mine + s) * positions, positions, 0, width), 0,
                Spot(None, lambda me, t, s=s: s * length + t * positions, positions, 0, width),
            ))
            moves.append((
                Spot(there, s * positions, positions, 0, width), 0,
                Spot(None, lambda me, t, s=s: s * length + (1 - t) * positions, positions, 0, width),
            ))
        (out,) = arrange(where, [(mine * length, width)], moves, fresh=[there], after=after)
        return out.reshape(mine, length, width), out

    gather = (Gather if dp == 16 else GatherPlain)(w_qkv, w_out, w_up, w_down)
    gather.round1()
    def columns(first, count):
        return (gather.pieces, first, count, dp, block)

    qkv_w = columns(0, 3 * half)
    out_w = columns(3 * half, half)
    part = 2 * half
    up_parts = [columns(4 * half + p, part) for p in range(0, ff_half, part)]
    up_w = columns(4 * half, ff_half)
    down_w = columns(4 * half + ff_half, ff_half)

    a_t = jnp.swapaxes(adapt_a, 2, 3)
    ua_t = jnp.swapaxes(up_a, 1, 2)
    da_t = jnp.swapaxes(down_a, 1, 2)

    flat_x, gate, there_x = send_half(hidden_in, [gather.gate])
    flat_c, gate, there_c = send_half(grad_out, [gate])
    gate, met = gather.round2([meta, seg_col, seg_row, picks, gate])
    x, gate = join(flat_x, there_x, [gate])
    cotangent, gate = join(flat_c, there_c, [gate])
    _, met = gather.round3([met, gate])
    gate, _ = gather.round4([met])
    tokens = mine * length
    tiles = 2
    tile = length // tiles
    seq3 = lambda s, i, m: (s, 0, 0)
    row3 = lambda s, i, m: (s, i, 0)
    fixed2 = lambda s, i, m: (0, 0)
    picked3 = lambda s, i, m: (m[s], 0, 0)
    slots4 = lambda s, i, m: (0, m[s], 0, 0)
    last4 = lambda s, i, m: (3, m[s], 0, 0)
    full = lambda a: (a, (1, *a.shape[1:]), seq3)
    row = lambda a: (a, (1, tile, a.shape[2]), row3)
    across = lambda a: (a, (1, a.shape[1], tile), lambda s, i, m: (s, 0, i))
    whole = lambda a: (a, a.shape, fixed2)
    factor = lambda a: (a, (1, *a.shape[1:]), picked3)
    slots = lambda a: (a, (a.shape[0], 1, *a.shape[2:]), slots4)
    last = lambda a: (a, (1, 1, *a.shape[2:]), last4)
    rows_made = lambda dtype, cols: ((mine, length, cols), dtype, (1, tile, cols), row3)
    across_made = lambda rows: ((mine, rows, length), BF, (1, rows, tile), lambda s, i, m: (s, 0, i))
    def kept_made(dtype):
        block = (1, positions, width)
        return [
            ((2 * mine, positions, width), dtype, block, lambda s, i, m: (m[mine + 1] * mine + s, 0, 0)),
            ((mine, positions, width), dtype, block, seq3),
        ]

    sum_made = lambda rows, cols: ((mine, rows, cols), BF, (1, rows, cols), seq3)

    qkv, rank_qkv, whole_qkv = call(
        qkv_kernel, meta,
        [row(x), slots(a_t), slots(adapt_b)],
        [((mine, 3, length, width), BF, (1, 3, tile, width), lambda s, i, m: (s, 0, i, 0)),
         across_made(3 * rank)],
        6 * tokens * width * width,
        weights=[qkv_w],
        after=[gate],
        limit=24 * 2**20,
        tiles=tiles,
        saves=[(0, 3 * half, 0, None)],
    )
    gate, met = gather.round5([qkv])

    groups = width // GROUP

    def heads_of(slot, first, group=0):
        return pl.BlockSpec((1, 1, length, GROUP), lambda s, h: (s + first, slot, 0, h + group))

    def seg_specs(first):
        return [
            pl.BlockSpec((1, length, 1), lambda s, h: (s + first, 0, 0)),
            pl.BlockSpec((1, 1, length), lambda s, h: (s + first, 0, 0)),
        ]

    def lse_at(first, group=0):
        return pl.BlockSpec((1, 1, 8, length), lambda s, h: (s + first, h + group, 0, 0))

    def heads_at(first, group=0):
        return pl.BlockSpec((1, length, GROUP), lambda s, h: (s + first, 0, h + group))

    after_specs, after = waits([gate])
    attention, lse = pl.pallas_call(
        lambda q, k, v, sc, sr, *refs: attend_kernel(q, k, v, sc, sr, *refs[len(after) :]),
        grid=(mine, groups),
        in_specs=[heads_of(j, 0) for j in range(3)] + seg_specs(0) + after_specs,
        out_specs=[heads_at(0), lse_at(0)],
        out_shape=[
            pltpu.HBM((mine, length, width), BF),
            pltpu.HBM((mine, groups, 8, length), F32),
        ],
        **params(16 * tokens * length * width, tokens * width * 8, 16 * 2**20),
    )(*[in_hbm(a) for a in [qkv, qkv, qkv, seg_col, seg_row]], *after)
    gate, _ = gather.round6([lse, met])

    normed, inverse, middle_low, rank_out, whole_out = call(
        out_kernel, meta,
        [row(attention), row(x), last(a_t), last(adapt_b), whole(ln_gain), whole(ln_bias)],
        [rows_made(F32, width), rows_made(F32, 128), rows_made(BF, width), across_made(rank)],
        2 * tokens * width * width,
        scratch=[pltpu.VMEM((tile, width), F32)],
        weights=[out_w],
        limit=18 * 2**20,
        after=[gate],
        tiles=tiles,
        stays=[0],
    )

    gate = rank_out
    blocks = ff_half // part
    made_up, whole_up = [], []
    for index, weight in enumerate(up_parts):
        up_cols = [
            (up_b, (1, rank, part), lambda s, i, m, at=h * blocks + index: (m[s], 0, at)) for h in range(2)
        ]
        units_made = (
            (mine, 2, length, ff_half), BF, (1, 2, tile, part), lambda s, i, m, index=index: (s, 0, i, index)
        )
        last_part = index == len(up_parts) - 1
        made = call(
            up_kernel, meta,
            [row(middle_low), factor(ua_t), *up_cols],
            [units_made, units_made, across_made(rank)],
            4 * tokens * width * part * 2,
            weights=[weight, down_w] if last_part else [weight],
            limit=18 * 2**20,
            after=[gate],
            tiles=tiles,
            filled=made_up,
            stays=list(range(1 + last_part)),
        )
        *made_up, rank_up = made[:3]
        gate = rank_up
        whole_up.append(made[3])
        if last_part:
            whole_down = made[4]
        elif index == 0:
            gate, _ = gather.last([rank_up])
    units = lambda a: (a, (1, 2, tile, ff_half), lambda s, i, m: (s, 0, i, 0))
    act, slope = made_up

    layer_out, layer_sent, grad_first, grad_att, sooner = call(
        middle_kernel, meta,
        [units(act), units(slope), row(normed), row(inverse), row(cotangent), row(middle_low), row(attention),
         across(rank_up), across(rank_out), factor(da_t), factor(down_b), factor(ua_t), factor(up_b),
         last(a_t), last(adapt_b), whole(ln_gain), whole(ln_bias)],
        [*kept_made(BF), rows_made(F32, width), rows_made(BF, width),
         sum_made(rank, 2 * ff + 4 * width)],
        tokens * width * (6 * ff + 2 * width),
        scratch=[pltpu.VMEM((tile, width), F32), pltpu.VMEM((tile, width), F32), pltpu.VMEM((tile, width), BF),
                 pltpu.VMEM((tile, ff), BF), pltpu.VMEM((tile, width), BF),
                 pltpu.VMEM((rank, ff), F32), pltpu.VMEM((rank, width), F32),
                 pltpu.VMEM((rank, width), F32), pltpu.VMEM((rank, ff), F32),
                 pltpu.VMEM((rank, width), F32), pltpu.VMEM((rank, width), F32)],
        tiles=tiles,
        held=[whole_down, *whole_up, whole_out],
        limit=34 * 2**20,
    )

    layer_there = swap(layer_sent)
    flat = lambda g: g.reshape(mine * rank, g.shape[-1])
    sooner_widths = [ff, width, width, ff, width, width]
    later_widths = [width] * 6
    fast = dp == 16
    gate = None
    if fast:
        first_sum = GradientSum(where, flat(sooner), sooner_widths, mine, rank, adapters, picks)
        gate = first_sum.cores()

    halves = 2
    span = groups // halves

    def attend_back(first, group, made, after):
        after_specs, after = waits(after)
        extra = len(made) + len(after)

        def body(q, k, v, sc, sr, l, o, do, *refs):
            attend_back_kernel(q, k, v, sc, sr, l, o, do, *refs[extra:])

        args = [qkv, qkv, qkv, seg_col, seg_row, lse, attention, grad_att, *made]
        return pl.pallas_call(
            body,
            grid=(1, span),
            in_specs=[heads_of(j, first, group) for j in range(3)]
            + seg_specs(first)
            + [lse_at(first, group), heads_at(first, group), heads_at(first, group)]
            + [pl.BlockSpec(memory_space=pltpu.HBM) for _ in made]
            + after_specs,
            out_specs=[heads_at(first, group)] * 3,
            out_shape=[pltpu.HBM((mine, length, width), BF)] * 3,
            input_output_aliases={8 + i: i for i in range(len(made))},
            **params(40 * length * length * width // halves, length * width * 16, 32 * 2**20),
        )(*[in_hbm(a) for a in args], *after)

    grads_qkv = []
    between = iter([first_sum.plane, first_sum.fold, first_sum.depth, first_sum.back] if fast else [])
    for index in range(mine):
        for group in range(0, groups, span):
            grads_qkv = attend_back(index, group, grads_qkv, [gate])
            gate = None
            phase = next(between, None)
            if phase is not None and (index, group) != (mine - 1, groups - span):
                gate = phase([grads_qkv[0]])
    gate = first_sum.back([grads_qkv[0]]) if fast else None

    grad_rank, later = call(
        rank_back_kernel, meta,
        [full(g) for g in grads_qkv] + [full(x), full(rank_qkv), slots(adapt_b)],
        [sum_made(3 * rank, length), sum_made(rank, 6 * width)],
        18 * tokens * width * rank,
        after=[gate],
        limit=32 * 2**20,
    )
    gate = grad_rank
    if fast:
        second_sum = GradientSum(where, flat(later), later_widths, mine, rank, adapters, picks)
        gate = second_sum.cores([gate])
        gate = first_sum.spread([gate])
        gate = second_sum.plane([gate])

    grad_in, grad_sent = call(
        qkv_back_kernel, meta,
        [row(g) for g in grads_qkv] + [across(grad_rank), row(grad_first), slots(a_t)],
        kept_made(F32),
        6 * tokens * width * width,
        held=[whole_qkv],
        after=[gate],
        limit=40 * 2**20,
        tiles=tiles,
    )
    turned = lambda v: jnp.swapaxes(v, -1, -2)
    if fast:
        gate = second_sum.fold([grad_in])
        gate = first_sum.give([gate])
        layer_out = place(where, layer_out, layer_there, [gate])
        gate = second_sum.depth([layer_out])
        there = swap(hold(grad_sent, [gate]))
        gate = second_sum.back([gate])
        done1 = finish(where, [first_sum], [[(0, 0)], [(0, 1)], [(0, 2)], [(0, 3)]], [gate])
        gate = second_sum.spread([done1[0]])
        grad_in = place(where, grad_in, there, [gate])
        second_sum.give([grad_in])
        all_a, all_b = finish(
            where, [second_sum, first_sum],
            [[(0, 0), (0, 1), (0, 2), (1, 4)], [(0, 3), (0, 4), (0, 5), (1, 5)]],
        )
        shaped = lambda v: v.reshape(-1, adapters, rank, v.shape[1])
        da, db, ua, ub = (shaped(v)[0] for v in done1)
        return (layer_out, grad_in, turned(shaped(all_a)), shaped(all_b), turned(ua), ub, turned(da), db)

    layer_out = place(where, layer_out, layer_there)
    grad_in = place(where, grad_in, swap(grad_sent))
    onehot = (pick[:, None] == jnp.arange(adapters)[None, :]).astype(F32)

    def fold(per_sequence):
        total = onehot[0][:, None, None] * per_sequence[0][None].astype(F32)
        for index in range(1, mine):
            total += onehot[index][:, None, None] * per_sequence[index][None].astype(F32)
        return total

    def apart(array, widths):
        chunks, at, parts = array.reshape(mine, rank, 8, -1), 0, []
        for columns_of in widths:
            part = chunks[..., at : at + columns_of // 8]
            parts.append(part.reshape(mine, rank, columns_of))
            at += columns_of // 8
        return parts

    g_down_a, g_down_b, g_up_a, g_up_b, g_out_a, g_out_b = apart(sooner, sooner_widths)
    qkv_sums = apart(later, later_widths)
    sums = lax.psum(
        tuple(
            fold(g)
            for g in [*qkv_sums[:3], g_out_a, *qkv_sums[3:], g_out_b, g_up_a, g_up_b, g_down_a, g_down_b]
        ),
        ("dp", "tensor"),
    )
    return (
        layer_out,
        grad_in,
        turned(jnp.stack(sums[:4])),
        jnp.stack(sums[4:8]),
        turned(sums[8]),
        sums[9],
        turned(sums[10]),
        sums[11],
    )


def solution(mesh):
    placed = (
        P("dp", "tensor", None),
        P("dp", None),
        P("dp"),
        P(None, "dp", "tensor"),
        P("tensor", "dp"),
        P("dp", "tensor"),
        P("tensor", "dp"),
        P(),
        P(),
        P(),
        P(),
        P(),
        P(),
        P(),
        P(),
        P("dp", "tensor", None),
    )
    return jax.shard_map(
        shards,
        mesh=mesh,
        in_specs=placed,
        out_specs=(P("dp", "tensor", None), P("dp", "tensor", None), P(), P(), P(), P(), P(), P()),
        check_vma=False,
    )
```
